32 devices in a mesh: rep: 4 (over x, core), tp: 8 (over z, y).
Axes of the slice: x: 2, y: 2, z: 4, core: 2. Of those that a mesh axis runs over, the one named last changes fastest.
Arguments:
- activations: bfloat16 [4, 256, 2560], P('rep', 'tp'), may hold values from -6 to 6
- out_grad: bfloat16 [4, 256, 2560], P('rep', 'tp'), may hold values from -6 to 6
- gate_weight: bfloat16 [4, 2560, 6912], P('rep', None, 'tp'), may hold values from -6 to 6
- up_weight: bfloat16 [4, 2560, 6912], P('rep', None, 'tp'), may hold values from -6 to 6
- down_weight: bfloat16 [4, 6912, 2560], P('rep', 'tp'), may hold values from -6 to 6
- step_index: int32 [1], replicated, may hold values from 0 to 999
Outputs:
- layer_out: bfloat16 [4, 256, 2560], P('rep', 'tp')
- grad_in: bfloat16 [4, 256, 2560], P('rep', 'tp')
- new_gate: bfloat16 [4, 2560, 6912], P('rep', None, 'tp')
- new_up: bfloat16 [4, 2560, 6912], P('rep', None, 'tp')
- new_down: bfloat16 [4, 6912, 2560], P('rep', 'tp')
The draws below stay inside these ranges and needn't reach their ends.
All inputs are finite; a program needn't handle non-finite values.
Results may differ from the reference program's by a relative error of at most 0.0052.
Values may be sent and summed in bfloat16 or wider, within the bound.
No kernel may reach another device: no remote copies, remote signals or barrier semaphores. Data moves between devices by JAX's collectives and lax.ppermute only.
A program may use at most 128 MiB of HBM per device.

```python
import math
import jax
import jax.numpy as jnp
from jax import lax

D = 2560
FF = 6912
TOK = 256
REPS = 4


def block_levels(own_key, shape, cuts, least, top_value):
    level, own = 1.0, jax.random.fold_in(own_key, 6)
    for axis_at, parts in cuts:
        heights = jnp.exp(jax.random.uniform(jax.random.fold_in(own, axis_at), (parts,), jnp.float32, least / len(cuts), top_value / len(cuts)))
        level = level * jnp.repeat(heights, shape[axis_at] // parts).reshape([-1 if axis == axis_at else 1 for axis in range(len(shape))])
    return level


def scatter_about(stream_key, dims, width, limit, cuts=(), held_as=jnp.bfloat16):
    loudness = block_levels(stream_key, dims, cuts, -0.22, 0.18) if cuts else 1.0
    result = jax.random.normal(stream_key, dims, jnp.float32) * width * loudness
    return jnp.minimum(jnp.maximum(result, -limit), limit).astype(held_as)


def setup_inputs(seed: int = 0) -> dict:
    keys = jax.random.split(jax.random.key(seed), 7)
    return {
        "activations": scatter_about(keys[0], (REPS, TOK, D), 1.0, 6.0, ((0, 4), (1, 8))),
        "out_grad": scatter_about(keys[1], (REPS, TOK, D), 1.0, 6.0, ((0, 4), (1, 8))),
        "gate_weight": scatter_about(keys[2], (REPS, D, FF), 1.0, 6.0, ((0, 4), (2, 8))),
        "up_weight": scatter_about(keys[3], (REPS, D, FF), 1.0, 6.0, ((0, 4), (2, 8))),
        "down_weight": scatter_about(keys[4], (REPS, FF, D), 1.0, 6.0, ((0, 4), (1, 8))),
        "step_index": jax.random.randint(keys[5], (1,), 0, 1000).astype(jnp.int32),
    }


def replica_step(operands):
    tokens_in, grads_out, gate_w, up_w, down_w = operands
    width_scale = 1.0 / math.sqrt(D)
    hidden_scale = 1.0 / math.sqrt(FF)
    gate_pre = jnp.dot(tokens_in, gate_w, preferred_element_type=jnp.float32) * width_scale
    up_pre = jnp.dot(tokens_in, up_w, preferred_element_type=jnp.float32) * width_scale
    sigmoid_gate = jax.nn.sigmoid(gate_pre)
    activated = gate_pre * sigmoid_gate
    hidden = (activated * up_pre).astype(jnp.bfloat16)
    layer_out = (jnp.dot(hidden, down_w, preferred_element_type=jnp.float32) * hidden_scale).astype(jnp.bfloat16)
    d_hidden = jnp.dot(grads_out, down_w.T, preferred_element_type=jnp.float32) * hidden_scale
    d_gate = (d_hidden * up_pre * (sigmoid_gate * (1.0 + gate_pre * (1.0 - sigmoid_gate)))).astype(jnp.bfloat16)
    d_up = (d_hidden * activated).astype(jnp.bfloat16)
    grad_down = jnp.dot(hidden.T, grads_out, preferred_element_type=jnp.float32) * hidden_scale
    grad_gate = jnp.dot(tokens_in.T, d_gate, preferred_element_type=jnp.float32) * width_scale
    grad_upw = jnp.dot(tokens_in.T, d_up, preferred_element_type=jnp.float32) * width_scale
    grad_in = ((jnp.dot(d_gate, gate_w.T, preferred_element_type=jnp.float32) + jnp.dot(d_up, up_w.T, preferred_element_type=jnp.float32)) * width_scale).astype(jnp.bfloat16)
    stepped_gate = (gate_w.astype(jnp.float32) - 0.8 * grad_gate).astype(jnp.bfloat16)
    stepped_up = (up_w.astype(jnp.float32) - 0.8 * grad_upw).astype(jnp.bfloat16)
    stepped_down = (down_w.astype(jnp.float32) - 0.8 * grad_down).astype(jnp.bfloat16)
    return (layer_out, grad_in, stepped_gate, stepped_up, stepped_down)

def reference(activations, out_grad, gate_weight, up_weight, down_weight, step_index):
    layer_out, grad_in, stepped_gate, stepped_up, stepped_down = lax.map(replica_step, (activations, out_grad, gate_weight, up_weight, down_weight))
    levels = REPS.bit_length() - 1
    shift_bits = (step_index[0] % levels).astype(jnp.int32)
    distance = jnp.left_shift(jnp.ones((), jnp.int32), shift_bits)

    def average(stepped):
        received = jnp.roll(stepped, distance, axis=0)
        return ((stepped.astype(jnp.float32) + received.astype(jnp.float32)) * 0.5).astype(jnp.bfloat16)
    return (layer_out, grad_in, average(stepped_gate), average(stepped_up), average(stepped_down))
```

```python
from functools import partial
import math

import jax
import jax.numpy as jnp
from jax import lax
from jax.sharding import PartitionSpec as P

D = 2560
FF = 6912


learn_rate = 0.8
width_scale = 1.0 / math.sqrt(D)
hidden_scale = 1.0 / math.sqrt(FF)


def shifted(x, by):
    devices = lax.axis_size("rep")
    return lax.ppermute(x, "rep", [(i, (i + by) % devices) for i in range(devices)])


def gathered(x):
    return lax.all_gather(x, "tp", axis=0, tiled=True)


def mm(a, b, dims):
    return lax.dot_general(a, b, (dims, ((), ())), preferred_element_type=jnp.float32)


def step_of(weight, left, right, scale):
    grad = mm(left, right, ((0,), (0,))) * scale
    return (weight.astype(jnp.float32) - learn_rate * grad).astype(jnp.bfloat16)


def mean_of(mine, theirs):
    return ((mine.astype(jnp.float32) + theirs.astype(jnp.float32)) * 0.5).astype(jnp.bfloat16)


def whole_step(distance, tokens_local, grads_local, gate_w, up_w, down_w):
    send = partial(shifted, by=distance)
    raw_gate_too = distance == 1
    their_tokens_local = send(tokens_local)
    their_up_raw = send(up_w)
    if raw_gate_too:
        their_gate_raw = send(gate_w)
    tokens = gathered(tokens_local)
    grads = gathered(grads_local)
    their_tokens = gathered(their_tokens_local)

    gate_pre = mm(tokens, gate_w, ((1,), (1,))) * width_scale
    up_pre = mm(tokens, up_w, ((1,), (1,))) * width_scale
    sigmoid_gate = jax.nn.sigmoid(gate_pre)
    activated = gate_pre * sigmoid_gate
    hidden = (activated * up_pre).astype(jnp.bfloat16)
    d_hidden = mm(grads, down_w, ((1,), (1,))) * hidden_scale
    d_gate = (d_hidden * up_pre * (sigmoid_gate * (1.0 + gate_pre * (1.0 - sigmoid_gate)))).astype(jnp.bfloat16)
    d_up = (d_hidden * activated).astype(jnp.bfloat16)

    their_d_up = send(d_up)
    if raw_gate_too:
        their_d_gate = send(d_gate)
    down_new = step_of(down_w, hidden, grads, hidden_scale)
    their_down = send(down_new)
    gate_new = step_of(gate_w, d_gate, tokens, width_scale)
    if not raw_gate_too:
        their_gate = send(gate_new)
    up_new = step_of(up_w, d_up, tokens, width_scale)

    layer_part = mm(hidden, down_w, ((1,), (0,))) * hidden_scale
    grad_part = (mm(d_gate, gate_w, ((1,), (0,))) + mm(d_up, up_w, ((1,), (0,)))) * width_scale
    devices = lax.axis_size("tp")
    parts = jnp.stack([layer_part.astype(jnp.bfloat16), grad_part.astype(jnp.bfloat16)])
    parts = parts.reshape(2, devices, -1, parts.shape[-1])
    parts = lax.all_to_all(parts, "tp", split_axis=1, concat_axis=1, tiled=True)
    sums = jnp.sum(parts.astype(jnp.float32), axis=1).astype(jnp.bfloat16)

    their_up = step_of(their_up_raw, their_d_up, their_tokens, width_scale)
    if raw_gate_too:
        their_gate = step_of(their_gate_raw, their_d_gate, their_tokens, width_scale)
    return (
        sums[0],
        sums[1],
        mean_of(gate_new, their_gate),
        mean_of(up_new, their_up),
        mean_of(down_new, their_down),
    )


def shards(activations, out_grad, gate_weight, up_weight, down_weight, step_index):
    levels = lax.axis_size("rep").bit_length() - 1
    branches = [partial(whole_step, 1 << level) for level in range(levels)]
    layer_out, grad_in, gate, up, down = lax.switch(
        step_index[0] % levels,
        branches,
        activations[0],
        out_grad[0],
        gate_weight[0].T,
        up_weight[0].T,
        down_weight[0],
    )
    return layer_out[None], grad_in[None], gate.T[None], up.T[None], down[None]


def solution(mesh):
    in_specs = (
        P("rep", "tp", None),
        P("rep", "tp", None),
        P("rep", None, "tp"),
        P("rep", None, "tp"),
        P("rep", "tp", None),
        P(),
    )
    out_specs = (
        P("rep", "tp", None),
        P("rep", "tp", None),
        P("rep", None, "tp"),
        P("rep", None, "tp"),
        P("rep", "tp", None),
    )
    return jax.shard_map(shards, mesh=mesh, in_specs=in_specs, out_specs=out_specs, check_vma=False)
```

```python
from functools import partial
import math

import jax
import jax.numpy as jnp
from jax import lax
from jax.experimental import pallas as pl
from jax.experimental.pallas import tpu as pltpu
from jax.sharding import PartitionSpec as P

D = 2560
FF = 6912
BLOCK = 144


learn_rate = 0.8
width_scale = 1.0 / math.sqrt(D)
hidden_scale = 1.0 / math.sqrt(FF)

ANY = pl.BlockSpec(memory_space=pl.ANY)
PARAMS = pltpu.CompilerParams(vmem_limit_bytes=40 * 1024 * 1024)


def ring_of(devices):
    y_size = 1 << ((devices.bit_length() - 1) // 2)
    z_size = devices // y_size
    walk = [(z, 0) for z in range(z_size)]
    for z in reversed(range(z_size)):
        ys = list(range(1, y_size))
        walk += [(z, y) for y in (ys if (z_size - 1 - z) % 2 == 0 else reversed(ys))]
    return [z * y_size + y for z, y in walk]


def mm(a, b, dims):
    return lax.dot_general(a, b, (dims, ((), ())), preferred_element_type=jnp.float32)


def cost(matmuls, rows, blocks_moved):
    return pl.CostEstimate(
        flops=2 * matmuls * rows * 256 * D, bytes_accessed=blocks_moved * rows * D * 2, transcendentals=0
    )


def rows_spec(first=0, width=D):
    return pl.BlockSpec((BLOCK, width), lambda i: (i + first, 0))


def whole_spec(x):
    return pl.BlockSpec(x.shape, lambda i: (0,) * x.ndim)


def forward(tokens, grads, gate_w, up_w, down_w):
    units, count = gate_w.shape[0], tokens.shape[0]

    def body(tokens_ref, grads_ref, gate_ref, up_ref, down_ref, hidden_ref, d_gate_ref, d_up_ref):
        gate_pre = mm(gate_ref[...], tokens_ref[...], ((1,), (1,))) * width_scale
        up_pre = mm(up_ref[...], tokens_ref[...], ((1,), (1,))) * width_scale
        d_hidden = mm(down_ref[...], grads_ref[...], ((1,), (1,))) * hidden_scale
        sigmoid_gate = jax.nn.sigmoid(gate_pre)
        activated = gate_pre * sigmoid_gate
        slope = sigmoid_gate * (1.0 + gate_pre * (1.0 - sigmoid_gate))
        hidden_ref[...] = (activated * up_pre).astype(jnp.bfloat16)
        d_gate_ref[...] = (d_hidden * up_pre * slope).astype(jnp.bfloat16)
        d_up_ref[...] = (d_hidden * activated).astype(jnp.bfloat16)

    out = jax.ShapeDtypeStruct((units, count), jnp.bfloat16)
    return pl.pallas_call(
        body,
        grid=(units // BLOCK,),
        in_specs=[whole_spec(tokens), whole_spec(grads)] + [rows_spec()] * 3,
        out_specs=[rows_spec(0, count)] * 3,
        out_shape=[out] * 3,
        compiler_params=PARAMS,
        cost_estimate=cost(3, units, 3),
        name="forward",
    )(tokens, grads, gate_w, up_w, down_w)


def stepped(weight, left, right, scale):
    return weight.astype(jnp.float32) - learn_rate * (mm(left, right, ((1,), (0,))) * scale)


def step_rows(weight, left, right, scale, first, rows, after=()):
    at = first // BLOCK

    def body(weight_ref, left_ref, right_ref, *rest):
        rest[-1][...] = stepped(weight_ref[...], left_ref[...], right_ref[...], scale).astype(jnp.bfloat16)

    return pl.pallas_call(
        body,
        grid=(rows // BLOCK,),
        in_specs=[rows_spec(at), rows_spec(at, left.shape[1]), whole_spec(right)] + [ANY] * len(after),
        out_specs=rows_spec(),
        out_shape=jax.ShapeDtypeStruct((rows, D), jnp.bfloat16),
        compiler_params=PARAMS,
        cost_estimate=cost(1, rows, 2),
        name="step_rows",
    )(weight, left, right, *after)


def halved_sum(mine, theirs):
    return ((mine.astype(jnp.float32) + theirs.astype(jnp.float32)) * 0.5).astype(jnp.bfloat16)


def into_rows(body, ins, in_specs, base, first, rows, units, costs, name):
    def with_base(*refs):
        body(*refs[: len(ins)], refs[-1])

    extra = () if base is None else (base,)
    return pl.pallas_call(
        with_base,
        grid=(rows // BLOCK,),
        in_specs=in_specs + [ANY] * len(extra),
        out_specs=rows_spec(first // BLOCK),
        out_shape=jax.ShapeDtypeStruct((units, D), jnp.bfloat16),
        input_output_aliases={len(ins): 0} if extra else {},
        compiler_params=PARAMS,
        cost_estimate=costs,
        name=name,
    )(*ins, *extra)


def mean_rows(mine, theirs, base, first, units):
    def body(mine_ref, theirs_ref, out_ref):
        out_ref[...] = halved_sum(mine_ref[...], theirs_ref[...])

    rows = theirs.shape[0]
    return into_rows(
        body, (mine, theirs), [rows_spec(), rows_spec()], base, first, rows, units, cost(0, rows, 3), "mean_rows"
    )


def mean_of_steps(mine, left, right, theirs, their_left, their_right, scale, units):
    def body(mine_ref, left_ref, right_ref, theirs_ref, their_left_ref, their_right_ref, out_ref):
        own = stepped(mine_ref[...], left_ref[...], right_ref[...], scale).astype(jnp.bfloat16)
        other = stepped(theirs_ref[...], their_left_ref[...], their_right_ref[...], scale).astype(jnp.bfloat16)
        out_ref[...] = halved_sum(own, other)

    rows, count = theirs.shape[0], left.shape[1]
    return into_rows(
        body,
        (mine, left, right, theirs, their_left, their_right),
        [rows_spec(), rows_spec(0, count), whole_spec(right)] * 2,
        None,
        0,
        rows,
        units,
        cost(2, rows, 3),
        "mean_of_steps",
    )


def partial_sums(hidden, d_gate, d_up, gate_w, up_w, down_w, devices):
    units, count = hidden.shape
    part = count // devices
    steps = units // BLOCK

    def body(hidden_ref, d_gate_ref, d_up_ref, gate_ref, up_ref, down_ref, *rest):
        outs, (layer, grad) = rest[:devices], rest[devices:]

        @pl.when(pl.program_id(0) == 0)
        def _():
            layer[...] = jnp.zeros_like(layer)
            grad[...] = jnp.zeros_like(grad)

        layer[...] += mm(hidden_ref[...], down_ref[...], ((0,), (0,)))
        grad[...] += mm(d_gate_ref[...], gate_ref[...], ((0,), (0,)))
        grad[...] += mm(d_up_ref[...], up_ref[...], ((0,), (0,)))

        @pl.when(pl.program_id(0) == steps - 1)
        def _():
            for at, out in enumerate(outs):
                out[0] = (layer[pl.ds(at * part, part)] * hidden_scale).astype(jnp.bfloat16)
                out[1] = (grad[pl.ds(at * part, part)] * width_scale).astype(jnp.bfloat16)

    out = jax.ShapeDtypeStruct((2, part, D), jnp.bfloat16)
    return pl.pallas_call(
        body,
        grid=(steps,),
        in_specs=[rows_spec(0, count)] * 3 + [rows_spec()] * 3,
        out_specs=[pl.BlockSpec(out.shape, lambda i: (0, 0, 0))] * devices,
        out_shape=[out] * devices,
        scratch_shapes=[pltpu.VMEM((count, D), jnp.float32)] * 2,
        compiler_params=PARAMS,
        cost_estimate=cost(3, units, 3),
        name="partial_sums",
    )(hidden, d_gate, d_up, gate_w, up_w, down_w)


def whole_step(distance, tokens_local, grads_local, gate_w, up_w, down_w):
    units = gate_w.shape[0]
    devices = lax.axis_size("tp")
    ring = ring_of(devices)
    blocks = units // BLOCK
    raw = (blocks if distance == 1 else blocks // 2) * BLOCK

    def send(x):
        replicas = lax.axis_size("rep")
        return lax.ppermute(x, "rep", [(i, (i + distance) % replicas) for i in range(replicas)])

    def along(x, by):
        return lax.ppermute(x, "tp", [(ring[i], ring[(i + by) % devices]) for i in range(devices)])

    their_tokens_local = send(tokens_local)
    their_up_raw = send(up_w[:raw])

    token_blocks, grad_blocks = [tokens_local] * devices, [grads_local] * devices
    for hop in range(1, devices // 2 + 1):
        for held, last_way in ((token_blocks, 1), (grad_blocks, -1)):
            for way in (1, -1):
                if hop < devices // 2 or way == last_way:
                    held[-way * hop] = along(held[-way * (hop - 1)], way)
    tokens = jnp.concatenate(token_blocks)
    grads = jnp.concatenate(grad_blocks)

    their_tokens_local, tokens = lax.optimization_barrier((their_tokens_local, tokens))
    their_tokens = lax.all_gather(their_tokens_local, "tp", axis=0)
    orders = [[ring[(ring.index(own) + at) % devices] for at in range(devices)] for own in range(devices)]
    order = jnp.array(orders, jnp.int32)[lax.axis_index("tp")]
    their_tokens = jnp.concatenate(
        [lax.dynamic_index_in_dim(their_tokens, order[at], keepdims=False) for at in range(devices)]
    )

    hidden, d_gate, d_up = forward(tokens, grads, gate_w, up_w, down_w)
    their_d_up = send(d_up[:raw])
    down_new = step_rows(down_w, hidden, grads, hidden_scale, 0, units)
    their_down = send(down_new)
    after = [(their_d_up,), (their_down,)]
    if raw < units:
        up_rest = step_rows(up_w, d_up, tokens, width_scale, raw, units - raw, after.pop(0))
        their_up_rest = send(up_rest)
        after.append((their_up_rest,))
    cut = units - BLOCK
    gate_head = step_rows(gate_w, d_gate, tokens, width_scale, 0, cut, after.pop(0))
    their_gate_head = send(gate_head)
    gate_tail = step_rows(gate_w, d_gate, tokens, width_scale, cut, BLOCK, after.pop(0))
    their_gate_tail = send(gate_tail)

    parts = partial_sums(hidden, d_gate, d_up, gate_w, up_w, down_w, devices)
    sums = parts[0].astype(jnp.float32)
    for by in range(1, devices):
        sums = sums + along(parts[by], by).astype(jnp.float32)
    sums = sums.astype(jnp.bfloat16)

    new_up = mean_of_steps(up_w, d_up, tokens, their_up_raw, their_d_up, their_tokens, width_scale, units)
    if raw < units:
        new_up = mean_rows(up_rest, their_up_rest, new_up, raw, units)
    new_down = mean_rows(down_new, their_down, None, 0, units)
    new_gate = mean_rows(gate_head, their_gate_head, None, 0, units)
    new_gate = mean_rows(gate_tail, their_gate_tail, new_gate, cut, units)
    return sums[0], sums[1], new_gate, new_up, new_down


def shards(activations, out_grad, gate_weight, up_weight, down_weight, step_index):
    levels = lax.axis_size("rep").bit_length() - 1
    branches = [partial(whole_step, 1 << level) for level in range(levels)]
    layer_out, grad_in, gate, up, down = lax.switch(
        step_index[0] % levels,
        branches,
        activations[0],
        out_grad[0],
        gate_weight[0].T,
        up_weight[0].T,
        down_weight[0],
    )
    return layer_out[None], grad_in[None], gate.T[None], up.T[None], down[None]


def solution(mesh):
    in_specs = (
        P("rep", "tp", None),
        P("rep", "tp", None),
        P("rep", None, "tp"),
        P("rep", None, "tp"),
        P("rep", "tp", None),
        P(),
    )
    out_specs = (
        P("rep", "tp", None),
        P("rep", "tp", None),
        P("rep", None, "tp"),
        P("rep", None, "tp"),
        P("rep", "tp", None),
    )
    return jax.shard_map(shards, mesh=mesh, in_specs=in_specs, out_specs=out_specs, check_vma=False)
```

```python
from functools import partial
import math

import jax
import jax.numpy as jnp
from jax import lax
from jax.experimental import pallas as pl
from jax.experimental.pallas import tpu as pltpu
from jax.sharding import PartitionSpec as P

D = 2560
FF = 6912
BLOCK = 144


learn_rate = 0.8
width_scale = 1.0 / math.sqrt(D)
hidden_scale = 1.0 / math.sqrt(FF)

ANY = pl.BlockSpec(memory_space=pl.ANY)
PARAMS = pltpu.CompilerParams(vmem_limit_bytes=40 * 1024 * 1024)


def ring_of(devices):
    y_size = 1 << ((devices.bit_length() - 1) // 2)
    z_size = devices // y_size
    walk = [(z, 0) for z in range(z_size)]
    for z in reversed(range(z_size)):
        ys = list(range(1, y_size))
        walk += [(z, y) for y in (ys if (z_size - 1 - z) % 2 == 0 else reversed(ys))]
    return [z * y_size + y for z, y in walk]


def mm(a, b, dims):
    return lax.dot_general(a, b, (dims, ((), ())), preferred_element_type=jnp.float32)


def cost(matmuls, rows, blocks_moved):
    return pl.CostEstimate(
        flops=2 * matmuls * rows * 256 * D, bytes_accessed=blocks_moved * rows * D * 2, transcendentals=0
    )


def rows_spec(first=0, width=D, block=BLOCK):
    return pl.BlockSpec((block, width), lambda i: (i + first, 0))


def block_of(units, most):
    return max(size for size in range(BLOCK, most + 1, BLOCK) if units % size == 0)


def whole_spec(x):
    return pl.BlockSpec(x.shape, lambda i: (0,) * x.ndim)


def forward(token_blocks, grad_blocks, gate_w, up_w, down_w):
    units, devices = gate_w.shape[0], len(token_blocks)
    part = token_blocks[0].shape[0]
    count = devices * part
    block = block_of(units, 288)

    def body(*refs):
        gate_ref, up_ref, down_ref = refs[2 * devices : 2 * devices + 3]
        tokens_ref, grads_ref, hidden_ref, d_gate_ref, d_up_ref, turned, turned_grads = refs[2 * devices + 3 :]

        @pl.when(pl.program_id(0) == 0)
        def _():
            for at in range(devices):
                tokens_ref[pl.ds(at * part, part)] = refs[at][...]
                grads_ref[pl.ds(at * part, part)] = refs[devices + at][...]
            turned[...] = tokens_ref[...].T
            turned_grads[...] = grads_ref[...].T

        gate_pre = mm(gate_ref[...], turned[...], ((1,), (0,))) * width_scale
        up_pre = mm(up_ref[...], turned[...], ((1,), (0,))) * width_scale
        d_hidden = mm(down_ref[...], turned_grads[...], ((1,), (0,))) * hidden_scale
        sigmoid_gate = jax.nn.sigmoid(gate_pre)
        activated = gate_pre * sigmoid_gate
        slope = sigmoid_gate * (1.0 + gate_pre * (1.0 - sigmoid_gate))
        hidden_ref[...] = (activated * up_pre).astype(jnp.bfloat16)
        d_gate_ref[...] = (d_hidden * up_pre * slope).astype(jnp.bfloat16)
        d_up_ref[...] = (d_hidden * activated).astype(jnp.bfloat16)

    whole = jax.ShapeDtypeStruct((count, D), jnp.bfloat16)
    out = jax.ShapeDtypeStruct((units, count), jnp.bfloat16)
    pieces = [*token_blocks, *grad_blocks]
    return pl.pallas_call(
        body,
        grid=(units // block,),
        in_specs=[whole_spec(piece) for piece in pieces] + [rows_spec(block=block)] * 3,
        out_specs=[whole_spec(whole)] * 2 + [rows_spec(0, count, block)] * 3,
        out_shape=[whole] * 2 + [out] * 3,
        scratch_shapes=[pltpu.VMEM((D, count), jnp.bfloat16)] * 2,
        compiler_params=PARAMS,
        cost_estimate=cost(3, units, 3),
        name="forward",
    )(*pieces, gate_w, up_w, down_w)


def stepped(weight, left, right, scale):
    return weight.astype(jnp.float32) - learn_rate * (mm(left, right, ((1,), (0,))) * scale)


def step_rows(weight, left, right, scale, first, rows, after=(), beside=None):
    at = first // BLOCK
    count = left.shape[1]
    ins, specs, width = (weight, left, right), [rows_spec(at), rows_spec(at, count), whole_spec(right)], D
    if beside is not None:
        ins, specs, width = (*ins, beside), specs + [rows_spec(0, count)], D + count

    def body(weight_ref, left_ref, right_ref, *rest):
        out_ref = rest[-1]
        out_ref[:, :D] = stepped(weight_ref[...], left_ref[...], right_ref[...], scale).astype(jnp.bfloat16)
        if beside is not None:
            out_ref[:, D:] = rest[0][...]

    return pl.pallas_call(
        body,
        grid=(rows // BLOCK,),
        in_specs=specs + [ANY] * len(after),
        out_specs=rows_spec(0, width),
        out_shape=jax.ShapeDtypeStruct((rows, width), jnp.bfloat16),
        compiler_params=PARAMS,
        cost_estimate=cost(1, rows, 2),
        name="step_rows",
    )(*ins, *after)


def halved_sum(mine, theirs):
    return ((mine.astype(jnp.float32) + theirs.astype(jnp.float32)) * 0.5).astype(jnp.bfloat16)


def into_rows(body, ins, in_specs, base, first, rows, units, costs, name, after, scratch=()):
    others = after if base is None else (base, *after)

    def with_others(*refs):
        body(*refs[: len(ins)], *refs[len(ins) + len(others) :])
    return pl.pallas_call(
        with_others,
        grid=(rows // BLOCK,),
        in_specs=in_specs + [ANY] * len(others),
        out_specs=rows_spec(first // BLOCK),
        out_shape=jax.ShapeDtypeStruct((units, D), jnp.bfloat16),
        input_output_aliases={} if base is None else {len(ins): 0},
        scratch_shapes=scratch,
        compiler_params=PARAMS,
        cost_estimate=costs,
        name=name,
    )(*ins, *others)


def mean_rows(mine, theirs, base, first, units, after=()):
    def body(mine_ref, theirs_ref, out_ref):
        out_ref[...] = halved_sum(mine_ref[...], theirs_ref[...])

    rows = theirs.shape[0]
    specs = [rows_spec(), rows_spec()]
    return into_rows(
        body, (mine, theirs), specs, base, first, rows, units, cost(0, rows, 3), "mean_rows", after
    )


def mean_of_steps(order, mine, left, right, theirs, their_left, their_right, scale, units, after):
    devices, part, _ = their_right.shape

    def body(order_ref, mine_ref, left_ref, right_ref, theirs_ref, their_left_ref, their_right_ref, out_ref, ordered):
        @pl.when(pl.program_id(0) == 0)
        def _():
            for at in range(devices):
                ordered[pl.ds(at * part, part)] = their_right_ref[order_ref[at]]

        own = stepped(mine_ref[...], left_ref[...], right_ref[...], scale).astype(jnp.bfloat16)
        other = stepped(theirs_ref[...], their_left_ref[...], ordered[...], scale).astype(jnp.bfloat16)
        out_ref[...] = halved_sum(own, other)

    rows, count = theirs.shape[0], left.shape[1]
    return into_rows(
        body,
        (order, mine, left, right, theirs, their_left, their_right),
        [pl.BlockSpec(memory_space=pltpu.SMEM)]
        + [rows_spec(), rows_spec(0, count), whole_spec(right)]
        + [rows_spec(), pl.BlockSpec((BLOCK, count), lambda i: (i, D // count)), whole_spec(their_right)],
        None,
        0,
        rows,
        units,
        cost(2, rows, 3),
        "mean_of_steps",
        after,
        [pltpu.VMEM((count, D), jnp.bfloat16)],
    )


def partial_sums(order, hidden, d_gate, d_up, gate_w, up_w, down_w, after):
    units, count = hidden.shape
    devices = order.shape[0]
    part = count // devices
    block = block_of(units, 432)
    steps = units // block

    def body(order_ref, hidden_ref, d_gate_ref, d_up_ref, gate_ref, up_ref, down_ref, *rest):
        out, layer, grad = rest[-3:]

        @pl.when(pl.program_id(0) == 0)
        def _():
            layer[...] = jnp.zeros_like(layer)
            grad[...] = jnp.zeros_like(grad)

        layer[...] += mm(hidden_ref[...], down_ref[...], ((0,), (0,)))
        grad[...] += mm(d_gate_ref[...], gate_ref[...], ((0,), (0,))) + mm(d_up_ref[...], up_ref[...], ((0,), (0,)))

        @pl.when(pl.program_id(0) == steps - 1)
        def _():
            for at in range(devices):
                owner = order_ref[at]
                out[owner, 0] = (layer[pl.ds(at * part, part)] * hidden_scale).astype(jnp.bfloat16)
                out[owner, 1] = (grad[pl.ds(at * part, part)] * width_scale).astype(jnp.bfloat16)

    out = jax.ShapeDtypeStruct((devices, 2, part, D), jnp.bfloat16)
    return pl.pallas_call(
        body,
        grid=(steps,),
        in_specs=[pl.BlockSpec(memory_space=pltpu.SMEM)]
        + [rows_spec(0, count, block)] * 3
        + [rows_spec(block=block)] * 3
        + [ANY] * len(after),
        out_specs=whole_spec(out),
        out_shape=out,
        scratch_shapes=[pltpu.VMEM((count, D), jnp.float32)] * 2,
        compiler_params=PARAMS,
        cost_estimate=cost(3, units, 3),
        name="partial_sums",
    )(order, hidden, d_gate, d_up, gate_w, up_w, down_w, *after)


def whole_step(distance, tokens_local, grads_local, gate_w, up_w, down_w):
    units = gate_w.shape[0]
    devices = lax.axis_size("tp")
    ring = ring_of(devices)

    def send(x):
        replicas = lax.axis_size("rep")
        return lax.ppermute(x, "rep", [(i, (i + distance) % replicas) for i in range(replicas)])

    def along(x, by):
        return lax.ppermute(x, "tp", [(ring[i], ring[(i + by) % devices]) for i in range(devices)])

    their_tokens_local = send(tokens_local)
    their_up_raw = send(up_w)

    token_blocks, grad_blocks = [tokens_local] * devices, [grads_local] * devices
    for hop in range(1, devices // 2 + 1):
        for held, last_way in ((token_blocks, 1), (grad_blocks, -1)):
            for way in (1, -1):
                if hop < devices // 2 or way == last_way:
                    held[-way * hop] = along(held[-way * (hop - 1)], way)
    their_tokens_local, token_blocks[devices // 2] = lax.optimization_barrier(
        (their_tokens_local, token_blocks[devices // 2])
    )
    their_tokens = lax.all_gather(their_tokens_local, "tp", axis=0)
    orders = [[ring[(ring.index(own) + at) % devices] for at in range(devices)] for own in range(devices)]
    order = jnp.array(orders, jnp.int32)[lax.axis_index("tp")]

    tokens, grads, hidden, d_gate, d_up = forward(token_blocks, grad_blocks, gate_w, up_w, down_w)

    down_new = step_rows(down_w, hidden, grads, hidden_scale, 0, units, beside=d_up)
    their_down = send(down_new)
    parts = partial_sums(order, hidden, d_gate, d_up, gate_w, up_w, down_w, (down_new, their_up_raw))
    parts = lax.all_to_all(parts, "tp", split_axis=0, concat_axis=0, tiled=True)
    sums = jnp.sum(parts.astype(jnp.float32), axis=0).astype(jnp.bfloat16)
    cut = units - BLOCK
    gate_head = step_rows(gate_w, d_gate, tokens, width_scale, 0, cut, (their_up_raw,))
    their_gate_head = send(gate_head)
    gate_tail = step_rows(gate_w, d_gate, tokens, width_scale, cut, BLOCK, (their_down,))
    their_gate_tail = send(gate_tail)

    new_up = mean_of_steps(
        order, up_w, d_up, tokens, their_up_raw, their_down, their_tokens, width_scale, units, (gate_tail,)
    )
    new_down = mean_rows(down_new, their_down, None, 0, units, (new_up,))
    new_gate = mean_rows(gate_head, their_gate_head, None, 0, units, (new_down,))
    new_gate = mean_rows(gate_tail, their_gate_tail, new_gate, cut, units)
    return sums[0], sums[1], new_gate, new_up, new_down


def shards(activations, out_grad, gate_weight, up_weight, down_weight, step_index):
    levels = lax.axis_size("rep").bit_length() - 1
    branches = [partial(whole_step, 1 << level) for level in range(levels)]
    layer_out, grad_in, gate, up, down = lax.switch(
        step_index[0] % levels,
        branches,
        activations[0],
        out_grad[0],
        gate_weight[0].T,
        up_weight[0].T,
        down_weight[0],
    )
    return layer_out[None], grad_in[None], gate.T[None], up.T[None], down[None]


def solution(mesh):
    in_specs = (
        P("rep", "tp", None),
        P("rep", "tp", None),
        P("rep", None, "tp"),
        P("rep", None, "tp"),
        P("rep", "tp", None),
        P(),
    )
    out_specs = (
        P("rep", "tp", None),
        P("rep", "tp", None),
        P("rep", None, "tp"),
        P("rep", None, "tp"),
        P("rep", "tp", None),
    )
    return jax.shard_map(shards, mesh=mesh, in_specs=in_specs, out_specs=out_specs, check_vma=False)
```

```python
from functools import partial
import math

import jax
import jax.numpy as jnp
from jax import lax
from jax.experimental import pallas as pl
from jax.experimental.pallas import tpu as pltpu
from jax.sharding import PartitionSpec as P

D = 2560
FF = 6912
BLOCK = 144


learn_rate = 0.8
width_scale = 1.0 / math.sqrt(D)
hidden_scale = 1.0 / math.sqrt(FF)

ANY = pl.BlockSpec(memory_space=pl.ANY)
PARAMS = pltpu.CompilerParams(vmem_limit_bytes=40 * 1024 * 1024)


def ring_of(devices):
    y_size = 1 << ((devices.bit_length() - 1) // 2)
    z_size = devices // y_size
    walk = [(z, 0) for z in range(z_size)]
    for z in reversed(range(z_size)):
        ys = list(range(1, y_size))
        walk += [(z, y) for y in (ys if (z_size - 1 - z) % 2 == 0 else reversed(ys))]
    return [z * y_size + y for z, y in walk]


def mm(a, b, dims):
    return lax.dot_general(a, b, (dims, ((), ())), preferred_element_type=jnp.float32)


def cost(matmuls, rows, blocks_moved):
    return pl.CostEstimate(
        flops=2 * matmuls * rows * 256 * D, bytes_accessed=blocks_moved * rows * D * 2, transcendentals=0
    )


def rows_spec(first=0, width=D, block=BLOCK):
    return pl.BlockSpec((block, width), lambda i: (i + first, 0))


def block_of(units, most):
    return max(size for size in range(BLOCK, most + 1, BLOCK) if units % size == 0)


def whole_spec(x):
    return pl.BlockSpec(x.shape, lambda i: (0,) * x.ndim)


def forward(token_blocks, grad_blocks, gate_w, up_w, down_w):
    units, devices = gate_w.shape[0], len(token_blocks)
    part = token_blocks[0].shape[0]
    count = devices * part
    block = block_of(units, 288)

    def body(*refs):
        gate_ref, up_ref, down_ref = refs[2 * devices : 2 * devices + 3]
        tokens_ref, grads_ref, hidden_ref, d_gate_ref, d_up_ref, turned, turned_grads = refs[2 * devices + 3 :]

        @pl.when(pl.program_id(0) == 0)
        def _():
            for at in range(devices):
                tokens_ref[pl.ds(at * part, part)] = refs[at][...]
                grads_ref[pl.ds(at * part, part)] = refs[devices + at][...]
            turned[...] = tokens_ref[...].T
            turned_grads[...] = grads_ref[...].T

        gate_pre = mm(gate_ref[...], turned[...], ((1,), (0,))) * width_scale
        up_pre = mm(up_ref[...], turned[...], ((1,), (0,))) * width_scale
        d_hidden = mm(down_ref[...], turned_grads[...], ((1,), (0,))) * hidden_scale
        sigmoid_gate = jax.nn.sigmoid(gate_pre)
        activated = gate_pre * sigmoid_gate
        slope = sigmoid_gate * (1.0 + gate_pre * (1.0 - sigmoid_gate))
        hidden_ref[...] = (activated * up_pre).astype(jnp.bfloat16)
        d_gate_ref[...] = (d_hidden * up_pre * slope).astype(jnp.bfloat16)
        d_up_ref[...] = (d_hidden * activated).astype(jnp.bfloat16)

    whole = jax.ShapeDtypeStruct((count, D), jnp.bfloat16)
    out = jax.ShapeDtypeStruct((units, count), jnp.bfloat16)
    pieces = [*token_blocks, *grad_blocks]
    return pl.pallas_call(
        body,
        grid=(units // block,),
        in_specs=[whole_spec(piece) for piece in pieces] + [rows_spec(block=block)] * 3,
        out_specs=[whole_spec(whole)] * 2 + [rows_spec(0, count, block)] * 3,
        out_shape=[whole] * 2 + [out] * 3,
        scratch_shapes=[pltpu.VMEM((D, count), jnp.bfloat16)] * 2,
        compiler_params=PARAMS,
        cost_estimate=cost(3, units, 3),
        name="forward",
    )(*pieces, gate_w, up_w, down_w)


def stepped(weight, left, right, scale):
    return weight.astype(jnp.float32) - learn_rate * (mm(left, right, ((1,), (0,))) * scale)


def step_rows(weight, left, right, scale, first, rows, after=(), beside=None, costs=None):
    at = first // BLOCK
    count = left.shape[1]
    ins, specs, width = (weight, left, right), [rows_spec(at), rows_spec(at, count), whole_spec(right)], D
    if beside is not None:
        ins, specs, width = (*ins, beside), specs + [rows_spec(0, count)], D + count

    def body(weight_ref, left_ref, right_ref, *rest):
        out_ref = rest[-1]
        out_ref[:, :D] = stepped(weight_ref[...], left_ref[...], right_ref[...], scale).astype(jnp.bfloat16)
        if beside is not None:
            out_ref[:, D:] = rest[0][...]

    return pl.pallas_call(
        body,
        grid=(rows // BLOCK,),
        in_specs=specs + [ANY] * len(after),
        out_specs=rows_spec(0, width),
        out_shape=jax.ShapeDtypeStruct((rows, width), jnp.bfloat16),
        compiler_params=PARAMS,
        cost_estimate=costs or cost(1, rows, 2),
        name="step_rows",
    )(*ins, *after)


def halved_sum(mine, theirs):
    return ((mine.astype(jnp.float32) + theirs.astype(jnp.float32)) * 0.5).astype(jnp.bfloat16)


def into_rows(body, ins, in_specs, base, first, rows, units, costs, name, after, scratch=()):
    others = after if base is None else (base, *after)

    def with_others(*refs):
        body(*refs[: len(ins)], *refs[len(ins) + len(others) :])
    return pl.pallas_call(
        with_others,
        grid=(rows // BLOCK,),
        in_specs=in_specs + [ANY] * len(others),
        out_specs=rows_spec(first // BLOCK),
        out_shape=jax.ShapeDtypeStruct((units, D), jnp.bfloat16),
        input_output_aliases={} if base is None else {len(ins): 0},
        scratch_shapes=scratch,
        compiler_params=PARAMS,
        cost_estimate=costs,
        name=name,
    )(*ins, *others)


def mean_rows(mine, theirs, base, first, units, after=()):
    def body(mine_ref, theirs_ref, out_ref):
        out_ref[...] = halved_sum(mine_ref[...], theirs_ref[...])

    rows = theirs.shape[0]
    specs = [rows_spec(), rows_spec()]
    return into_rows(
        body, (mine, theirs), specs, base, first, rows, units, cost(0, rows, 3), "mean_rows", after
    )


def mean_of_steps(order, mine, left, right, theirs, their_left, their_right, scale, rows, units, after):
    devices, part, _ = their_right.shape

    def body(order_ref, mine_ref, left_ref, right_ref, theirs_ref, their_left_ref, their_right_ref, out_ref, ordered):
        @pl.when(pl.program_id(0) == 0)
        def _():
            for at in range(devices):
                ordered[pl.ds(at * part, part)] = their_right_ref[order_ref[at]]

        own = stepped(mine_ref[...], left_ref[...], right_ref[...], scale).astype(jnp.bfloat16)
        other = stepped(theirs_ref[...], their_left_ref[...], ordered[...], scale).astype(jnp.bfloat16)
        out_ref[...] = halved_sum(own, other)

    count = left.shape[1]
    return into_rows(
        body,
        (order, mine, left, right, theirs, their_left, their_right),
        [pl.BlockSpec(memory_space=pltpu.SMEM)]
        + [rows_spec(), rows_spec(0, count), whole_spec(right)]
        + [rows_spec(), pl.BlockSpec((BLOCK, count), lambda i: (i, D // count)), whole_spec(their_right)],
        None,
        0,
        rows,
        units,
        cost(2, rows, 3),
        "mean_of_steps",
        after,
        [pltpu.VMEM((count, D), jnp.bfloat16)],
    )


def partial_sums(order, hidden, d_gate, d_up, gate_w, up_w, down_w, after):
    units, count = hidden.shape
    devices = order.shape[0]
    part = count // devices
    block = block_of(units, 432)
    steps = units // block

    def body(order_ref, hidden_ref, d_gate_ref, d_up_ref, gate_ref, up_ref, down_ref, *rest):
        out, layer, grad = rest[-3:]

        @pl.when(pl.program_id(0) == 0)
        def _():
            layer[...] = jnp.zeros_like(layer)
            grad[...] = jnp.zeros_like(grad)

        layer[...] += mm(hidden_ref[...], down_ref[...], ((0,), (0,)))
        grad[...] += mm(d_gate_ref[...], gate_ref[...], ((0,), (0,))) + mm(d_up_ref[...], up_ref[...], ((0,), (0,)))

        @pl.when(pl.program_id(0) == steps - 1)
        def _():
            for at in range(devices):
                owner = order_ref[at]
                out[owner, 0] = (layer[pl.ds(at * part, part)] * hidden_scale).astype(jnp.bfloat16)
                out[owner, 1] = (grad[pl.ds(at * part, part)] * width_scale).astype(jnp.bfloat16)

    out = jax.ShapeDtypeStruct((devices, 2, part, D), jnp.bfloat16)
    return pl.pallas_call(
        body,
        grid=(steps,),
        in_specs=[pl.BlockSpec(memory_space=pltpu.SMEM)]
        + [rows_spec(0, count, block)] * 3
        + [rows_spec(block=block)] * 3
        + [ANY] * len(after),
        out_specs=whole_spec(out),
        out_shape=out,
        scratch_shapes=[pltpu.VMEM((count, D), jnp.float32)] * 2,
        compiler_params=PARAMS,
        cost_estimate=cost(3, units, 3),
        name="partial_sums",
    )(order, hidden, d_gate, d_up, gate_w, up_w, down_w, *after)


def sum_parts(parts):
    def body(parts_ref, layer_ref, grad_ref):
        for at, out_ref in enumerate((layer_ref, grad_ref)):
            total = parts_ref[0, at].astype(jnp.float32)
            for sender in range(1, parts.shape[0]):
                total += parts_ref[sender, at].astype(jnp.float32)
            out_ref[...] = total.astype(jnp.bfloat16)

    out = jax.ShapeDtypeStruct(parts.shape[2:], jnp.bfloat16)
    return pl.pallas_call(
        body,
        out_shape=[out] * 2,
        compiler_params=PARAMS,
        cost_estimate=cost(0, parts.shape[0] * 2 * parts.shape[2], 1),
        name="sum_parts",
    )(parts)


def packed(weight, rows, tail):
    part = tail.shape[0]

    def body(weight_ref, tail_ref, out_ref, sems):
        copies = [
            pltpu.make_async_copy(weight_ref.at[pl.ds(at, BLOCK)], out_ref.at[pl.ds(at, BLOCK)], sems.at[at // BLOCK])
            for at in range(0, rows, BLOCK)
        ]
        copies.append(pltpu.make_async_copy(tail_ref, out_ref.at[pl.ds(rows, part)], sems.at[rows // BLOCK]))
        for copy in copies:
            copy.start()
        for copy in copies:
            copy.wait()

    return pl.pallas_call(
        body,
        in_specs=[ANY, ANY],
        out_specs=ANY,
        out_shape=jax.ShapeDtypeStruct((rows + part, D), weight.dtype),
        scratch_shapes=[pltpu.SemaphoreType.DMA((rows // BLOCK + 1,))],
        compiler_params=PARAMS,
        cost_estimate=cost(0, rows, 2),
        name="packed",
    )(weight, tail)


def last_rows(x, rows):
    at = (x.shape[0] - rows) // 16

    def body(x_ref, out_ref):
        out_ref[...] = x_ref[...]

    return pl.pallas_call(
        body,
        grid=(rows // 16,),
        in_specs=[pl.BlockSpec((16, D), lambda i: (i + at, 0))],
        out_specs=pl.BlockSpec((16, D), lambda i: (i, 0)),
        out_shape=jax.ShapeDtypeStruct((rows, D), x.dtype),
        compiler_params=PARAMS,
        cost_estimate=cost(0, rows, 2),
        name="last_rows",
    )(x)


def whole_step(distance, turned, tokens_local, grads_local, gate_w, up_w, down_w):
    units = gate_w.shape[0]
    devices = lax.axis_size("tp")
    ring = ring_of(devices)

    def send(x):
        replicas = lax.axis_size("rep")
        return lax.ppermute(x, "rep", [(i, (i + distance) % replicas) for i in range(replicas)])

    def along(x, by):
        return lax.ppermute(x, "tp", [(ring[i], ring[(i + by) % devices]) for i in range(devices)])

    blocks = units // BLOCK
    raw = (blocks if distance == 1 else blocks // 2) * BLOCK
    theirs_raw = send(packed(up_w, raw, tokens_local))

    def from_the_ring(turn, tokens_local, grads_local):
        token_blocks, grad_blocks = [tokens_local] * devices, [grads_local] * devices
        for hop in range(1, devices // 2 + 1):
            for held, last_way in ((token_blocks, turn), (grad_blocks, -turn)):
                for way in (turn, -turn):
                    if hop < devices // 2 or way == last_way:
                        held[-way * hop] = along(held[-way * (hop - 1)], way)
        tokens, grads, hidden, d_gate, d_up = forward(token_blocks, grad_blocks, gate_w, up_w, down_w)
        if raw < units:
            first = step_rows(up_w, d_up, tokens, width_scale, raw, units - raw, beside=d_up)
        else:
            first = step_rows(down_w, hidden, grads, hidden_scale, 0, units, beside=d_up)
        return tokens, grads, hidden, d_gate, d_up, first

    orders = [[ring[(ring.index(own) + at) % devices] for at in range(devices)] for own in range(devices)]
    order = jnp.array(orders, jnp.int32)[lax.axis_index("tp")]

    tokens, grads, hidden, d_gate, d_up, first = lax.cond(
        turned, partial(from_the_ring, 1), partial(from_the_ring, -1), tokens_local, grads_local
    )
    their_first = send(first)
    landed = [theirs_raw, their_first]
    long_step = cost(20, units, 40)
    if raw < units:
        down_new = step_rows(down_w, hidden, grads, hidden_scale, 0, units, landed[:1], costs=long_step)
        their_down = send(down_new)
        landed = [their_first, their_down]
    else:
        down_new, their_down = first, their_first
    cut = units - BLOCK
    gate_head = step_rows(gate_w, d_gate, tokens, width_scale, 0, cut, landed[:1], costs=long_step)
    their_gate_head = send(gate_head)
    gate_tail = step_rows(gate_w, d_gate, tokens, width_scale, cut, BLOCK, landed[1:])
    their_gate_tail = send(gate_tail)

    their_tokens = lax.all_gather(last_rows(theirs_raw, tokens_local.shape[0]), "tp", axis=0)
    parts = partial_sums(order, hidden, d_gate, d_up, gate_w, up_w, down_w, (theirs_raw,))
    parts = lax.all_to_all(parts, "tp", split_axis=0, concat_axis=0, tiled=True)
    layer_out, grad_in = sum_parts(parts)

    new_up = mean_of_steps(
        order, up_w, d_up, tokens, theirs_raw, their_first, their_tokens, width_scale, raw, units, (gate_tail,)
    )
    if raw < units:
        new_up = mean_rows(first, their_first, new_up, raw, units)
    new_down = mean_rows(down_new, their_down, None, 0, units, (new_up,))
    new_gate = mean_rows(gate_head, their_gate_head, None, 0, units, (new_down, layer_out))
    new_gate = mean_rows(gate_tail, their_gate_tail, new_gate, cut, units)
    return layer_out, grad_in, new_gate, new_up, new_down


def shards(activations, out_grad, gate_weight, up_weight, down_weight, step_index):
    levels = lax.axis_size("rep").bit_length() - 1
    branches = [partial(whole_step, 1 << level) for level in range(levels)]
    layer_out, grad_in, gate, up, down = lax.switch(
        step_index[0] % levels,
        branches,
        (step_index[0] // levels) % 2 == 0,
        activations[0],
        out_grad[0],
        gate_weight[0].T,
        up_weight[0].T,
        down_weight[0],
    )
    return layer_out[None], grad_in[None], gate.T[None], up.T[None], down[None]


def solution(mesh):
    in_specs = (
        P("rep", "tp", None),
        P("rep", "tp", None),
        P("rep", None, "tp"),
        P("rep", None, "tp"),
        P("rep", "tp", None),
        P(),
    )
    out_specs = (
        P("rep", "tp", None),
        P("rep", "tp", None),
        P("rep", None, "tp"),
        P("rep", None, "tp"),
        P("rep", "tp", None),
    )
    return jax.shard_map(shards, mesh=mesh, in_specs=in_specs, out_specs=out_specs, check_vma=False)
```

```python
from functools import partial
import math

import jax
import jax.numpy as jnp
from jax import lax
from jax.experimental import pallas as pl
from jax.experimental.pallas import tpu as pltpu
from jax.sharding import PartitionSpec as P

D = 2560
FF = 6912
BLOCK = 144


learn_rate = 0.8
width_scale = 1.0 / math.sqrt(D)
hidden_scale = 1.0 / math.sqrt(FF)

ANY = pl.BlockSpec(memory_space=pl.ANY)
PARAMS = pltpu.CompilerParams(vmem_limit_bytes=40 * 1024 * 1024)


def ring_of(devices):
    y_size = 1 << ((devices.bit_length() - 1) // 2)
    z_size = devices // y_size
    walk = [(z, 0) for z in range(z_size)]
    for z in reversed(range(z_size)):
        ys = list(range(1, y_size))
        walk += [(z, y) for y in (ys if (z_size - 1 - z) % 2 == 0 else reversed(ys))]
    return [z * y_size + y for z, y in walk]


def mm(a, b, dims):
    return lax.dot_general(a, b, (dims, ((), ())), preferred_element_type=jnp.float32)


def cost(matmuls, rows, blocks_moved):
    return pl.CostEstimate(
        flops=2 * matmuls * rows * 256 * D, bytes_accessed=blocks_moved * rows * D * 2, transcendentals=0
    )


def rows_spec(first=0, width=D, block=BLOCK):
    return pl.BlockSpec((block, width), lambda i: (i + first, 0))


def block_of(units, most):
    return max(size for size in range(BLOCK, most + 1, BLOCK) if units % size == 0)


def whole_spec(x):
    return pl.BlockSpec(x.shape, lambda i: (0,) * x.ndim)


def forward(token_blocks, grad_blocks, gate_w, up_w, down_w, after):
    units, devices = gate_w.shape[0], len(token_blocks)
    part = token_blocks[0].shape[0]
    count = devices * part
    block = block_of(units, 288)

    def body(*refs):
        gate_ref, up_ref, down_ref = refs[2 * devices : 2 * devices + 3]
        tokens_ref, grads_ref, hidden_ref, d_gate_ref, d_up_ref, turned, turned_grads = refs[-7:]

        @pl.when(pl.program_id(0) == 0)
        def _():
            for at in range(devices):
                tokens_ref[pl.ds(at * part, part)] = refs[at][...]
                grads_ref[pl.ds(at * part, part)] = refs[devices + at][...]
            turned[...] = tokens_ref[...].T
            turned_grads[...] = grads_ref[...].T

        gate_pre = mm(gate_ref[...], turned[...], ((1,), (0,))) * width_scale
        up_pre = mm(up_ref[...], turned[...], ((1,), (0,))) * width_scale
        d_hidden = mm(down_ref[...], turned_grads[...], ((1,), (0,))) * hidden_scale
        sigmoid_gate = jax.nn.sigmoid(gate_pre)
        activated = gate_pre * sigmoid_gate
        slope = sigmoid_gate * (1.0 + gate_pre * (1.0 - sigmoid_gate))
        hidden_ref[...] = (activated * up_pre).astype(jnp.bfloat16)
        d_gate_ref[...] = (d_hidden * up_pre * slope).astype(jnp.bfloat16)
        d_up_ref[...] = (d_hidden * activated).astype(jnp.bfloat16)

    whole = jax.ShapeDtypeStruct((count, D), jnp.bfloat16)
    out = jax.ShapeDtypeStruct((units, count), jnp.bfloat16)
    pieces = [*token_blocks, *grad_blocks]
    return pl.pallas_call(
        body,
        grid=(units // block,),
        in_specs=[whole_spec(piece) for piece in pieces] + [rows_spec(block=block)] * 3 + [ANY] * len(after),
        out_specs=[whole_spec(whole)] * 2 + [rows_spec(0, count, block)] * 3,
        out_shape=[whole] * 2 + [out] * 3,
        scratch_shapes=[pltpu.VMEM((D, count), jnp.bfloat16)] * 2,
        compiler_params=PARAMS,
        cost_estimate=cost(3, units, 3),
        name="forward",
    )(*pieces, gate_w, up_w, down_w, *after)


def stepped(weight, left, right, scale):
    return weight.astype(jnp.float32) - learn_rate * (mm(left, right, ((1,), (0,))) * scale)


def step_rows(weight, left, right, scale, first, rows, after=(), beside=None, costs=None):
    at = first // BLOCK
    count = left.shape[1]
    ins, specs, width = (weight, left, right), [rows_spec(at), rows_spec(at, count), whole_spec(right)], D
    if beside is not None:
        ins, specs, width = (*ins, beside), specs + [rows_spec(0, count)], D + count

    def body(weight_ref, left_ref, right_ref, *rest):
        out_ref = rest[-1]
        out_ref[:, :D] = stepped(weight_ref[...], left_ref[...], right_ref[...], scale).astype(jnp.bfloat16)
        if beside is not None:
            out_ref[:, D:] = rest[0][...]

    return pl.pallas_call(
        body,
        grid=(rows // BLOCK,),
        in_specs=specs + [ANY] * len(after),
        out_specs=rows_spec(0, width),
        out_shape=jax.ShapeDtypeStruct((rows, width), jnp.bfloat16),
        compiler_params=PARAMS,
        cost_estimate=costs or cost(1, rows, 2),
        name="step_rows",
    )(*ins, *after)


def halved_sum(mine, theirs):
    return ((mine.astype(jnp.float32) + theirs.astype(jnp.float32)) * 0.5).astype(jnp.bfloat16)


def into_rows(body, ins, in_specs, base, first, rows, units, costs, name, after, scratch=(), block=BLOCK):
    others = after if base is None else (base, *after)

    def with_others(*refs):
        body(*refs[: len(ins)], *refs[len(ins) + len(others) :])
    return pl.pallas_call(
        with_others,
        grid=(rows // block,),
        in_specs=in_specs + [ANY] * len(others),
        out_specs=rows_spec(first // block, block=block),
        out_shape=jax.ShapeDtypeStruct((units, D), jnp.bfloat16),
        input_output_aliases={} if base is None else {len(ins): 0},
        scratch_shapes=scratch,
        compiler_params=PARAMS,
        cost_estimate=costs,
        name=name,
    )(*ins, *others)


def mean_rows(mine, theirs, base, first, units, after=()):
    def body(mine_ref, theirs_ref, out_ref):
        out_ref[...] = halved_sum(mine_ref[...], theirs_ref[...])

    rows = theirs.shape[0]
    block = BLOCK if rows > BLOCK else BLOCK // 3
    specs = [rows_spec(block=block)] * 2
    costs = cost(0, rows, 3)
    return into_rows(
        body, (mine, theirs), specs, base, first, rows, units, costs, "mean_rows", after, block=block
    )


def mean_of_steps(order, mine, left, right, theirs, their_left, their_right, scale, rows, units, after):
    devices, part, _ = their_right.shape

    def body(order_ref, mine_ref, left_ref, right_ref, theirs_ref, their_left_ref, their_right_ref, out_ref, ordered):
        @pl.when(pl.program_id(0) == 0)
        def _():
            for at in range(devices):
                ordered[pl.ds(at * part, part)] = their_right_ref[order_ref[at]]

        own = stepped(mine_ref[...], left_ref[...], right_ref[...], scale).astype(jnp.bfloat16)
        other = stepped(theirs_ref[...], their_left_ref[...], ordered[...], scale).astype(jnp.bfloat16)
        out_ref[...] = halved_sum(own, other)

    count = left.shape[1]
    return into_rows(
        body,
        (order, mine, left, right, theirs, their_left, their_right),
        [pl.BlockSpec(memory_space=pltpu.SMEM)]
        + [rows_spec(), rows_spec(0, count), whole_spec(right)]
        + [rows_spec(), pl.BlockSpec((BLOCK, count), lambda i: (i, D // count)), whole_spec(their_right)],
        None,
        0,
        rows,
        units,
        cost(2, rows, 3),
        "mean_of_steps",
        after,
        [pltpu.VMEM((count, D), jnp.bfloat16)],
    )


def partial_sums(order, hidden, d_gate, d_up, gate_w, up_w, down_w, after):
    units, count = hidden.shape
    devices = order.shape[0]
    part = count // devices
    block = block_of(units, 432)
    steps = units // block

    def body(order_ref, hidden_ref, d_gate_ref, d_up_ref, gate_ref, up_ref, down_ref, *rest):
        out, layer, grad = rest[-3:]

        @pl.when(pl.program_id(0) == 0)
        def _():
            layer[...] = jnp.zeros_like(layer)
            grad[...] = jnp.zeros_like(grad)

        layer[...] += mm(hidden_ref[...], down_ref[...], ((0,), (0,)))
        grad[...] += mm(d_gate_ref[...], gate_ref[...], ((0,), (0,))) + mm(d_up_ref[...], up_ref[...], ((0,), (0,)))

        @pl.when(pl.program_id(0) == steps - 1)
        def _():
            for at in range(devices):
                owner = order_ref[at]
                out[owner, 0] = (layer[pl.ds(at * part, part)] * hidden_scale).astype(jnp.bfloat16)
                out[owner, 1] = (grad[pl.ds(at * part, part)] * width_scale).astype(jnp.bfloat16)

    out = jax.ShapeDtypeStruct((devices, 2, part, D), jnp.bfloat16)
    return pl.pallas_call(
        body,
        grid=(steps,),
        in_specs=[pl.BlockSpec(memory_space=pltpu.SMEM)]
        + [rows_spec(0, count, block)] * 3
        + [rows_spec(block=block)] * 3
        + [ANY] * len(after),
        out_specs=whole_spec(out),
        out_shape=out,
        scratch_shapes=[pltpu.VMEM((count, D), jnp.float32)] * 2,
        compiler_params=PARAMS,
        cost_estimate=cost(3, units, 3),
        name="partial_sums",
    )(order, hidden, d_gate, d_up, gate_w, up_w, down_w, *after)


def sum_parts(parts):
    def body(parts_ref, layer_ref, grad_ref):
        for at, out_ref in enumerate((layer_ref, grad_ref)):
            total = parts_ref[0, at].astype(jnp.float32)
            for sender in range(1, parts.shape[0]):
                total += parts_ref[sender, at].astype(jnp.float32)
            out_ref[...] = total.astype(jnp.bfloat16)

    out = jax.ShapeDtypeStruct(parts.shape[2:], jnp.bfloat16)
    return pl.pallas_call(
        body,
        out_shape=[out] * 2,
        compiler_params=PARAMS,
        cost_estimate=cost(0, parts.shape[0] * 2 * parts.shape[2], 1),
        name="sum_parts",
    )(parts)


def relay(x, after):
    def body(x_ref, *rest):
        rest[-1][...] = x_ref[...]

    return pl.pallas_call(
        body,
        in_specs=[pl.BlockSpec(memory_space=pltpu.VMEM)] + [ANY] * len(after),
        out_specs=pl.BlockSpec(memory_space=pltpu.VMEM),
        out_shape=jax.ShapeDtypeStruct(x.shape, x.dtype),
        compiler_params=PARAMS,
        cost_estimate=cost(0, x.shape[0], 2),
        name="relay",
    )(x, *after)


def whole_step(distance, turned, tokens_local, grads_local, gate_w, up_w, down_w):
    units = gate_w.shape[0]
    devices = lax.axis_size("tp")
    ring = ring_of(devices)

    def send(x):
        replicas = lax.axis_size("rep")
        return lax.ppermute(x, "rep", [(i, (i + distance) % replicas) for i in range(replicas)])

    def along(x, by):
        return lax.ppermute(x, "tp", [(ring[i], ring[(i + by) % devices]) for i in range(devices)])

    blocks = units // BLOCK
    raw = (blocks if distance == 1 else blocks // 2) * BLOCK
    their_tokens = send(tokens_local)
    their_tokens, up_sent = lax.optimization_barrier((their_tokens, up_w[:raw]))
    theirs_raw = send(up_sent)

    def from_the_ring(turn, tokens_local, grads_local):
        token_blocks, grad_blocks = [tokens_local] * devices, [grads_local] * devices
        for hop in range(1, devices // 2 + 1):
            for held, last_way in ((token_blocks, turn), (grad_blocks, -turn)):
                for way in (turn, -turn):
                    if hop < devices // 2 or way == last_way:
                        held[-way * hop] = along(held[-way * (hop - 1)], way)
        return token_blocks[1:], grad_blocks[1:]

    orders = [[ring[(ring.index(own) + at) % devices] for at in range(devices)] for own in range(devices)]
    order = jnp.array(orders, jnp.int32)[lax.axis_index("tp")]

    token_blocks, grad_blocks = lax.cond(
        turned, partial(from_the_ring, 1), partial(from_the_ring, -1), tokens_local, grads_local
    )
    their_tokens = relay(their_tokens, token_blocks[:1])
    tokens, grads, hidden, d_gate, d_up = forward(
        [tokens_local, *token_blocks], [grads_local, *grad_blocks], gate_w, up_w, down_w, (their_tokens,)
    )
    their_tokens = lax.all_gather(their_tokens, "tp", axis=0)
    if raw < units:
        first = step_rows(up_w, d_up, tokens, width_scale, raw, units - raw, beside=d_up)
    else:
        first = step_rows(down_w, hidden, grads, hidden_scale, 0, units, beside=d_up)
    their_first = send(first)
    landed = [theirs_raw, their_first]
    long_step = cost(20, units, 40)
    if raw < units:
        down_new = step_rows(down_w, hidden, grads, hidden_scale, 0, units, landed[:1], costs=long_step)
        their_down = send(down_new)
        landed = [their_first, their_down]
    else:
        down_new, their_down = first, their_first
    cut = units - BLOCK
    gate_head = step_rows(gate_w, d_gate, tokens, width_scale, 0, cut, landed[:1], costs=long_step)
    their_gate_head = send(gate_head)
    gate_tail = step_rows(gate_w, d_gate, tokens, width_scale, cut, BLOCK, (landed[1], their_tokens))
    their_gate_tail = send(gate_tail)

    parts = partial_sums(order, hidden, d_gate, d_up, gate_w, up_w, down_w, (theirs_raw,))
    parts = lax.all_to_all(parts, "tp", split_axis=0, concat_axis=0, tiled=True)
    layer_out, grad_in = sum_parts(parts)

    new_up = mean_of_steps(
        order, up_w, d_up, tokens, theirs_raw, their_first, their_tokens, width_scale, raw, units, (gate_tail,)
    )
    if raw < units:
        new_up = mean_rows(first, their_first, new_up, raw, units)
    new_down = mean_rows(down_new, their_down, None, 0, units, (new_up,))
    new_gate = mean_rows(gate_head, their_gate_head, None, 0, units, (new_down, layer_out))
    new_gate = mean_rows(gate_tail, their_gate_tail, new_gate, cut, units)
    return layer_out, grad_in, new_gate, new_up, new_down


def shards(activations, out_grad, gate_weight, up_weight, down_weight, step_index):
    levels = lax.axis_size("rep").bit_length() - 1
    branches = [partial(whole_step, 1 << level) for level in range(levels)]
    layer_out, grad_in, gate, up, down = lax.switch(
        step_index[0] % levels,
        branches,
        (step_index[0] // levels) % 2 == 0,
        activations[0],
        out_grad[0],
        gate_weight[0].T,
        up_weight[0].T,
        down_weight[0],
    )
    return layer_out[None], grad_in[None], gate.T[None], up.T[None], down[None]


def solution(mesh):
    in_specs = (
        P("rep", "tp", None),
        P("rep", "tp", None),
        P("rep", None, "tp"),
        P("rep", None, "tp"),
        P("rep", "tp", None),
        P(),
    )
    out_specs = (
        P("rep", "tp", None),
        P("rep", "tp", None),
        P("rep", None, "tp"),
        P("rep", None, "tp"),
        P("rep", "tp", None),
    )
    return jax.shard_map(shards, mesh=mesh, in_specs=in_specs, out_specs=out_specs, check_vma=False)
```

```python
from functools import partial
import math

import jax
import jax.numpy as jnp
from jax import lax
from jax.experimental import pallas as pl
from jax.experimental.pallas import tpu as pltpu
from jax.sharding import PartitionSpec as P

D = 2560
FF = 6912
BLOCK = 144


learn_rate = 0.8
width_scale = 1.0 / math.sqrt(D)
hidden_scale = 1.0 / math.sqrt(FF)

ANY = pl.BlockSpec(memory_space=pl.ANY)
PARAMS = pltpu.CompilerParams(vmem_limit_bytes=40 * 1024 * 1024)


def ring_of(devices):
    y_size = 1 << ((devices.bit_length() - 1) // 2)
    z_size = devices // y_size
    walk = [(z, 0) for z in range(z_size)]
    for z in reversed(range(z_size)):
        ys = list(range(1, y_size))
        walk += [(z, y) for y in (ys if (z_size - 1 - z) % 2 == 0 else reversed(ys))]
    return [z * y_size + y for z, y in walk]


def mm(a, b, dims):
    return lax.dot_general(a, b, (dims, ((), ())), preferred_element_type=jnp.float32)


def cost(matmuls, rows, blocks_moved):
    return pl.CostEstimate(
        flops=2 * matmuls * rows * 256 * D, bytes_accessed=blocks_moved * rows * D * 2, transcendentals=0
    )


def rows_spec(first=0, width=D, block=BLOCK):
    return pl.BlockSpec((block, width), lambda i: (i + first, 0))


def block_of(units, most):
    return max(size for size in range(BLOCK, most + 1, BLOCK) if units % size == 0)


def whole_spec(x):
    return pl.BlockSpec(x.shape, lambda i: (0,) * x.ndim)


def forward(token_blocks, grad_blocks, gate_w, up_w, down_w):
    units, devices = gate_w.shape[0], len(token_blocks)
    part = token_blocks[0].shape[0]
    count = devices * part
    block = block_of(units, 288)

    def body(*refs):
        gate_ref, up_ref, down_ref = refs[2 * devices : 2 * devices + 3]
        tokens_ref, grads_ref, hidden_ref, d_gate_ref, d_up_ref, turned, turned_grads = refs[-7:]

        @pl.when(pl.program_id(0) == 0)
        def _():
            for at in range(devices):
                tokens_ref[pl.ds(at * part, part)] = refs[at][...]
                grads_ref[pl.ds(at * part, part)] = refs[devices + at][...]
            turned[...] = tokens_ref[...].T
            turned_grads[...] = grads_ref[...].T

        gate_pre = mm(gate_ref[...], turned[...], ((1,), (0,))) * width_scale
        up_pre = mm(up_ref[...], turned[...], ((1,), (0,))) * width_scale
        d_hidden = mm(down_ref[...], turned_grads[...], ((1,), (0,))) * hidden_scale
        sigmoid_gate = jax.nn.sigmoid(gate_pre)
        activated = gate_pre * sigmoid_gate
        slope = sigmoid_gate * (1.0 + gate_pre * (1.0 - sigmoid_gate))
        hidden_ref[...] = (activated * up_pre).astype(jnp.bfloat16)
        d_gate_ref[...] = (d_hidden * up_pre * slope).astype(jnp.bfloat16)
        d_up_ref[...] = (d_hidden * activated).astype(jnp.bfloat16)

    whole = jax.ShapeDtypeStruct((count, D), jnp.bfloat16)
    out = jax.ShapeDtypeStruct((units, count), jnp.bfloat16)
    pieces = [*token_blocks, *grad_blocks]
    return pl.pallas_call(
        body,
        grid=(units // block,),
        in_specs=[whole_spec(piece) for piece in pieces] + [rows_spec(block=block)] * 3,
        out_specs=[whole_spec(whole)] * 2 + [rows_spec(0, count, block)] * 3,
        out_shape=[whole] * 2 + [out] * 3,
        scratch_shapes=[pltpu.VMEM((D, count), jnp.bfloat16)] * 2,
        compiler_params=PARAMS,
        cost_estimate=cost(3, units, 3),
        name="forward",
    )(*pieces, gate_w, up_w, down_w)


def stepped(weight, left, right, scale):
    return weight.astype(jnp.float32) - learn_rate * (mm(left, right, ((1,), (0,))) * scale)


def step_rows(weight, left, right, scale, first, rows, after=(), beside=None, costs=None):
    at = first // BLOCK
    count = left.shape[1]
    ins, specs, width = (weight, left, right), [rows_spec(at), rows_spec(at, count), whole_spec(right)], D
    if beside is not None:
        ins, specs, width = (*ins, beside), specs + [rows_spec(0, count)], D + count

    def body(weight_ref, left_ref, right_ref, *rest):
        out_ref = rest[-1]
        out_ref[:, :D] = stepped(weight_ref[...], left_ref[...], right_ref[...], scale).astype(jnp.bfloat16)
        if beside is not None:
            out_ref[:, D:] = rest[0][...]

    return pl.pallas_call(
        body,
        grid=(rows // BLOCK,),
        in_specs=specs + [ANY] * len(after),
        out_specs=rows_spec(0, width),
        out_shape=jax.ShapeDtypeStruct((rows, width), jnp.bfloat16),
        compiler_params=PARAMS,
        cost_estimate=costs or cost(1, rows, 2),
        name="step_rows",
    )(*ins, *after)


def halved_sum(mine, theirs):
    return ((mine.astype(jnp.float32) + theirs.astype(jnp.float32)) * 0.5).astype(jnp.bfloat16)


def into_rows(body, ins, in_specs, base, first, rows, units, costs, name, after, scratch=(), block=BLOCK):
    others = after if base is None else (base, *after)

    def with_others(*refs):
        body(*refs[: len(ins)], *refs[len(ins) + len(others) :])
    return pl.pallas_call(
        with_others,
        grid=(rows // block,),
        in_specs=in_specs + [ANY] * len(others),
        out_specs=rows_spec(first // block, block=block),
        out_shape=jax.ShapeDtypeStruct((units, D), jnp.bfloat16),
        input_output_aliases={} if base is None else {len(ins): 0},
        scratch_shapes=scratch,
        compiler_params=PARAMS,
        cost_estimate=costs,
        name=name,
    )(*ins, *others)


def mean_rows(mine, theirs, base, first, units, after=()):
    def body(mine_ref, theirs_ref, out_ref):
        out_ref[...] = halved_sum(mine_ref[...], theirs_ref[...])

    rows = theirs.shape[0]
    block = BLOCK if rows > BLOCK else BLOCK // 3
    specs = [rows_spec(block=block)] * 2
    costs = cost(0, rows, 3)
    return into_rows(
        body, (mine, theirs), specs, base, first, rows, units, costs, "mean_rows", after, block=block
    )


def mean_of_steps(mine, left, right, theirs, their_left, their_blocks, scale, rows, units, after):
    part = their_blocks[0].shape[0]

    def body(mine_ref, left_ref, right_ref, theirs_ref, their_left_ref, *rest):
        out_ref, their_right = rest[-2:]

        @pl.when(pl.program_id(0) == 0)
        def _():
            for at in range(len(their_blocks)):
                their_right[pl.ds(at * part, part)] = rest[at][...]

        own = stepped(mine_ref[...], left_ref[...], right_ref[...], scale).astype(jnp.bfloat16)
        other = stepped(theirs_ref[...], their_left_ref[...], their_right[...], scale).astype(jnp.bfloat16)
        out_ref[...] = halved_sum(own, other)

    count = left.shape[1]
    return into_rows(
        body,
        (mine, left, right, theirs, their_left, *their_blocks),
        [rows_spec(), rows_spec(0, count), whole_spec(right)]
        + [rows_spec(), pl.BlockSpec((BLOCK, count), lambda i: (i, D // count))]
        + [whole_spec(block) for block in their_blocks],
        None,
        0,
        rows,
        units,
        cost(2, rows, 3),
        "mean_of_steps",
        after,
        [pltpu.VMEM((count, D), jnp.bfloat16)],
    )


def partial_sums(hidden, d_gate, d_up, gate_w, up_w, down_w, after):
    units, count = hidden.shape
    block = block_of(units, 432)
    steps = units // block

    def body(hidden_ref, d_gate_ref, d_up_ref, gate_ref, up_ref, down_ref, *rest):
        layer_ref, grad_ref = rest[-2:]

        @pl.when(pl.program_id(0) == 0)
        def _():
            layer_ref[...] = jnp.zeros_like(layer_ref)
            grad_ref[...] = jnp.zeros_like(grad_ref)

        layer_ref[...] += mm(hidden_ref[...], down_ref[...], ((0,), (0,))) * hidden_scale
        grad_sum = mm(d_gate_ref[...], gate_ref[...], ((0,), (0,))) + mm(d_up_ref[...], up_ref[...], ((0,), (0,)))
        grad_ref[...] += grad_sum * width_scale

    out = jax.ShapeDtypeStruct((count, D), jnp.float32)
    return pl.pallas_call(
        body,
        grid=(steps,),
        in_specs=[rows_spec(0, count, block)] * 3 + [rows_spec(block=block)] * 3 + [ANY] * len(after),
        out_specs=[whole_spec(out)] * 2,
        out_shape=[out] * 2,
        compiler_params=PARAMS,
        cost_estimate=cost(3, units, 3),
        name="partial_sums",
    )(hidden, d_gate, d_up, gate_w, up_w, down_w, *after)


def whole_step(distance, turned, tokens_local, grads_local, gate_w, up_w, down_w):
    units = gate_w.shape[0]
    devices = lax.axis_size("tp")
    ring = ring_of(devices)

    def send(x):
        replicas = lax.axis_size("rep")
        return lax.ppermute(x, "rep", [(i, (i + distance) % replicas) for i in range(replicas)])

    def along(x, by):
        return lax.ppermute(x, "tp", [(ring[i], ring[(i + by) % devices]) for i in range(devices)])

    blocks = units // BLOCK
    raw = (blocks if distance == 1 else blocks // 2) * BLOCK
    their_tokens = send(tokens_local)
    their_tokens, up_sent = lax.optimization_barrier((their_tokens, up_w[:raw]))
    theirs_raw = send(up_sent)

    half = devices // 2

    def gather(turn, locals_):
        held = [[x] * devices for x in locals_]
        for hop in range(1, half + 1):
            for at, blocks_held in enumerate(held):
                last_way = turn if at % 2 == 0 else -turn
                for way in (turn, -turn):
                    if hop < half or way == last_way:
                        blocks_held[-way * hop] = along(blocks_held[-way * (hop - 1)], way)
        return [blocks_held[1:] for blocks_held in held]

    def sums(turn, terms):
        part = terms[0].shape[0] // devices
        block_at = lambda term, offset: term[(offset % devices) * part : (offset % devices + 1) * part]
        ways = [(at, way, half - (0 if (way == turn) == (at == 0) else 1)) for at in (0, 1) for way in (turn, -turn)]
        moving = {}
        for hop in range(1, half + 1):
            for at, way, hops in ways:
                if hop <= hops:
                    block = block_at(terms[at], way * (hops + 1 - hop))
                    if hop > 1:
                        block = block + moving[at, way].astype(jnp.float32)
                    moving[at, way] = along(block.astype(jnp.bfloat16), way)
        totals = []
        for at, term in enumerate(terms):
            total = block_at(term, 0)
            for way in (turn, -turn):
                total = total + moving[at, way].astype(jnp.float32)
            totals.append(total.astype(jnp.bfloat16))
        return totals

    token_blocks, grad_blocks = lax.cond(
        turned, partial(gather, 1), partial(gather, -1), [tokens_local, grads_local]
    )
    tokens, grads, hidden, d_gate, d_up = forward(
        [tokens_local, *token_blocks], [grads_local, *grad_blocks], gate_w, up_w, down_w
    )
    cut = units - BLOCK
    down_step = partial(step_rows, down_w, hidden, grads, hidden_scale, 0, units)
    head_step = partial(step_rows, gate_w, d_gate, tokens, width_scale, 0, cut)
    long_step = cost(20, units, 40)
    if raw < units:
        first = step_rows(up_w, d_up, tokens, width_scale, raw, units - raw, beside=d_up)
        their_first = send(first)
        second = down_new = down_step((theirs_raw,), costs=long_step)
        their_down = send(down_new)
    else:
        first = down_new = down_step(beside=d_up)
        their_first = their_down = send(down_new)
        second = gate_head = head_step((theirs_raw,), costs=long_step)
        their_gate_head = send(gate_head)
    terms = partial_sums(hidden, d_gate, d_up, gate_w, up_w, down_w, (second,))
    layer_out, grad_in = lax.cond(turned, partial(sums, 1), partial(sums, -1), terms)
    their_tokens, layer_out = lax.optimization_barrier((their_tokens, layer_out))
    (their_blocks,) = lax.cond(turned, partial(gather, 1), partial(gather, -1), [their_tokens])
    if raw < units:
        gate_head = head_step((their_first, layer_out))
        their_gate_head = send(gate_head)
    gate_tail = step_rows(gate_w, d_gate, tokens, width_scale, cut, BLOCK, (their_down, layer_out))
    their_gate_tail = send(gate_tail)

    new_up = mean_of_steps(
        up_w,
        d_up,
        tokens,
        theirs_raw,
        their_first,
        [their_tokens, *their_blocks],
        width_scale,
        raw,
        units,
        (gate_tail,),
    )
    if raw < units:
        new_up = mean_rows(first, their_first, new_up, raw, units)
    new_down = mean_rows(down_new, their_down, None, 0, units, (new_up,))
    new_gate = mean_rows(gate_head, their_gate_head, None, 0, units, (new_down,))
    new_gate = mean_rows(gate_tail, their_gate_tail, new_gate, cut, units)
    return layer_out, grad_in, new_gate, new_up, new_down


def shards(activations, out_grad, gate_weight, up_weight, down_weight, step_index):
    levels = lax.axis_size("rep").bit_length() - 1
    branches = [partial(whole_step, 1 << level) for level in range(levels)]
    layer_out, grad_in, gate, up, down = lax.switch(
        step_index[0] % levels,
        branches,
        (step_index[0] // levels) % 2 == 0,
        activations[0],
        out_grad[0],
        gate_weight[0].T,
        up_weight[0].T,
        down_weight[0],
    )
    return layer_out[None], grad_in[None], gate.T[None], up.T[None], down[None]


def solution(mesh):
    in_specs = (
        P("rep", "tp", None),
        P("rep", "tp", None),
        P("rep", None, "tp"),
        P("rep", None, "tp"),
        P("rep", "tp", None),
        P(),
    )
    out_specs = (
        P("rep", "tp", None),
        P("rep", "tp", None),
        P("rep", None, "tp"),
        P("rep", None, "tp"),
        P("rep", "tp", None),
    )
    return jax.shard_map(shards, mesh=mesh, in_specs=in_specs, out_specs=out_specs, check_vma=False)
```

```python
from functools import partial
import math

import jax
import jax.numpy as jnp
from jax import lax
from jax.experimental import pallas as pl
from jax.experimental.pallas import tpu as pltpu
from jax.sharding import PartitionSpec as P

D = 2560
FF = 6912
BLOCK = 144


learn_rate = 0.8
width_scale = 1.0 / math.sqrt(D)
hidden_scale = 1.0 / math.sqrt(FF)

ANY = pl.BlockSpec(memory_space=pl.ANY)
PARAMS = pltpu.CompilerParams(vmem_limit_bytes=40 * 1024 * 1024)


def ring_of(devices):
    y_size = 1 << ((devices.bit_length() - 1) // 2)
    z_size = devices // y_size
    walk = [(z, 0) for z in range(z_size)]
    for z in reversed(range(z_size)):
        ys = list(range(1, y_size))
        walk += [(z, y) for y in (ys if (z_size - 1 - z) % 2 == 0 else reversed(ys))]
    return [z * y_size + y for z, y in walk]


def mm(a, b, dims):
    return lax.dot_general(a, b, (dims, ((), ())), preferred_element_type=jnp.float32)


def cost(matmuls, rows, blocks_moved):
    return pl.CostEstimate(
        flops=2 * matmuls * rows * 256 * D, bytes_accessed=blocks_moved * rows * D * 2, transcendentals=0
    )


def rows_spec(first=0, width=D, block=BLOCK):
    return pl.BlockSpec((block, width), lambda i: (i + first, 0))


def block_of(units, most):
    return max(size for size in range(BLOCK, most + 1, BLOCK) if units % size == 0)


def whole_spec(x):
    return pl.BlockSpec(x.shape, lambda i: (0,) * x.ndim)


def forward(token_blocks, grad_blocks, gate_w, up_w, down_w):
    units, devices = gate_w.shape[0], len(token_blocks)
    part = token_blocks[0].shape[0]
    count = devices * part
    block = block_of(units, 288)

    def body(*refs):
        gate_ref, up_ref, down_ref = refs[2 * devices : 2 * devices + 3]
        tokens_ref, grads_ref, hidden_ref, d_gate_ref, d_up_ref, turned, turned_grads = refs[-7:]

        @pl.when(pl.program_id(0) == 0)
        def _():
            for at in range(devices):
                tokens_ref[pl.ds(at * part, part)] = refs[at][...]
                grads_ref[pl.ds(at * part, part)] = refs[devices + at][...]
            turned[...] = tokens_ref[...].T
            turned_grads[...] = grads_ref[...].T

        gate_pre = mm(gate_ref[...], turned[...], ((1,), (0,))) * width_scale
        up_pre = mm(up_ref[...], turned[...], ((1,), (0,))) * width_scale
        d_hidden = mm(down_ref[...], turned_grads[...], ((1,), (0,))) * hidden_scale
        sigmoid_gate = jax.nn.sigmoid(gate_pre)
        activated = gate_pre * sigmoid_gate
        slope = sigmoid_gate * (1.0 + gate_pre * (1.0 - sigmoid_gate))
        hidden_ref[...] = (activated * up_pre).astype(jnp.bfloat16)
        d_gate_ref[...] = (d_hidden * up_pre * slope).astype(jnp.bfloat16)
        d_up_ref[...] = (d_hidden * activated).astype(jnp.bfloat16)

    whole = jax.ShapeDtypeStruct((count, D), jnp.bfloat16)
    out = jax.ShapeDtypeStruct((units, count), jnp.bfloat16)
    pieces = [*token_blocks, *grad_blocks]
    return pl.pallas_call(
        body,
        grid=(units // block,),
        in_specs=[whole_spec(piece) for piece in pieces] + [rows_spec(block=block)] * 3,
        out_specs=[whole_spec(whole)] * 2 + [rows_spec(0, count, block)] * 3,
        out_shape=[whole] * 2 + [out] * 3,
        scratch_shapes=[pltpu.VMEM((D, count), jnp.bfloat16)] * 2,
        compiler_params=PARAMS,
        cost_estimate=cost(3, units, 3),
        name="forward",
    )(*pieces, gate_w, up_w, down_w)


def stepped(weight, left, right, scale):
    return weight.astype(jnp.float32) - learn_rate * (mm(left, right, ((1,), (0,))) * scale)


def step_rows(weight, left, right, scale, first, rows, after=(), beside=None, below=None, costs=None):
    at, steps = first // BLOCK, rows // BLOCK
    count = left.shape[1]
    here = lambda i: (jnp.minimum(i, steps - 1) + at, 0)
    ins = (weight, left, right)
    specs = [pl.BlockSpec((BLOCK, D), here), pl.BlockSpec((BLOCK, count), here), whole_spec(right)]
    out_rows, width = rows, D
    if beside is not None:
        ins = (*ins, beside, below)
        specs += [pl.BlockSpec((BLOCK, count), lambda i: (jnp.minimum(i, steps - 1), 0)), whole_spec(below)]
        out_rows, width = rows + below.shape[0], D + count

    def body(weight_ref, left_ref, right_ref, *rest):
        out_ref = rest[-1]

        @pl.when(pl.program_id(0) < steps)
        def _():
            out_ref[:, :D] = stepped(weight_ref[...], left_ref[...], right_ref[...], scale).astype(jnp.bfloat16)
            if beside is not None:
                out_ref[:, D:] = rest[0][...]

        if below is not None:

            @pl.when(pl.program_id(0) == steps)
            def _():
                out_ref[pl.ds(0, below.shape[0]), :D] = rest[1][...]

    return pl.pallas_call(
        body,
        grid=(steps if below is None else steps + 1,),
        in_specs=specs + [ANY] * len(after),
        out_specs=rows_spec(0, width),
        out_shape=jax.ShapeDtypeStruct((out_rows, width), jnp.bfloat16),
        compiler_params=PARAMS,
        cost_estimate=costs or cost(1, rows, 2),
        name="step_rows",
    )(*ins, *after)


def rows_of(x, first, rows, block):
    at = first // block

    def body(x_ref, out_ref):
        out_ref[...] = x_ref[...]

    return pl.pallas_call(
        body,
        grid=(rows // block,),
        in_specs=[rows_spec(at, block=block)],
        out_specs=rows_spec(block=block),
        out_shape=jax.ShapeDtypeStruct((rows, D), x.dtype),
        compiler_params=PARAMS,
        cost_estimate=cost(0, rows, 2),
        name="rows_of",
    )(x)


def halved_sum(mine, theirs):
    return ((mine.astype(jnp.float32) + theirs.astype(jnp.float32)) * 0.5).astype(jnp.bfloat16)


def into_rows(body, ins, in_specs, base, first, rows, units, costs, name, after, scratch=()):
    others = after if base is None else (base, *after)

    def with_others(*refs):
        body(*refs[: len(ins)], *refs[len(ins) + len(others) :])
    return pl.pallas_call(
        with_others,
        grid=(rows // BLOCK,),
        in_specs=in_specs + [ANY] * len(others),
        out_specs=rows_spec(first // BLOCK),
        out_shape=jax.ShapeDtypeStruct((units, D), jnp.bfloat16),
        input_output_aliases={} if base is None else {len(ins): 0},
        scratch_shapes=scratch,
        compiler_params=PARAMS,
        cost_estimate=costs,
        name=name,
    )(*ins, *others)


def mean_rows(mine, theirs, rows, base, first, units, after=()):
    def body(mine_ref, theirs_ref, out_ref):
        out_ref[...] = halved_sum(mine_ref[...], theirs_ref[...])

    specs = [rows_spec()] * 2
    return into_rows(
        body, (mine, theirs), specs, base, first, rows, units, cost(0, rows, 3), "mean_rows", after
    )


def mean_of_steps(mine, left, right, theirs, their_left, their_blocks, scale, rows, units, after):
    part = their_blocks[0].shape[0]

    def body(mine_ref, left_ref, right_ref, theirs_ref, their_left_ref, *rest):
        out_ref, their_right = rest[-2:]

        @pl.when(pl.program_id(0) == 0)
        def _():
            for at in range(len(their_blocks)):
                their_right[pl.ds(at * part, part)] = rest[at][...]

        own = stepped(mine_ref[...], left_ref[...], right_ref[...], scale).astype(jnp.bfloat16)
        other = stepped(theirs_ref[...], their_left_ref[...], their_right[...], scale).astype(jnp.bfloat16)
        out_ref[...] = halved_sum(own, other)

    count = left.shape[1]
    return into_rows(
        body,
        (mine, left, right, theirs, their_left, *their_blocks),
        [rows_spec(), rows_spec(0, count), whole_spec(right)]
        + [rows_spec(), pl.BlockSpec((BLOCK, count), lambda i: (i, D // count))]
        + [whole_spec(block) for block in their_blocks],
        None,
        0,
        rows,
        units,
        cost(2, rows, 3),
        "mean_of_steps",
        after,
        [pltpu.VMEM((count, D), jnp.bfloat16)],
    )


def partial_sums(hidden, d_gate, d_up, gate_w, up_w, down_w, after):
    units, count = hidden.shape
    block = block_of(units, 432)
    steps = units // block

    def body(hidden_ref, d_gate_ref, d_up_ref, gate_ref, up_ref, down_ref, *rest):
        layer_ref, grad_ref = rest[-2:]

        @pl.when(pl.program_id(0) == 0)
        def _():
            layer_ref[...] = jnp.zeros_like(layer_ref)
            grad_ref[...] = jnp.zeros_like(grad_ref)

        layer_ref[...] += mm(hidden_ref[...], down_ref[...], ((0,), (0,))) * hidden_scale
        grad_sum = mm(d_gate_ref[...], gate_ref[...], ((0,), (0,))) + mm(d_up_ref[...], up_ref[...], ((0,), (0,)))
        grad_ref[...] += grad_sum * width_scale

    out = jax.ShapeDtypeStruct((count, D), jnp.float32)
    return pl.pallas_call(
        body,
        grid=(steps,),
        in_specs=[rows_spec(0, count, block)] * 3 + [rows_spec(block=block)] * 3 + [ANY] * len(after),
        out_specs=[whole_spec(out)] * 2,
        out_shape=[out] * 2,
        compiler_params=PARAMS,
        cost_estimate=cost(3, units, 3),
        name="partial_sums",
    )(hidden, d_gate, d_up, gate_w, up_w, down_w, *after)


def whole_step(distance, turned, tokens_local, grads_local, gate_w, up_w, down_w):
    units = gate_w.shape[0]
    devices = lax.axis_size("tp")
    ring = ring_of(devices)

    def send(x):
        replicas = lax.axis_size("rep")
        return lax.ppermute(x, "rep", [(i, (i + distance) % replicas) for i in range(replicas)])

    def along(x, by):
        return lax.ppermute(x, "tp", [(ring[i], ring[(i + by) % devices]) for i in range(devices)])

    blocks = units // BLOCK
    raw = (blocks if distance == 1 else blocks // 2) * BLOCK
    theirs_raw = send(up_w if raw == units else rows_of(up_w, 0, raw, BLOCK))

    half = devices // 2

    def gather(turn, locals_):
        held = [[x] * devices for x in locals_]
        for hop in range(1, half + 1):
            for at, blocks_held in enumerate(held):
                last_way = turn if at % 2 == 0 else -turn
                for way in (turn, -turn):
                    if hop < half or way == last_way:
                        blocks_held[-way * hop] = along(blocks_held[-way * (hop - 1)], way)
        return [blocks_held[1:] for blocks_held in held]

    def gathered(*locals_):
        if devices > 8:
            return [list(lax.all_gather(x, "tp")) for x in locals_]
        others = lax.cond(turned, partial(gather, 1), partial(gather, -1), locals_)
        return [[x, *rest] for x, rest in zip(locals_, others)]

    def gathered_beside(x, mine, theirs):
        if devices > 8:
            return list(lax.all_gather(x, "tp")), mean_rows(mine, theirs, units, None, 0, units)

        def branch(turn, x, mine, theirs):
            (others,) = gather(turn, (x,))
            return others, mean_rows(mine, theirs, units, None, 0, units)

        others, mean = lax.cond(turned, partial(branch, 1), partial(branch, -1), x, mine, theirs)
        return [x, *others], mean

    def summed(terms):
        if devices > 8:
            totals = [lax.psum_scatter(term, "tp", scatter_dimension=0, tiled=True) for term in terms]
            return [total.astype(jnp.bfloat16) for total in totals]
        return lax.cond(turned, partial(sums, 1), partial(sums, -1), terms)

    def sums(turn, terms):
        part = terms[0].shape[0] // devices
        block_at = lambda term, offset: term[(offset % devices) * part : (offset % devices + 1) * part]
        ways = [(at, way, half - (0 if (way == turn) == (at == 0) else 1)) for at in (0, 1) for way in (turn, -turn)]
        moving = {}
        for hop in range(1, half + 1):
            for at, way, hops in ways:
                if hop <= hops:
                    block = block_at(terms[at], way * (hops + 1 - hop))
                    if hop > 1:
                        block = block + moving[at, way].astype(jnp.float32)
                    moving[at, way] = along(block.astype(jnp.bfloat16), way)
        totals = []
        for at, term in enumerate(terms):
            total = block_at(term, 0)
            for way in (turn, -turn):
                total = total + moving[at, way].astype(jnp.float32)
            totals.append(total.astype(jnp.bfloat16))
        return totals

    token_blocks, grad_blocks = gathered(tokens_local, grads_local)
    tokens, grads, hidden, d_gate, d_up = forward(token_blocks, grad_blocks, gate_w, up_w, down_w)
    cut = units - BLOCK
    down_step = partial(step_rows, down_w, hidden, grads, hidden_scale, 0, units)
    head_step = partial(step_rows, gate_w, d_gate, tokens, width_scale, 0, cut)
    long_step = cost(20, units, 40)
    if raw < units:
        first = step_rows(
            up_w, d_up, tokens, width_scale, raw, units - raw, beside=d_up, below=tokens_local
        )
        their_first = send(first)
        second = down_new = down_step((theirs_raw,), costs=long_step)
        their_down = send(down_new)
    else:
        first = down_new = down_step(beside=d_up, below=tokens_local)
        their_first = their_down = send(down_new)
        second = gate_head = head_step((theirs_raw,), costs=long_step)
        their_gate_head = send(gate_head)
    terms = partial_sums(hidden, d_gate, d_up, gate_w, up_w, down_w, (second,))
    layer_out, grad_in = summed(terms)
    if raw < units:
        gate_head = head_step((their_first, layer_out))
        their_gate_head = send(gate_head)
    gate_tail = step_rows(gate_w, d_gate, tokens, width_scale, cut, BLOCK, (their_down, layer_out))
    their_gate_tail = send(gate_tail)

    their_tokens = rows_of(their_first, units - raw if raw < units else units, tokens_local.shape[0], 16)
    their_tokens, gate_tail = lax.optimization_barrier((their_tokens, gate_tail))
    their_blocks, new_down = gathered_beside(their_tokens, down_new, their_down)
    new_up = mean_of_steps(
        up_w, d_up, tokens, theirs_raw, their_first, their_blocks, width_scale, raw, units, (gate_tail,)
    )
    if raw < units:
        new_up = mean_rows(first, their_first, units - raw, new_up, raw, units)
    new_gate = mean_rows(gate_head, their_gate_head, cut, None, 0, units, (new_up, new_down))
    new_gate = mean_rows(gate_tail, their_gate_tail, BLOCK, new_gate, cut, units)
    return layer_out, grad_in, new_gate, new_up, new_down


def shards(activations, out_grad, gate_weight, up_weight, down_weight, step_index):
    levels = lax.axis_size("rep").bit_length() - 1
    branches = [partial(whole_step, 1 << level) for level in range(levels)]
    layer_out, grad_in, gate, up, down = lax.switch(
        step_index[0] % levels,
        branches,
        (step_index[0] // levels) % 2 == 0,
        activations[0],
        out_grad[0],
        gate_weight[0].T,
        up_weight[0].T,
        down_weight[0],
    )
    return layer_out[None], grad_in[None], gate.T[None], up.T[None], down[None]


def solution(mesh):
    in_specs = (
        P("rep", "tp", None),
        P("rep", "tp", None),
        P("rep", None, "tp"),
        P("rep", None, "tp"),
        P("rep", "tp", None),
        P(),
    )
    out_specs = (
        P("rep", "tp", None),
        P("rep", "tp", None),
        P("rep", None, "tp"),
        P("rep", None, "tp"),
        P("rep", "tp", None),
    )
    return jax.shard_map(shards, mesh=mesh, in_specs=in_specs, out_specs=out_specs, check_vma=False)
```

```python
from functools import partial
import math

import jax
import jax.numpy as jnp
from jax import lax
from jax.experimental import pallas as pl
from jax.experimental.pallas import tpu as pltpu
from jax.sharding import PartitionSpec as P

D = 2560
FF = 6912
BLOCK = 144


learn_rate = 0.8
width_scale = 1.0 / math.sqrt(D)
hidden_scale = 1.0 / math.sqrt(FF)

ANY = pl.BlockSpec(memory_space=pl.ANY)


def vmem(mebibytes):
    return pltpu.CompilerParams(vmem_limit_bytes=mebibytes * 1024 * 1024)


def ring_of(devices):
    y_size = 1 << ((devices.bit_length() - 1) // 2)
    z_size = devices // y_size
    walk = [(z, 0) for z in range(z_size)]
    for z in reversed(range(z_size)):
        ys = list(range(1, y_size))
        walk += [(z, y) for y in (ys if (z_size - 1 - z) % 2 == 0 else reversed(ys))]
    return [z * y_size + y for z, y in walk]


def mm(a, b, dims):
    return lax.dot_general(a, b, (dims, ((), ())), preferred_element_type=jnp.float32)


def cost(matmuls, rows, blocks_moved):
    return pl.CostEstimate(
        flops=2 * matmuls * rows * 256 * D, bytes_accessed=blocks_moved * rows * D * 2, transcendentals=0
    )


def rows_spec(first=0, width=D, block=BLOCK):
    return pl.BlockSpec((block, width), lambda i: (i + first, 0))


def block_of(units, most):
    return max(size for size in range(BLOCK, most + 1, BLOCK) if units % size == 0)


def whole_spec(x):
    return pl.BlockSpec(x.shape, lambda i: (0,) * x.ndim)


def forward(token_blocks, grad_blocks, gate_w, up_w, down_w):
    units, devices = gate_w.shape[0], len(token_blocks)
    part = token_blocks[0].shape[0]
    count = devices * part
    block = block_of(units, 288)

    def body(*refs):
        gate_ref, up_ref, down_ref = refs[2 * devices : 2 * devices + 3]
        tokens_ref, grads_ref, hidden_ref, d_gate_ref, d_up_ref, turned, turned_grads = refs[-7:]

        @pl.when(pl.program_id(0) == 0)
        def _():
            for at in range(devices):
                tokens_ref[pl.ds(at * part, part)] = refs[at][...]
                grads_ref[pl.ds(at * part, part)] = refs[devices + at][...]
            turned[...] = tokens_ref[...].T
            turned_grads[...] = grads_ref[...].T

        gate_pre = mm(gate_ref[...], turned[...], ((1,), (0,))) * width_scale
        up_pre = mm(up_ref[...], turned[...], ((1,), (0,))) * width_scale
        d_hidden = mm(down_ref[...], turned_grads[...], ((1,), (0,))) * hidden_scale
        sigmoid_gate = jax.nn.sigmoid(gate_pre)
        activated = gate_pre * sigmoid_gate
        slope = sigmoid_gate * (1.0 + gate_pre * (1.0 - sigmoid_gate))
        hidden_ref[...] = (activated * up_pre).astype(jnp.bfloat16)
        d_gate_ref[...] = (d_hidden * up_pre * slope).astype(jnp.bfloat16)
        d_up_ref[...] = (d_hidden * activated).astype(jnp.bfloat16)

    whole = jax.ShapeDtypeStruct((count, D), jnp.bfloat16)
    out = jax.ShapeDtypeStruct((units, count), jnp.bfloat16)
    pieces = [*token_blocks, *grad_blocks]
    return pl.pallas_call(
        body,
        grid=(units // block,),
        in_specs=[whole_spec(piece) for piece in pieces] + [rows_spec(block=block)] * 3,
        out_specs=[whole_spec(whole)] * 2 + [rows_spec(0, count, block)] * 3,
        out_shape=[whole] * 2 + [out] * 3,
        scratch_shapes=[pltpu.VMEM((D, count), jnp.bfloat16)] * 2,
        compiler_params=vmem(32),
        cost_estimate=cost(3, units, 3),
        name="forward",
    )(*pieces, gate_w, up_w, down_w)


def stepped(weight, left, right, scale):
    return weight.astype(jnp.float32) - learn_rate * (mm(left, right, ((1,), (0,))) * scale)


def step_rows(weight, left, right, scale, first, rows, after=(), beside=None, below=None, costs=None):
    at, steps = first // BLOCK, rows // BLOCK
    count = left.shape[1]
    here = lambda i: (jnp.minimum(i, steps - 1) + at, 0)
    ins = (weight, left, right)
    specs = [pl.BlockSpec((BLOCK, D), here), pl.BlockSpec((BLOCK, count), here), whole_spec(right)]
    out_rows, width = rows, D
    if beside is not None:
        ins = (*ins, beside, below)
        specs += [pl.BlockSpec((BLOCK, count), lambda i: (jnp.minimum(i, steps - 1), 0)), whole_spec(below)]
        out_rows, width = rows + below.shape[0], D + count

    def body(weight_ref, left_ref, right_ref, *rest):
        out_ref = rest[-1]

        @pl.when(pl.program_id(0) < steps)
        def _():
            out_ref[:, :D] = stepped(weight_ref[...], left_ref[...], right_ref[...], scale).astype(jnp.bfloat16)
            if beside is not None:
                out_ref[:, D:] = rest[0][...]

        if below is not None:

            @pl.when(pl.program_id(0) == steps)
            def _():
                out_ref[pl.ds(0, below.shape[0]), :D] = rest[1][...]

    return pl.pallas_call(
        body,
        grid=(steps if below is None else steps + 1,),
        in_specs=specs + [ANY] * len(after),
        out_specs=rows_spec(0, width),
        out_shape=jax.ShapeDtypeStruct((out_rows, width), jnp.bfloat16),
        compiler_params=vmem(16),
        cost_estimate=costs or cost(1, rows, 2),
        name="step_rows",
    )(*ins, *after)


def rows_of(x, first, rows, block):
    at = first // block

    def body(x_ref, out_ref):
        out_ref[...] = x_ref[...]

    return pl.pallas_call(
        body,
        grid=(rows // block,),
        in_specs=[rows_spec(at, block=block)],
        out_specs=rows_spec(block=block),
        out_shape=jax.ShapeDtypeStruct((rows, D), x.dtype),
        compiler_params=vmem(8),
        cost_estimate=cost(0, rows, 2),
        name="rows_of",
    )(x)


def first_rows(x, rows):
    def body(x_ref, out_ref, sems):
        copies = [
            pltpu.make_async_copy(x_ref.at[pl.ds(at, BLOCK)], out_ref.at[pl.ds(at, BLOCK)], sems.at[at // BLOCK])
            for at in range(0, rows, BLOCK)
        ]
        for copy in copies:
            copy.start()
        for copy in copies:
            copy.wait()

    return pl.pallas_call(
        body,
        in_specs=[ANY],
        out_specs=pl.BlockSpec(memory_space=pltpu.VMEM),
        out_shape=jax.ShapeDtypeStruct((rows, D), x.dtype),
        scratch_shapes=[pltpu.SemaphoreType.DMA((rows // BLOCK,))],
        compiler_params=vmem(8),
        cost_estimate=cost(0, rows, 2),
        name="first_rows",
    )(x)


def halved_sum(mine, theirs):
    return ((mine.astype(jnp.float32) + theirs.astype(jnp.float32)) * 0.5).astype(jnp.bfloat16)


def into_rows(body, ins, in_specs, base, first, rows, units, costs, name, after, scratch=()):
    others = after if base is None else (base, *after)

    def with_others(*refs):
        body(*refs[: len(ins)], *refs[len(ins) + len(others) :])
    return pl.pallas_call(
        with_others,
        grid=(rows // BLOCK,),
        in_specs=in_specs + [ANY] * len(others),
        out_specs=rows_spec(first // BLOCK),
        out_shape=jax.ShapeDtypeStruct((units, D), jnp.bfloat16),
        input_output_aliases={} if base is None else {len(ins): 0},
        scratch_shapes=scratch,
        compiler_params=vmem(16),
        cost_estimate=costs,
        name=name,
    )(*ins, *others)


def mean_rows(mine, theirs, rows, base, first, units, after=()):
    def body(mine_ref, theirs_ref, out_ref):
        out_ref[...] = halved_sum(mine_ref[...], theirs_ref[...])

    specs = [rows_spec()] * 2
    return into_rows(
        body, (mine, theirs), specs, base, first, rows, units, cost(0, rows, 3), "mean_rows", after
    )


def mean_of_steps(mine, left, right, theirs, their_left, their_blocks, scale, rows, units, after):
    part = their_blocks[0].shape[0]

    def body(mine_ref, left_ref, right_ref, theirs_ref, their_left_ref, *rest):
        out_ref, their_right = rest[-2:]

        @pl.when(pl.program_id(0) == 0)
        def _():
            for at in range(len(their_blocks)):
                their_right[pl.ds(at * part, part)] = rest[at][...]

        own = stepped(mine_ref[...], left_ref[...], right_ref[...], scale).astype(jnp.bfloat16)
        other = stepped(theirs_ref[...], their_left_ref[...], their_right[...], scale).astype(jnp.bfloat16)
        out_ref[...] = halved_sum(own, other)

    count = left.shape[1]
    return into_rows(
        body,
        (mine, left, right, theirs, their_left, *their_blocks),
        [rows_spec(), rows_spec(0, count), whole_spec(right)]
        + [rows_spec(), pl.BlockSpec((BLOCK, count), lambda i: (i, D // count))]
        + [whole_spec(block) for block in their_blocks],
        None,
        0,
        rows,
        units,
        cost(2, rows, 3),
        "mean_of_steps",
        after,
        [pltpu.VMEM((count, D), jnp.bfloat16)],
    )


def partial_sums(hidden, d_gate, d_up, gate_w, up_w, down_w, after):
    units, count = hidden.shape
    block = block_of(units, 432)
    steps = units // block

    def body(hidden_ref, d_gate_ref, d_up_ref, gate_ref, up_ref, down_ref, *rest):
        layer_ref, grad_ref = rest[-2:]

        @pl.when(pl.program_id(0) == 0)
        def _():
            layer_ref[...] = jnp.zeros_like(layer_ref)
            grad_ref[...] = jnp.zeros_like(grad_ref)

        layer_ref[...] += mm(hidden_ref[...], down_ref[...], ((0,), (0,))) * hidden_scale
        grad_sum = mm(d_gate_ref[...], gate_ref[...], ((0,), (0,))) + mm(d_up_ref[...], up_ref[...], ((0,), (0,)))
        grad_ref[...] += grad_sum * width_scale

    out = jax.ShapeDtypeStruct((count, D), jnp.float32)
    return pl.pallas_call(
        body,
        grid=(steps,),
        in_specs=[rows_spec(0, count, block)] * 3 + [rows_spec(block=block)] * 3 + [ANY] * len(after),
        out_specs=[whole_spec(out)] * 2,
        out_shape=[out] * 2,
        compiler_params=vmem(36),
        cost_estimate=cost(3, units, 3),
        name="partial_sums",
    )(hidden, d_gate, d_up, gate_w, up_w, down_w, *after)


def whole_step(distance, turned, tokens_local, grads_local, gate_w, up_w, down_w):
    units = gate_w.shape[0]
    devices = lax.axis_size("tp")
    ring = ring_of(devices)

    def send(x):
        replicas = lax.axis_size("rep")
        return lax.ppermute(x, "rep", [(i, (i + distance) % replicas) for i in range(replicas)])

    def along(x, by):
        return lax.ppermute(x, "tp", [(ring[i], ring[(i + by) % devices]) for i in range(devices)])

    blocks = units // BLOCK
    raw = (blocks if distance == 1 else blocks // 2) * BLOCK
    theirs_raw = send(up_w if raw == units else first_rows(up_w, raw))

    half = devices // 2

    def gather(turn, locals_):
        held = [[x] * devices for x in locals_]
        for hop in range(1, half + 1):
            for at, blocks_held in enumerate(held):
                last_way = turn if at % 2 == 0 else -turn
                for way in (turn, -turn):
                    if hop < half or way == last_way:
                        blocks_held[-way * hop] = along(blocks_held[-way * (hop - 1)], way)
        return [blocks_held[1:] for blocks_held in held]

    def gathered(*locals_):
        if devices > 8:
            return [list(lax.all_gather(x, "tp")) for x in locals_]
        others = lax.cond(turned, partial(gather, 1), partial(gather, -1), locals_)
        return [[x, *rest] for x, rest in zip(locals_, others)]

    def gathered_beside(x, mine, theirs):
        if devices > 8:
            return list(lax.all_gather(x, "tp")), mean_rows(mine, theirs, units, None, 0, units)

        def branch(turn, x, mine, theirs):
            (others,) = gather(turn, (x,))
            return others, mean_rows(mine, theirs, units, None, 0, units)

        others, mean = lax.cond(turned, partial(branch, 1), partial(branch, -1), x, mine, theirs)
        return [x, *others], mean

    def summed(terms):
        if devices > 8:
            totals = [lax.psum_scatter(term, "tp", scatter_dimension=0, tiled=True) for term in terms]
            return [total.astype(jnp.bfloat16) for total in totals]
        return lax.cond(turned, partial(sums, 1), partial(sums, -1), terms)

    def sums(turn, terms):
        part = terms[0].shape[0] // devices
        block_at = lambda term, offset: term[(offset % devices) * part : (offset % devices + 1) * part]
        ways = [(at, way, half - (0 if (way == turn) == (at == 0) else 1)) for at in (0, 1) for way in (turn, -turn)]
        moving = {}
        for hop in range(1, half + 1):
            for at, way, hops in ways:
                if hop <= hops:
                    block = block_at(terms[at], way * (hops + 1 - hop))
                    if hop > 1:
                        block = block + moving[at, way].astype(jnp.float32)
                    moving[at, way] = along(block.astype(jnp.bfloat16), way)
        totals = []
        for at, term in enumerate(terms):
            total = block_at(term, 0)
            for way in (turn, -turn):
                total = total + moving[at, way].astype(jnp.float32)
            totals.append(total.astype(jnp.bfloat16))
        return totals

    token_blocks, grad_blocks = gathered(tokens_local, grads_local)
    tokens, grads, hidden, d_gate, d_up = forward(token_blocks, grad_blocks, gate_w, up_w, down_w)
    cut = units - BLOCK
    down_step = partial(step_rows, down_w, hidden, grads, hidden_scale, 0, units)
    head_step = partial(step_rows, gate_w, d_gate, tokens, width_scale, 0, cut)
    long_step = cost(20, units, 40)
    if raw < units:
        first = step_rows(
            up_w, d_up, tokens, width_scale, raw, units - raw, beside=d_up, below=tokens_local
        )
        their_first = send(first)
        second = down_new = down_step((theirs_raw,), costs=long_step)
        their_down = send(down_new)
    else:
        first = down_new = down_step(beside=d_up, below=tokens_local)
        their_first = their_down = send(down_new)
        second = gate_head = head_step((theirs_raw,), costs=long_step)
        their_gate_head = send(gate_head)
    terms = partial_sums(hidden, d_gate, d_up, gate_w, up_w, down_w, (second,))
    layer_out, grad_in = summed(terms)
    if raw < units:
        gate_head = head_step((their_first, layer_out))
        their_gate_head = send(gate_head)
    gate_tail = step_rows(gate_w, d_gate, tokens, width_scale, cut, BLOCK, (their_down, layer_out))
    their_gate_tail = send(gate_tail)

    their_tokens = rows_of(their_first, units - raw if raw < units else units, tokens_local.shape[0], 16)
    their_tokens, gate_tail = lax.optimization_barrier((their_tokens, gate_tail))
    their_blocks, new_down = gathered_beside(their_tokens, down_new, their_down)
    new_up = mean_of_steps(
        up_w, d_up, tokens, theirs_raw, their_first, their_blocks, width_scale, raw, units, (gate_tail,)
    )
    if raw < units:
        new_up = mean_rows(first, their_first, units - raw, new_up, raw, units)
    new_gate = mean_rows(gate_head, their_gate_head, cut, None, 0, units, (new_up, new_down))
    new_gate = mean_rows(gate_tail, their_gate_tail, BLOCK, new_gate, cut, units)
    return layer_out, grad_in, new_gate, new_up, new_down


def shards(activations, out_grad, gate_weight, up_weight, down_weight, step_index):
    levels = lax.axis_size("rep").bit_length() - 1
    branches = [partial(whole_step, 1 << level) for level in range(levels)]
    layer_out, grad_in, gate, up, down = lax.switch(
        step_index[0] % levels,
        branches,
        (step_index[0] // levels) % 2 == 0,
        activations[0],
        out_grad[0],
        gate_weight[0].T,
        up_weight[0].T,
        down_weight[0],
    )
    return layer_out[None], grad_in[None], gate.T[None], up.T[None], down[None]


def solution(mesh):
    in_specs = (
        P("rep", "tp", None),
        P("rep", "tp", None),
        P("rep", None, "tp"),
        P("rep", None, "tp"),
        P("rep", "tp", None),
        P(),
    )
    out_specs = (
        P("rep", "tp", None),
        P("rep", "tp", None),
        P("rep", None, "tp"),
        P("rep", None, "tp"),
        P("rep", "tp", None),
    )
    return jax.shard_map(shards, mesh=mesh, in_specs=in_specs, out_specs=out_specs, check_vma=False)
```

```python
from functools import partial
import math

import jax
import jax.numpy as jnp
from jax import lax
from jax.experimental import pallas as pl
from jax.experimental.pallas import tpu as pltpu
from jax.sharding import PartitionSpec as P

D = 2560
FF = 6912
BLOCK = 144


learn_rate = 0.8
width_scale = 1.0 / math.sqrt(D)
hidden_scale = 1.0 / math.sqrt(FF)

ANY = pl.BlockSpec(memory_space=pl.ANY)


def vmem(mebibytes):
    return pltpu.CompilerParams(vmem_limit_bytes=mebibytes * 1024 * 1024)


def ring_of(devices):
    y_size = 1 << ((devices.bit_length() - 1) // 2)
    z_size = devices // y_size
    walk = [(z, 0) for z in range(z_size)]
    for z in reversed(range(z_size)):
        ys = list(range(1, y_size))
        walk += [(z, y) for y in (ys if (z_size - 1 - z) % 2 == 0 else reversed(ys))]
    return [z * y_size + y for z, y in walk]


def mm(a, b, dims):
    return lax.dot_general(a, b, (dims, ((), ())), preferred_element_type=jnp.float32)


def cost(matmuls, rows, blocks_moved):
    return pl.CostEstimate(
        flops=2 * matmuls * rows * 256 * D, bytes_accessed=blocks_moved * rows * D * 2, transcendentals=0
    )


def rows_spec(first=0, width=D, block=BLOCK):
    return pl.BlockSpec((block, width), lambda i: (i + first, 0))


def block_of(units, most):
    return max(size for size in range(BLOCK, most + 1, BLOCK) if units % size == 0)


def whole_spec(x):
    return pl.BlockSpec(x.shape, lambda i: (0,) * x.ndim)


def forward(token_blocks, grad_blocks, gate_w, up_w, down_w):
    units, devices = gate_w.shape[0], len(token_blocks)
    part = token_blocks[0].shape[0]
    count = devices * part
    block = block_of(units, 288)

    def body(*refs):
        gate_ref, up_ref, down_ref = refs[2 * devices : 2 * devices + 3]
        tokens_ref, grads_ref, hidden_ref, d_gate_ref, d_up_ref, turned, turned_grads = refs[-7:]

        @pl.when(pl.program_id(0) == 0)
        def _():
            for at in range(devices):
                tokens_ref[pl.ds(at * part, part)] = refs[at][...]
                grads_ref[pl.ds(at * part, part)] = refs[devices + at][...]
            turned[...] = tokens_ref[...].T
            turned_grads[...] = grads_ref[...].T

        gate_pre = mm(gate_ref[...], turned[...], ((1,), (0,))) * width_scale
        up_pre = mm(up_ref[...], turned[...], ((1,), (0,))) * width_scale
        d_hidden = mm(down_ref[...], turned_grads[...], ((1,), (0,))) * hidden_scale
        sigmoid_gate = jax.nn.sigmoid(gate_pre)
        activated = gate_pre * sigmoid_gate
        slope = sigmoid_gate * (1.0 + gate_pre * (1.0 - sigmoid_gate))
        hidden_ref[...] = (activated * up_pre).astype(jnp.bfloat16)
        d_gate_ref[...] = (d_hidden * up_pre * slope).astype(jnp.bfloat16)
        d_up_ref[...] = (d_hidden * activated).astype(jnp.bfloat16)

    whole = jax.ShapeDtypeStruct((count, D), jnp.bfloat16)
    out = jax.ShapeDtypeStruct((units, count), jnp.bfloat16)
    pieces = [*token_blocks, *grad_blocks]
    return pl.pallas_call(
        body,
        grid=(units // block,),
        in_specs=[whole_spec(piece) for piece in pieces] + [rows_spec(block=block)] * 3,
        out_specs=[whole_spec(whole)] * 2 + [rows_spec(0, count, block)] * 3,
        out_shape=[whole] * 2 + [out] * 3,
        scratch_shapes=[pltpu.VMEM((D, count), jnp.bfloat16)] * 2,
        compiler_params=vmem(32),
        cost_estimate=cost(3, units, 3),
        name="forward",
    )(*pieces, gate_w, up_w, down_w)


def stepped(weight, left, right, scale):
    return weight.astype(jnp.float32) - learn_rate * (mm(left, right, ((1,), (0,))) * scale)


def step_rows(weight, left, right, scale, first, rows, after=(), beside=None, below=None, costs=None):
    at, steps = first // BLOCK, rows // BLOCK
    count = left.shape[1]
    here = lambda i: (jnp.minimum(i, steps - 1) + at, 0)
    ins = (weight, left, right)
    specs = [pl.BlockSpec((BLOCK, D), here), pl.BlockSpec((BLOCK, count), here), whole_spec(right)]
    out_rows, width = rows, D
    if beside is not None:
        ins = (*ins, beside, below)
        specs += [pl.BlockSpec((BLOCK, count), lambda i: (jnp.minimum(i, steps - 1), 0)), whole_spec(below)]
        out_rows, width = rows + below.shape[0], D + count

    def body(weight_ref, left_ref, right_ref, *rest):
        out_ref = rest[-1]

        @pl.when(pl.program_id(0) < steps)
        def _():
            out_ref[:, :D] = stepped(weight_ref[...], left_ref[...], right_ref[...], scale).astype(jnp.bfloat16)
            if beside is not None:
                out_ref[:, D:] = rest[0][...]

        if below is not None:

            @pl.when(pl.program_id(0) == steps)
            def _():
                out_ref[pl.ds(0, below.shape[0]), :D] = rest[1][...]

    return pl.pallas_call(
        body,
        grid=(steps if below is None else steps + 1,),
        in_specs=specs + [ANY] * len(after),
        out_specs=rows_spec(0, width),
        out_shape=jax.ShapeDtypeStruct((out_rows, width), jnp.bfloat16),
        compiler_params=vmem(16),
        cost_estimate=costs or cost(1, rows, 2),
        name="step_rows",
    )(*ins, *after)


def rows_of(x, first, rows, block):
    at = first // block

    def body(x_ref, out_ref):
        out_ref[...] = x_ref[...]

    return pl.pallas_call(
        body,
        grid=(rows // block,),
        in_specs=[rows_spec(at, block=block)],
        out_specs=rows_spec(block=block),
        out_shape=jax.ShapeDtypeStruct((rows, D), x.dtype),
        compiler_params=vmem(8),
        cost_estimate=cost(0, rows, 2),
        name="rows_of",
    )(x)


def halved_sum(mine, theirs):
    return ((mine.astype(jnp.float32) + theirs.astype(jnp.float32)) * 0.5).astype(jnp.bfloat16)


def into_rows(body, ins, in_specs, base, first, rows, units, costs, name, after, scratch=()):
    others = after if base is None else (base, *after)

    def with_others(*refs):
        body(*refs[: len(ins)], *refs[len(ins) + len(others) :])
    return pl.pallas_call(
        with_others,
        grid=(rows // BLOCK,),
        in_specs=in_specs + [ANY] * len(others),
        out_specs=rows_spec(first // BLOCK),
        out_shape=jax.ShapeDtypeStruct((units, D), jnp.bfloat16),
        input_output_aliases={} if base is None else {len(ins): 0},
        scratch_shapes=scratch,
        compiler_params=vmem(16),
        cost_estimate=costs,
        name=name,
    )(*ins, *others)


def mean_rows(mine, theirs, rows, base, first, units, after=()):
    def body(mine_ref, theirs_ref, out_ref):
        out_ref[...] = halved_sum(mine_ref[...], theirs_ref[...])

    specs = [rows_spec()] * 2
    return into_rows(
        body, (mine, theirs), specs, base, first, rows, units, cost(0, rows, 3), "mean_rows", after
    )


def mean_of_steps(mine, left, right, theirs, their_left, their_blocks, scale, rows, units, after):
    part = their_blocks[0].shape[0]

    def body(mine_ref, left_ref, right_ref, theirs_ref, their_left_ref, *rest):
        out_ref, their_right = rest[-2:]

        @pl.when(pl.program_id(0) == 0)
        def _():
            for at in range(len(their_blocks)):
                their_right[pl.ds(at * part, part)] = rest[at][...]

        own = stepped(mine_ref[...], left_ref[...], right_ref[...], scale).astype(jnp.bfloat16)
        other = stepped(theirs_ref[...], their_left_ref[...], their_right[...], scale).astype(jnp.bfloat16)
        out_ref[...] = halved_sum(own, other)

    count = left.shape[1]
    return into_rows(
        body,
        (mine, left, right, theirs, their_left, *their_blocks),
        [rows_spec(), rows_spec(0, count), whole_spec(right)]
        + [rows_spec(), pl.BlockSpec((BLOCK, count), lambda i: (i, D // count))]
        + [whole_spec(block) for block in their_blocks],
        None,
        0,
        rows,
        units,
        cost(2, rows, 3),
        "mean_of_steps",
        after,
        [pltpu.VMEM((count, D), jnp.bfloat16)],
    )


def partial_sums(hidden, d_gate, d_up, gate_w, up_w, down_w, after):
    units, count = hidden.shape
    block = block_of(units, 432)
    steps = units // block

    def body(hidden_ref, d_gate_ref, d_up_ref, gate_ref, up_ref, down_ref, *rest):
        layer_ref, grad_ref = rest[-2:]

        @pl.when(pl.program_id(0) == 0)
        def _():
            layer_ref[...] = jnp.zeros_like(layer_ref)
            grad_ref[...] = jnp.zeros_like(grad_ref)

        layer_ref[...] += mm(hidden_ref[...], down_ref[...], ((0,), (0,))) * hidden_scale
        grad_sum = mm(d_gate_ref[...], gate_ref[...], ((0,), (0,))) + mm(d_up_ref[...], up_ref[...], ((0,), (0,)))
        grad_ref[...] += grad_sum * width_scale

    out = jax.ShapeDtypeStruct((count, D), jnp.float32)
    return pl.pallas_call(
        body,
        grid=(steps,),
        in_specs=[rows_spec(0, count, block)] * 3 + [rows_spec(block=block)] * 3 + [ANY] * len(after),
        out_specs=[whole_spec(out)] * 2,
        out_shape=[out] * 2,
        compiler_params=vmem(36),
        cost_estimate=cost(3, units, 3),
        name="partial_sums",
    )(hidden, d_gate, d_up, gate_w, up_w, down_w, *after)


def whole_step(distance, turned, tokens_local, grads_local, gate_w, up_w, down_w):
    units = gate_w.shape[0]
    devices = lax.axis_size("tp")
    ring = ring_of(devices)

    def send(x, parity=None):
        replicas = lax.axis_size("rep")
        senders = [i for i in range(replicas) if parity is None or i % 2 == parity]
        return lax.ppermute(x, "rep", [(i, (i + distance) % replicas) for i in senders])

    def along(x, by):
        return lax.ppermute(x, "tp", [(ring[i], ring[(i + by) % devices]) for i in range(devices)])

    shared = distance % 2 == 0
    early = 0 if shared else None
    is_early = lax.axis_index("rep") % 2 == 0
    theirs_raw = send(up_w, early)

    half = devices // 2

    def gather(turn, locals_):
        held = [[x] * devices for x in locals_]
        for hop in range(1, half + 1):
            for at, blocks_held in enumerate(held):
                last_way = turn if at % 2 == 0 else -turn
                for way in (turn, -turn):
                    if hop < half or way == last_way:
                        blocks_held[-way * hop] = along(blocks_held[-way * (hop - 1)], way)
        return [blocks_held[1:] for blocks_held in held]

    def gathered(*locals_):
        if devices > 8:
            return [list(lax.all_gather(x, "tp")) for x in locals_]
        others = lax.cond(turned, partial(gather, 1), partial(gather, -1), locals_)
        return [[x, *rest] for x, rest in zip(locals_, others)]

    def gathered_beside(x, mine, theirs):
        if devices > 8:
            return list(lax.all_gather(x, "tp")), mean_rows(mine, theirs, units, None, 0, units)

        def branch(turn, x, mine, theirs):
            (others,) = gather(turn, (x,))
            return others, mean_rows(mine, theirs, units, None, 0, units)

        others, mean = lax.cond(turned, partial(branch, 1), partial(branch, -1), x, mine, theirs)
        return [x, *others], mean

    def summed(terms):
        if devices > 8:
            totals = [lax.psum_scatter(term, "tp", scatter_dimension=0, tiled=True) for term in terms]
            return [total.astype(jnp.bfloat16) for total in totals]
        return lax.cond(turned, partial(sums, 1), partial(sums, -1), terms)

    def sums(turn, terms):
        part = terms[0].shape[0] // devices
        block_at = lambda term, offset: term[(offset % devices) * part : (offset % devices + 1) * part]
        ways = [(at, way, half - (0 if (way == turn) == (at == 0) else 1)) for at in (0, 1) for way in (turn, -turn)]
        moving = {}
        for hop in range(1, half + 1):
            for at, way, hops in ways:
                if hop <= hops:
                    block = block_at(terms[at], way * (hops + 1 - hop))
                    if hop > 1:
                        block = block + moving[at, way].astype(jnp.float32)
                    moving[at, way] = along(block.astype(jnp.bfloat16), way)
        totals = []
        for at, term in enumerate(terms):
            total = block_at(term, 0)
            for way in (turn, -turn):
                total = total + moving[at, way].astype(jnp.float32)
            totals.append(total.astype(jnp.bfloat16))
        return totals

    token_blocks, grad_blocks = gathered(tokens_local, grads_local)
    tokens, grads, hidden, d_gate, d_up = forward(token_blocks, grad_blocks, gate_w, up_w, down_w)
    cut = units - BLOCK
    down_step = partial(step_rows, down_w, hidden, grads, hidden_scale, 0, units)
    head_step = partial(step_rows, gate_w, d_gate, tokens, width_scale, 0, cut)
    long_step = cost(20, units, 40)
    first = down_step(beside=d_up, below=tokens_local)
    their_first = send(first, early)
    if shared:
        second = up_new = step_rows(up_w, d_up, tokens, width_scale, 0, units, (theirs_raw,), costs=long_step)
        their_up = send(up_new, 1)
    else:
        second = gate_head = head_step((theirs_raw,), costs=long_step)
        their_gate_head = send(gate_head)
    terms = partial_sums(hidden, d_gate, d_up, gate_w, up_w, down_w, (second,))
    layer_out, grad_in = summed(terms)
    if shared:
        down_new = down_step((layer_out,))
        their_down = send(down_new, 1)
        gate_head = head_step((their_first, down_new))
        their_gate_head = send(gate_head)
    landed = their_up if shared else their_first
    gate_tail = step_rows(gate_w, d_gate, tokens, width_scale, cut, BLOCK, (landed, gate_head, layer_out))
    their_gate_tail = send(gate_tail)

    their_tokens = rows_of(their_first, units, tokens_local.shape[0], 16)
    their_tokens, gate_tail = lax.optimization_barrier((their_tokens, gate_tail))

    def up_from_raw(their_blocks):
        return mean_of_steps(
            up_w, d_up, tokens, theirs_raw, their_first, their_blocks, width_scale, units, units, (gate_tail,)
        )

    if shared:
        (their_blocks,) = gathered(their_tokens)
        new_up = lax.cond(
            is_early,
            up_from_raw,
            lambda _: mean_rows(up_new, their_up, units, None, 0, units),
            their_blocks,
        )
        new_down = lax.cond(
            is_early,
            lambda after: mean_rows(first, their_first, units, None, 0, units, (after,)),
            lambda after: mean_rows(down_new, their_down, units, None, 0, units, (after,)),
            new_up,
        )
    else:
        their_blocks, new_down = gathered_beside(their_tokens, first, their_first)
        new_up = up_from_raw(their_blocks)
    new_gate = mean_rows(gate_head, their_gate_head, cut, None, 0, units, (new_up, new_down))
    new_gate = mean_rows(gate_tail, their_gate_tail, BLOCK, new_gate, cut, units)
    return layer_out, grad_in, new_gate, new_up, new_down


def shards(activations, out_grad, gate_weight, up_weight, down_weight, step_index):
    levels = lax.axis_size("rep").bit_length() - 1
    branches = [partial(whole_step, 1 << level) for level in range(levels)]
    layer_out, grad_in, gate, up, down = lax.switch(
        step_index[0] % levels,
        branches,
        (step_index[0] // levels) % 2 == 0,
        activations[0],
        out_grad[0],
        gate_weight[0].T,
        up_weight[0].T,
        down_weight[0],
    )
    return layer_out[None], grad_in[None], gate.T[None], up.T[None], down[None]


def solution(mesh):
    in_specs = (
        P("rep", "tp", None),
        P("rep", "tp", None),
        P("rep", None, "tp"),
        P("rep", None, "tp"),
        P("rep", "tp", None),
        P(),
    )
    out_specs = (
        P("rep", "tp", None),
        P("rep", "tp", None),
        P("rep", None, "tp"),
        P("rep", None, "tp"),
        P("rep", "tp", None),
    )
    return jax.shard_map(shards, mesh=mesh, in_specs=in_specs, out_specs=out_specs, check_vma=False)
```

```python
from functools import partial
import math

import jax
import jax.numpy as jnp
from jax import lax
from jax.experimental import pallas as pl
from jax.experimental.pallas import tpu as pltpu
from jax.sharding import PartitionSpec as P

D = 2560
FF = 6912
BLOCK = 144


learn_rate = 0.8
width_scale = 1.0 / math.sqrt(D)
hidden_scale = 1.0 / math.sqrt(FF)

ANY = pl.BlockSpec(memory_space=pl.ANY)
PARAMS = pltpu.CompilerParams(vmem_limit_bytes=40 * 1024 * 1024)


def ring_of(devices):
    y_size = 1 << ((devices.bit_length() - 1) // 2)
    z_size = devices // y_size
    walk = [(z, 0) for z in range(z_size)]
    for z in reversed(range(z_size)):
        ys = list(range(1, y_size))
        walk += [(z, y) for y in (ys if (z_size - 1 - z) % 2 == 0 else reversed(ys))]
    return [z * y_size + y for z, y in walk]


def mm(a, b, dims):
    return lax.dot_general(a, b, (dims, ((), ())), preferred_element_type=jnp.float32)


def cost(matmuls, rows, blocks_moved):
    return pl.CostEstimate(
        flops=2 * matmuls * rows * 256 * D, bytes_accessed=blocks_moved * rows * D * 2, transcendentals=0
    )


def rows_spec(first=0, width=D, block=BLOCK):
    return pl.BlockSpec((block, width), lambda i: (i + first, 0))


def block_of(units, most):
    return max(size for size in range(BLOCK, most + 1, BLOCK) if units % size == 0)


def whole_spec(x):
    return pl.BlockSpec(x.shape, lambda i: (0,) * x.ndim)


def forward(token_blocks, grad_blocks, gate_w, up_w, down_w):
    units, devices = gate_w.shape[0], len(token_blocks)
    part = token_blocks[0].shape[0]
    count = devices * part
    block = block_of(units, 288)

    def body(*refs):
        gate_ref, up_ref, down_ref = refs[2 * devices : 2 * devices + 3]
        tokens_ref, grads_ref, hidden_ref, d_gate_ref, d_up_ref, turned, turned_grads = refs[-7:]

        @pl.when(pl.program_id(0) == 0)
        def _():
            for at in range(devices):
                tokens_ref[pl.ds(at * part, part)] = refs[at][...]
                grads_ref[pl.ds(at * part, part)] = refs[devices + at][...]
            turned[...] = tokens_ref[...].T
            turned_grads[...] = grads_ref[...].T

        gate_pre = mm(gate_ref[...], turned[...], ((1,), (0,))) * width_scale
        up_pre = mm(up_ref[...], turned[...], ((1,), (0,))) * width_scale
        d_hidden = mm(down_ref[...], turned_grads[...], ((1,), (0,))) * hidden_scale
        sigmoid_gate = jax.nn.sigmoid(gate_pre)
        activated = gate_pre * sigmoid_gate
        slope = sigmoid_gate * (1.0 + gate_pre * (1.0 - sigmoid_gate))
        hidden_ref[...] = (activated * up_pre).astype(jnp.bfloat16)
        d_gate_ref[...] = (d_hidden * up_pre * slope).astype(jnp.bfloat16)
        d_up_ref[...] = (d_hidden * activated).astype(jnp.bfloat16)

    whole = jax.ShapeDtypeStruct((count, D), jnp.bfloat16)
    out = jax.ShapeDtypeStruct((units, count), jnp.bfloat16)
    pieces = [*token_blocks, *grad_blocks]
    return pl.pallas_call(
        body,
        grid=(units // block,),
        in_specs=[whole_spec(piece) for piece in pieces] + [rows_spec(block=block)] * 3,
        out_specs=[whole_spec(whole)] * 2 + [rows_spec(0, count, block)] * 3,
        out_shape=[whole] * 2 + [out] * 3,
        scratch_shapes=[pltpu.VMEM((D, count), jnp.bfloat16)] * 2,
        compiler_params=PARAMS,
        cost_estimate=cost(3, units, 3),
        name="forward",
    )(*pieces, gate_w, up_w, down_w)


def stepped(weight, left, right, scale):
    return weight.astype(jnp.float32) - learn_rate * (mm(left, right, ((1,), (0,))) * scale)


def step_rows(weight, left, right, scale, first, rows, after=(), beside=None, below=None, costs=None):
    at, steps = first // BLOCK, rows // BLOCK
    count = left.shape[1]
    here = lambda i: (jnp.minimum(i, steps - 1) + at, 0)
    ins = (weight, left, right)
    specs = [pl.BlockSpec((BLOCK, D), here), pl.BlockSpec((BLOCK, count), here), whole_spec(right)]
    out_rows, width = rows, D
    if beside is not None:
        ins = (*ins, beside, below)
        specs += [pl.BlockSpec((BLOCK, count), lambda i: (jnp.minimum(i, steps - 1), 0)), whole_spec(below)]
        out_rows, width = rows + below.shape[0], D + count

    def body(weight_ref, left_ref, right_ref, *rest):
        out_ref = rest[-1]

        @pl.when(pl.program_id(0) < steps)
        def _():
            out_ref[:, :D] = stepped(weight_ref[...], left_ref[...], right_ref[...], scale).astype(jnp.bfloat16)
            if beside is not None:
                out_ref[:, D:] = rest[0][...]

        if below is not None:

            @pl.when(pl.program_id(0) == steps)
            def _():
                out_ref[pl.ds(0, below.shape[0]), :D] = rest[1][...]

    return pl.pallas_call(
        body,
        grid=(steps if below is None else steps + 1,),
        in_specs=specs + [ANY] * len(after),
        out_specs=rows_spec(0, width),
        out_shape=jax.ShapeDtypeStruct((out_rows, width), jnp.bfloat16),
        compiler_params=PARAMS,
        cost_estimate=costs or cost(1, rows, 2),
        name="step_rows",
    )(*ins, *after)


def rows_of(x, first, rows, block):
    at = first // block

    def body(x_ref, out_ref):
        out_ref[...] = x_ref[...]

    return pl.pallas_call(
        body,
        grid=(rows // block,),
        in_specs=[rows_spec(at, block=block)],
        out_specs=rows_spec(block=block),
        out_shape=jax.ShapeDtypeStruct((rows, D), x.dtype),
        compiler_params=PARAMS,
        cost_estimate=cost(0, rows, 2),
        name="rows_of",
    )(x)


def halved_sum(mine, theirs):
    return ((mine.astype(jnp.float32) + theirs.astype(jnp.float32)) * 0.5).astype(jnp.bfloat16)


def into_rows(body, ins, in_specs, base, first, rows, units, costs, name, after, scratch=()):
    others = after if base is None else (base, *after)

    def with_others(*refs):
        body(*refs[: len(ins)], *refs[len(ins) + len(others) :])
    return pl.pallas_call(
        with_others,
        grid=(rows // BLOCK,),
        in_specs=in_specs + [ANY] * len(others),
        out_specs=rows_spec(first // BLOCK),
        out_shape=jax.ShapeDtypeStruct((units, D), jnp.bfloat16),
        input_output_aliases={} if base is None else {len(ins): 0},
        scratch_shapes=scratch,
        compiler_params=PARAMS,
        cost_estimate=costs,
        name=name,
    )(*ins, *others)


def mean_rows(mine, theirs, rows, base, first, units, after=(), source=0):
    def body(mine_ref, theirs_ref, out_ref):
        out_ref[...] = halved_sum(mine_ref[...], theirs_ref[...])

    specs = [rows_spec(source // BLOCK)] * 2
    return into_rows(
        body, (mine, theirs), specs, base, first, rows, units, cost(0, rows, 3), "mean_rows", after
    )


def mean_of_steps(mine, left, right, theirs, their_left, their_blocks, scale, rows, units, after):
    part = their_blocks[0].shape[0]

    def body(mine_ref, left_ref, right_ref, theirs_ref, their_left_ref, *rest):
        out_ref, their_right = rest[-2:]

        @pl.when(pl.program_id(0) == 0)
        def _():
            for at in range(len(their_blocks)):
                their_right[pl.ds(at * part, part)] = rest[at][...]

        own = stepped(mine_ref[...], left_ref[...], right_ref[...], scale).astype(jnp.bfloat16)
        other = stepped(theirs_ref[...], their_left_ref[...], their_right[...], scale).astype(jnp.bfloat16)
        out_ref[...] = halved_sum(own, other)

    count = left.shape[1]
    return into_rows(
        body,
        (mine, left, right, theirs, their_left, *their_blocks),
        [rows_spec(), rows_spec(0, count), whole_spec(right)]
        + [rows_spec(), pl.BlockSpec((BLOCK, count), lambda i: (i, D // count))]
        + [whole_spec(block) for block in their_blocks],
        None,
        0,
        rows,
        units,
        cost(2, rows, 3),
        "mean_of_steps",
        after,
        [pltpu.VMEM((count, D), jnp.bfloat16)],
    )


def partial_sums(hidden, d_gate, d_up, gate_w, up_w, down_w, after):
    units, count = hidden.shape
    block = block_of(units, 432)
    steps = units // block

    def body(hidden_ref, d_gate_ref, d_up_ref, gate_ref, up_ref, down_ref, *rest):
        layer_ref, grad_ref = rest[-2:]

        @pl.when(pl.program_id(0) == 0)
        def _():
            layer_ref[...] = jnp.zeros_like(layer_ref)
            grad_ref[...] = jnp.zeros_like(grad_ref)

        layer_ref[...] += mm(hidden_ref[...], down_ref[...], ((0,), (0,))) * hidden_scale
        grad_sum = mm(d_gate_ref[...], gate_ref[...], ((0,), (0,))) + mm(d_up_ref[...], up_ref[...], ((0,), (0,)))
        grad_ref[...] += grad_sum * width_scale

    out = jax.ShapeDtypeStruct((count, D), jnp.float32)
    return pl.pallas_call(
        body,
        grid=(steps,),
        in_specs=[rows_spec(0, count, block)] * 3 + [rows_spec(block=block)] * 3 + [ANY] * len(after),
        out_specs=[whole_spec(out)] * 2,
        out_shape=[out] * 2,
        compiler_params=PARAMS,
        cost_estimate=cost(3, units, 3),
        name="partial_sums",
    )(hidden, d_gate, d_up, gate_w, up_w, down_w, *after)


def whole_step(distance, turned, tokens_local, grads_local, gate_w, up_w, down_w):
    units = gate_w.shape[0]
    devices = lax.axis_size("tp")
    ring = ring_of(devices)

    def send(x, parity=None):
        replicas = lax.axis_size("rep")
        senders = [i for i in range(replicas) if parity is None or i % 2 == parity]
        return lax.ppermute(x, "rep", [(i, (i + distance) % replicas) for i in senders])

    def along(x, by):
        return lax.ppermute(x, "tp", [(ring[i], ring[(i + by) % devices]) for i in range(devices)])

    shared = distance % 2 == 0
    early = 0 if shared else None
    is_early = lax.axis_index("rep") % 2 == 0
    theirs_raw = send(up_w, early)

    half = devices // 2

    def gather(turn, locals_):
        held = [[x] * devices for x in locals_]
        for hop in range(1, half + 1):
            for at, blocks_held in enumerate(held):
                last_way = turn if at % 2 == 0 else -turn
                for way in (turn, -turn):
                    if hop < half or way == last_way:
                        blocks_held[-way * hop] = along(blocks_held[-way * (hop - 1)], way)
        return [blocks_held[1:] for blocks_held in held]

    def gathered(*locals_):
        if devices > 8:
            return [list(lax.all_gather(x, "tp")) for x in locals_]
        others = lax.cond(turned, partial(gather, 1), partial(gather, -1), locals_)
        return [[x, *rest] for x, rest in zip(locals_, others)]

    def gathered_beside(x, mine, theirs):
        if devices > 8:
            return list(lax.all_gather(x, "tp")), mean_rows(mine, theirs, units, None, 0, units)

        def branch(turn, x, mine, theirs):
            held, mean, done = [x] * devices, None, 0
            for hop in range(1, half + 1):
                for way in (turn, -turn):
                    if hop < half or way == turn:
                        held[-way * hop] = along(held[-way * (hop - 1)], way)
                if hop < half:
                    upto = units // BLOCK * hop // (half - 1) * BLOCK
                    mean = mean_rows(mine, theirs, upto - done, mean, done, units, (), done)
                    held[-turn * hop], mean = lax.optimization_barrier((held[-turn * hop], mean))
                    done = upto
            return held[1:], mean

        others, mean = lax.cond(turned, partial(branch, 1), partial(branch, -1), x, mine, theirs)
        return [x, *others], mean

    def summed(terms):
        if devices > 8:
            totals = [lax.psum_scatter(term, "tp", scatter_dimension=0, tiled=True) for term in terms]
            return [total.astype(jnp.bfloat16) for total in totals]
        return lax.cond(turned, partial(sums, 1), partial(sums, -1), terms)

    def sums(turn, terms):
        part = terms[0].shape[0] // devices
        block_at = lambda term, offset: term[(offset % devices) * part : (offset % devices + 1) * part]
        ways = [(at, way, half - (0 if (way == turn) == (at == 0) else 1)) for at in (0, 1) for way in (turn, -turn)]
        moving = {}
        for hop in range(1, half + 1):
            for at, way, hops in ways:
                if hop <= hops:
                    block = block_at(terms[at], way * (hops + 1 - hop))
                    if hop > 1:
                        block = block + moving[at, way].astype(jnp.float32)
                    moving[at, way] = along(block.astype(jnp.bfloat16), way)
        totals = []
        for at, term in enumerate(terms):
            total = block_at(term, 0)
            for way in (turn, -turn):
                total = total + moving[at, way].astype(jnp.float32)
            totals.append(total.astype(jnp.bfloat16))
        return totals

    token_blocks, grad_blocks = gathered(tokens_local, grads_local)
    tokens, grads, hidden, d_gate, d_up = forward(token_blocks, grad_blocks, gate_w, up_w, down_w)
    cut = units - BLOCK
    down_step = partial(step_rows, down_w, hidden, grads, hidden_scale, 0, units)
    head_step = partial(step_rows, gate_w, d_gate, tokens, width_scale, 0, cut)
    long_step = cost(20, units, 40)
    first = down_step(beside=d_up, below=tokens_local)
    their_first = send(first, early)
    if shared:
        second = up_new = step_rows(up_w, d_up, tokens, width_scale, 0, units, (theirs_raw,), costs=long_step)
        their_up = send(up_new, 1)
    else:
        second = gate_head = head_step((theirs_raw,), costs=long_step)
        their_gate_head = send(gate_head)
    terms = partial_sums(hidden, d_gate, d_up, gate_w, up_w, down_w, (second,))
    layer_out, grad_in = summed(terms)
    if shared:
        down_new = down_step((layer_out,))
        their_down = send(down_new, 1)
        gate_head = head_step((their_first, down_new))
        their_gate_head = send(gate_head)
    landed = their_up if shared else their_first
    gate_tail = step_rows(gate_w, d_gate, tokens, width_scale, cut, BLOCK, (landed, gate_head, layer_out))
    their_gate_tail = send(gate_tail)

    their_tokens = rows_of(their_first, units, tokens_local.shape[0], 16)
    their_tokens, gate_tail = lax.optimization_barrier((their_tokens, gate_tail))

    def up_from_raw(their_blocks):
        return mean_of_steps(
            up_w, d_up, tokens, theirs_raw, their_first, their_blocks, width_scale, units, units, (gate_tail,)
        )

    if shared:
        (their_blocks,) = gathered(their_tokens)
        new_up = lax.cond(
            is_early,
            up_from_raw,
            lambda _: mean_rows(up_new, their_up, units, None, 0, units),
            their_blocks,
        )
        new_down = lax.cond(
            is_early,
            lambda after: mean_rows(first, their_first, units, None, 0, units, (after,)),
            lambda after: mean_rows(down_new, their_down, units, None, 0, units, (after,)),
            new_up,
        )
    else:
        their_blocks, new_down = gathered_beside(their_tokens, first, their_first)
        new_up = up_from_raw(their_blocks)
    new_gate = mean_rows(gate_head, their_gate_head, cut, None, 0, units, (new_up, new_down))
    new_gate = mean_rows(gate_tail, their_gate_tail, BLOCK, new_gate, cut, units)
    return layer_out, grad_in, new_gate, new_up, new_down


def shards(activations, out_grad, gate_weight, up_weight, down_weight, step_index):
    levels = lax.axis_size("rep").bit_length() - 1
    branches = [partial(whole_step, 1 << level) for level in range(levels)]
    layer_out, grad_in, gate, up, down = lax.switch(
        step_index[0] % levels,
        branches,
        (step_index[0] // levels) % 2 == 0,
        activations[0],
        out_grad[0],
        gate_weight[0].T,
        up_weight[0].T,
        down_weight[0],
    )
    return layer_out[None], grad_in[None], gate.T[None], up.T[None], down[None]


def solution(mesh):
    in_specs = (
        P("rep", "tp", None),
        P("rep", "tp", None),
        P("rep", None, "tp"),
        P("rep", None, "tp"),
        P("rep", "tp", None),
        P(),
    )
    out_specs = (
        P("rep", "tp", None),
        P("rep", "tp", None),
        P("rep", None, "tp"),
        P("rep", None, "tp"),
        P("rep", "tp", None),
    )
    return jax.shard_map(shards, mesh=mesh, in_specs=in_specs, out_specs=out_specs, check_vma=False)
```

```python
from functools import partial
import math

import jax
import jax.numpy as jnp
from jax import lax
from jax.experimental import pallas as pl
from jax.experimental.pallas import tpu as pltpu
from jax.sharding import PartitionSpec as P

D = 2560
FF = 6912
BLOCK = 144


learn_rate = 0.8
width_scale = 1.0 / math.sqrt(D)
hidden_scale = 1.0 / math.sqrt(FF)

ANY = pl.BlockSpec(memory_space=pl.ANY)
PARAMS = pltpu.CompilerParams(vmem_limit_bytes=40 * 1024 * 1024)


def ring_of(devices):
    y_size = 1 << ((devices.bit_length() - 1) // 2)
    z_size = devices // y_size
    walk = [(z, 0) for z in range(z_size)]
    for z in reversed(range(z_size)):
        ys = list(range(1, y_size))
        walk += [(z, y) for y in (ys if (z_size - 1 - z) % 2 == 0 else reversed(ys))]
    return [z * y_size + y for z, y in walk]


def mm(a, b, dims):
    return lax.dot_general(a, b, (dims, ((), ())), preferred_element_type=jnp.float32)


def cost(matmuls, rows, blocks_moved):
    return pl.CostEstimate(
        flops=2 * matmuls * rows * 256 * D, bytes_accessed=blocks_moved * rows * D * 2, transcendentals=0
    )


def rows_spec(first=0, width=D, block=BLOCK):
    return pl.BlockSpec((block, width), lambda i: (i + first, 0))


def block_of(units, most):
    return max(size for size in range(BLOCK, most + 1, BLOCK) if units % size == 0)


def whole_spec(x):
    return pl.BlockSpec(x.shape, lambda i: (0,) * x.ndim)


def forward(token_blocks, grad_blocks, gate_w, up_w, down_w):
    units, devices = gate_w.shape[0], len(token_blocks)
    part = token_blocks[0].shape[0]
    count = devices * part
    block = block_of(units, 288)

    def body(*refs):
        gate_ref, up_ref, down_ref = refs[2 * devices : 2 * devices + 3]
        tokens_ref, grads_ref, hidden_ref, d_gate_ref, d_up_ref, turned, turned_grads = refs[-7:]

        @pl.when(pl.program_id(0) == 0)
        def _():
            for at in range(devices):
                tokens_ref[pl.ds(at * part, part)] = refs[at][...]
                grads_ref[pl.ds(at * part, part)] = refs[devices + at][...]
            turned[...] = tokens_ref[...].T
            turned_grads[...] = grads_ref[...].T

        gate_pre = mm(gate_ref[...], turned[...], ((1,), (0,))) * width_scale
        up_pre = mm(up_ref[...], turned[...], ((1,), (0,))) * width_scale
        d_hidden = mm(down_ref[...], turned_grads[...], ((1,), (0,))) * hidden_scale
        sigmoid_gate = jax.nn.sigmoid(gate_pre)
        activated = gate_pre * sigmoid_gate
        slope = sigmoid_gate * (1.0 + gate_pre * (1.0 - sigmoid_gate))
        hidden_ref[...] = (activated * up_pre).astype(jnp.bfloat16)
        d_gate_ref[...] = (d_hidden * up_pre * slope).astype(jnp.bfloat16)
        d_up_ref[...] = (d_hidden * activated).astype(jnp.bfloat16)

    whole = jax.ShapeDtypeStruct((count, D), jnp.bfloat16)
    out = jax.ShapeDtypeStruct((units, count), jnp.bfloat16)
    pieces = [*token_blocks, *grad_blocks]
    return pl.pallas_call(
        body,
        grid=(units // block,),
        in_specs=[whole_spec(piece) for piece in pieces] + [rows_spec(block=block)] * 3,
        out_specs=[whole_spec(whole)] * 2 + [rows_spec(0, count, block)] * 3,
        out_shape=[whole] * 2 + [out] * 3,
        scratch_shapes=[pltpu.VMEM((D, count), jnp.bfloat16)] * 2,
        compiler_params=PARAMS,
        cost_estimate=cost(3, units, 3),
        name="forward",
    )(*pieces, gate_w, up_w, down_w)


def stepped(weight, left, right, scale):
    return weight.astype(jnp.float32) - learn_rate * (mm(left, right, ((1,), (0,))) * scale)


def step_rows(weight, left, right, scale, first, rows, after=(), beside=None, below=None, costs=None):
    at, steps = first // BLOCK, rows // BLOCK
    count = left.shape[1]
    here = lambda i: (jnp.minimum(i, steps - 1) + at, 0)
    ins = (weight, left, right)
    specs = [pl.BlockSpec((BLOCK, D), here), pl.BlockSpec((BLOCK, count), here), whole_spec(right)]
    out_rows, width = rows, D
    if beside is not None:
        ins = (*ins, beside, below)
        specs += [pl.BlockSpec((BLOCK, count), lambda i: (jnp.minimum(i, steps - 1), 0)), whole_spec(below)]
        out_rows, width = rows + below.shape[0], D + count

    def body(weight_ref, left_ref, right_ref, *rest):
        out_ref = rest[-1]

        @pl.when(pl.program_id(0) < steps)
        def _():
            out_ref[:, :D] = stepped(weight_ref[...], left_ref[...], right_ref[...], scale).astype(jnp.bfloat16)
            if beside is not None:
                out_ref[:, D:] = rest[0][...]

        if below is not None:

            @pl.when(pl.program_id(0) == steps)
            def _():
                out_ref[pl.ds(0, below.shape[0]), :D] = rest[1][...]

    return pl.pallas_call(
        body,
        grid=(steps if below is None else steps + 1,),
        in_specs=specs + [ANY] * len(after),
        out_specs=rows_spec(0, width),
        out_shape=jax.ShapeDtypeStruct((out_rows, width), jnp.bfloat16),
        compiler_params=PARAMS,
        cost_estimate=costs or cost(1, rows, 2),
        name="step_rows",
    )(*ins, *after)


def rows_of(x, first, rows, block):
    at = first // block

    def body(x_ref, out_ref):
        out_ref[...] = x_ref[...]

    return pl.pallas_call(
        body,
        grid=(rows // block,),
        in_specs=[rows_spec(at, block=block)],
        out_specs=rows_spec(block=block),
        out_shape=jax.ShapeDtypeStruct((rows, D), x.dtype),
        compiler_params=PARAMS,
        cost_estimate=cost(0, rows, 2),
        name="rows_of",
    )(x)


def halved_sum(mine, theirs):
    return ((mine.astype(jnp.float32) + theirs.astype(jnp.float32)) * 0.5).astype(jnp.bfloat16)


def into_rows(body, ins, in_specs, base, first, rows, units, costs, name, after, scratch=()):
    others = after if base is None else (base, *after)

    def with_others(*refs):
        body(*refs[: len(ins)], *refs[len(ins) + len(others) :])
    return pl.pallas_call(
        with_others,
        grid=(rows // BLOCK,),
        in_specs=in_specs + [ANY] * len(others),
        out_specs=rows_spec(first // BLOCK),
        out_shape=jax.ShapeDtypeStruct((units, D), jnp.bfloat16),
        input_output_aliases={} if base is None else {len(ins): 0},
        scratch_shapes=scratch,
        compiler_params=PARAMS,
        cost_estimate=costs,
        name=name,
    )(*ins, *others)


def mean_rows(mine, theirs, rows, base, first, units, after=(), source=0):
    def body(mine_ref, theirs_ref, out_ref):
        @pl.loop(0, BLOCK // 48)
        def _(strip):
            at = pl.ds(pl.multiple_of(strip * 48, 48), 48)
            out_ref[at] = halved_sum(mine_ref[at], theirs_ref[at])

    specs = [rows_spec(source // BLOCK)] * 2
    return into_rows(
        body, (mine, theirs), specs, base, first, rows, units, cost(0, rows, 3), "mean_rows", after
    )


def mean_of_steps(mine, left, right, theirs, their_left, their_blocks, scale, rows, units, after):
    part = their_blocks[0].shape[0]

    def body(mine_ref, left_ref, right_ref, theirs_ref, their_left_ref, *rest):
        out_ref, their_right = rest[-2:]

        @pl.when(pl.program_id(0) == 0)
        def _():
            for at in range(len(their_blocks)):
                their_right[pl.ds(at * part, part)] = rest[at][...]

        own = stepped(mine_ref[...], left_ref[...], right_ref[...], scale).astype(jnp.bfloat16)
        other = stepped(theirs_ref[...], their_left_ref[...], their_right[...], scale).astype(jnp.bfloat16)
        out_ref[...] = halved_sum(own, other)

    count = left.shape[1]
    return into_rows(
        body,
        (mine, left, right, theirs, their_left, *their_blocks),
        [rows_spec(), rows_spec(0, count), whole_spec(right)]
        + [rows_spec(), pl.BlockSpec((BLOCK, count), lambda i: (i, D // count))]
        + [whole_spec(block) for block in their_blocks],
        None,
        0,
        rows,
        units,
        cost(2, rows, 3),
        "mean_of_steps",
        after,
        [pltpu.VMEM((count, D), jnp.bfloat16)],
    )


def partial_sums(hidden, d_gate, d_up, gate_w, up_w, down_w, after):
    units, count = hidden.shape
    block = block_of(units, 432)
    steps = units // block

    def body(hidden_ref, d_gate_ref, d_up_ref, gate_ref, up_ref, down_ref, *rest):
        layer_ref, grad_ref = rest[-2:]

        @pl.when(pl.program_id(0) == 0)
        def _():
            layer_ref[...] = jnp.zeros_like(layer_ref)
            grad_ref[...] = jnp.zeros_like(grad_ref)

        layer_ref[...] += mm(hidden_ref[...], down_ref[...], ((0,), (0,))) * hidden_scale
        grad_sum = mm(d_gate_ref[...], gate_ref[...], ((0,), (0,))) + mm(d_up_ref[...], up_ref[...], ((0,), (0,)))
        grad_ref[...] += grad_sum * width_scale

    out = jax.ShapeDtypeStruct((count, D), jnp.float32)
    return pl.pallas_call(
        body,
        grid=(steps,),
        in_specs=[rows_spec(0, count, block)] * 3 + [rows_spec(block=block)] * 3 + [ANY] * len(after),
        out_specs=[whole_spec(out)] * 2,
        out_shape=[out] * 2,
        compiler_params=PARAMS,
        cost_estimate=cost(3, units, 3),
        name="partial_sums",
    )(hidden, d_gate, d_up, gate_w, up_w, down_w, *after)


def whole_step(distance, turned, tokens_local, grads_local, gate_w, up_w, down_w):
    units = gate_w.shape[0]
    devices = lax.axis_size("tp")
    ring = ring_of(devices)

    def send(x, parity=None):
        replicas = lax.axis_size("rep")
        senders = [i for i in range(replicas) if parity is None or i % 2 == parity]
        return lax.ppermute(x, "rep", [(i, (i + distance) % replicas) for i in senders])

    def along(x, by):
        return lax.ppermute(x, "tp", [(ring[i], ring[(i + by) % devices]) for i in range(devices)])

    shared = distance % 2 == 0
    early = 0 if shared else None
    is_early = lax.axis_index("rep") % 2 == 0
    theirs_raw = send(up_w, early)

    half = devices // 2

    def gather(turn, locals_):
        held = [[x] * devices for x in locals_]
        for hop in range(1, half + 1):
            for at, blocks_held in enumerate(held):
                last_way = turn if at % 2 == 0 else -turn
                for way in (turn, -turn):
                    if hop < half or way == last_way:
                        blocks_held[-way * hop] = along(blocks_held[-way * (hop - 1)], way)
        return [blocks_held[1:] for blocks_held in held]

    def gathered(*locals_):
        if devices > 8:
            return [list(lax.all_gather(x, "tp")) for x in locals_]
        others = lax.cond(turned, partial(gather, 1), partial(gather, -1), locals_)
        return [[x, *rest] for x, rest in zip(locals_, others)]

    def gathered_beside(x, mine, theirs):
        if devices > 8:
            return list(lax.all_gather(x, "tp")), mean_rows(mine, theirs, units, None, 0, units)

        def branch(turn, x, mine, theirs):
            held, mean, done = [x] * devices, None, 0
            for hop in range(1, half + 1):
                for way in (turn, -turn):
                    if hop < half or way == turn:
                        held[-way * hop] = along(held[-way * (hop - 1)], way)
                if hop < half:
                    upto = units // BLOCK * hop // (half - 1) * BLOCK
                    mean = mean_rows(mine, theirs, upto - done, mean, done, units, (), done)
                    held[-turn * hop], mean = lax.optimization_barrier((held[-turn * hop], mean))
                    done = upto
            return held[1:], mean

        others, mean = lax.cond(turned, partial(branch, 1), partial(branch, -1), x, mine, theirs)
        return [x, *others], mean

    def summed(terms):
        if devices > 8:
            totals = [lax.psum_scatter(term, "tp", scatter_dimension=0, tiled=True) for term in terms]
            return [total.astype(jnp.bfloat16) for total in totals]
        return lax.cond(turned, partial(sums, 1), partial(sums, -1), terms)

    def sums(turn, terms):
        part = terms[0].shape[0] // devices
        block_at = lambda term, offset: term[(offset % devices) * part : (offset % devices + 1) * part]
        ways = [(at, way, half - (0 if (way == turn) == (at == 0) else 1)) for at in (0, 1) for way in (turn, -turn)]
        moving = {}
        for hop in range(1, half + 1):
            for at, way, hops in ways:
                if hop <= hops:
                    block = block_at(terms[at], way * (hops + 1 - hop))
                    if hop > 1:
                        block = block + moving[at, way].astype(jnp.float32)
                    moving[at, way] = along(block.astype(jnp.bfloat16), way)
        totals = []
        for at, term in enumerate(terms):
            total = block_at(term, 0)
            for way in (turn, -turn):
                total = total + moving[at, way].astype(jnp.float32)
            totals.append(total.astype(jnp.bfloat16))
        return totals

    token_blocks, grad_blocks = gathered(tokens_local, grads_local)
    tokens, grads, hidden, d_gate, d_up = forward(token_blocks, grad_blocks, gate_w, up_w, down_w)
    cut = units - BLOCK
    down_step = partial(step_rows, down_w, hidden, grads, hidden_scale, 0, units)
    head_step = partial(step_rows, gate_w, d_gate, tokens, width_scale, 0, cut)
    long_step = cost(20, units, 40)
    first = down_step(beside=d_up, below=tokens_local)
    their_first = send(first, early)
    if shared:
        second = up_new = step_rows(up_w, d_up, tokens, width_scale, 0, units, (theirs_raw,), costs=long_step)
        their_up = send(up_new, 1)
    else:
        second = gate_head = head_step((theirs_raw,), costs=long_step)
        their_gate_head = send(gate_head)
    terms = partial_sums(hidden, d_gate, d_up, gate_w, up_w, down_w, (second,))
    layer_out, grad_in = summed(terms)
    if shared:
        down_new = down_step((layer_out,))
        their_down = send(down_new, 1)
        gate_head = head_step((their_first, down_new))
        their_gate_head = send(gate_head)
    landed = their_up if shared else their_first
    gate_tail = step_rows(gate_w, d_gate, tokens, width_scale, cut, BLOCK, (landed, gate_head, layer_out))
    their_gate_tail = send(gate_tail)

    their_tokens = rows_of(their_first, units, tokens_local.shape[0], 16)
    their_tokens, gate_tail = lax.optimization_barrier((their_tokens, gate_tail))

    def up_from_raw(their_blocks):
        return mean_of_steps(
            up_w, d_up, tokens, theirs_raw, their_first, their_blocks, width_scale, units, units, (gate_tail,)
        )

    if shared:
        (their_blocks,) = gathered(their_tokens)
        new_up = lax.cond(
            is_early,
            up_from_raw,
            lambda _: mean_rows(up_new, their_up, units, None, 0, units),
            their_blocks,
        )
        new_down = lax.cond(
            is_early,
            lambda after: mean_rows(first, their_first, units, None, 0, units, (after,)),
            lambda after: mean_rows(down_new, their_down, units, None, 0, units, (after,)),
            new_up,
        )
    else:
        their_blocks, new_down = gathered_beside(their_tokens, first, their_first)
        new_up = up_from_raw(their_blocks)
    new_gate = mean_rows(gate_head, their_gate_head, cut, None, 0, units, (new_up, new_down))
    new_gate = mean_rows(gate_tail, their_gate_tail, BLOCK, new_gate, cut, units)
    return layer_out, grad_in, new_gate, new_up, new_down


def shards(activations, out_grad, gate_weight, up_weight, down_weight, step_index):
    levels = lax.axis_size("rep").bit_length() - 1
    branches = [partial(whole_step, 1 << level) for level in range(levels)]
    layer_out, grad_in, gate, up, down = lax.switch(
        step_index[0] % levels,
        branches,
        (step_index[0] // levels) % 2 == 0,
        activations[0],
        out_grad[0],
        gate_weight[0].T,
        up_weight[0].T,
        down_weight[0],
    )
    return layer_out[None], grad_in[None], gate.T[None], up.T[None], down[None]


def solution(mesh):
    in_specs = (
        P("rep", "tp", None),
        P("rep", "tp", None),
        P("rep", None, "tp"),
        P("rep", None, "tp"),
        P("rep", "tp", None),
        P(),
    )
    out_specs = (
        P("rep", "tp", None),
        P("rep", "tp", None),
        P("rep", None, "tp"),
        P("rep", None, "tp"),
        P("rep", "tp", None),
    )
    return jax.shard_map(shards, mesh=mesh, in_specs=in_specs, out_specs=out_specs, check_vma=False)
```

```python
from functools import partial
import math

import jax
import jax.numpy as jnp
from jax import lax
from jax.experimental import pallas as pl
from jax.experimental.pallas import tpu as pltpu
from jax.sharding import PartitionSpec as P

D = 2560
FF = 6912
BLOCK = 144


learn_rate = 0.8
width_scale = 1.0 / math.sqrt(D)
hidden_scale = 1.0 / math.sqrt(FF)

ANY = pl.BlockSpec(memory_space=pl.ANY)
PARAMS = pltpu.CompilerParams(vmem_limit_bytes=40 * 1024 * 1024)


def ring_of(devices):
    y_size = 1 << ((devices.bit_length() - 1) // 2)
    z_size = devices // y_size
    walk = [(z, 0) for z in range(z_size)]
    for z in reversed(range(z_size)):
        ys = list(range(1, y_size))
        walk += [(z, y) for y in (ys if (z_size - 1 - z) % 2 == 0 else reversed(ys))]
    return [z * y_size + y for z, y in walk]


def mm(a, b, dims):
    return lax.dot_general(a, b, (dims, ((), ())), preferred_element_type=jnp.float32)


def cost(matmuls, rows, blocks_moved):
    return pl.CostEstimate(
        flops=2 * matmuls * rows * 256 * D, bytes_accessed=blocks_moved * rows * D * 2, transcendentals=0
    )


def rows_spec(first=0, width=D, block=BLOCK):
    return pl.BlockSpec((block, width), lambda i: (i + first, 0))


def block_of(units, most):
    return max(size for size in range(BLOCK, most + 1, BLOCK) if units % size == 0)


def whole_spec(x):
    return pl.BlockSpec(x.shape, lambda i: (0,) * x.ndim)


def forward(token_blocks, grad_blocks, gate_w, up_w, down_w):
    units, devices = gate_w.shape[0], len(token_blocks)
    part = token_blocks[0].shape[0]
    count = devices * part
    block = block_of(units, 288)

    def body(*refs):
        gate_ref, up_ref, down_ref = refs[2 * devices : 2 * devices + 3]
        tokens_ref, grads_ref, hidden_ref, d_gate_ref, d_up_ref, turned, turned_grads = refs[-7:]

        @pl.when(pl.program_id(0) == 0)
        def _():
            for at in range(devices):
                tokens_ref[pl.ds(at * part, part)] = refs[at][...]
                grads_ref[pl.ds(at * part, part)] = refs[devices + at][...]
            turned[...] = tokens_ref[...].T
            turned_grads[...] = grads_ref[...].T

        gate_pre = mm(gate_ref[...], turned[...], ((1,), (0,))) * width_scale
        up_pre = mm(up_ref[...], turned[...], ((1,), (0,))) * width_scale
        d_hidden = mm(down_ref[...], turned_grads[...], ((1,), (0,))) * hidden_scale
        sigmoid_gate = jax.nn.sigmoid(gate_pre)
        activated = gate_pre * sigmoid_gate
        slope = sigmoid_gate * (1.0 + gate_pre * (1.0 - sigmoid_gate))
        hidden_ref[...] = (activated * up_pre).astype(jnp.bfloat16)
        d_gate_ref[...] = (d_hidden * up_pre * slope).astype(jnp.bfloat16)
        d_up_ref[...] = (d_hidden * activated).astype(jnp.bfloat16)

    whole = jax.ShapeDtypeStruct((count, D), jnp.bfloat16)
    out = jax.ShapeDtypeStruct((units, count), jnp.bfloat16)
    pieces = [*token_blocks, *grad_blocks]
    return pl.pallas_call(
        body,
        grid=(units // block,),
        in_specs=[whole_spec(piece) for piece in pieces] + [rows_spec(block=block)] * 3,
        out_specs=[whole_spec(whole)] * 2 + [rows_spec(0, count, block)] * 3,
        out_shape=[whole] * 2 + [out] * 3,
        scratch_shapes=[pltpu.VMEM((D, count), jnp.bfloat16)] * 2,
        compiler_params=PARAMS,
        cost_estimate=cost(3, units, 3),
        name="forward",
    )(*pieces, gate_w, up_w, down_w)


def stepped(weight, left, right, scale):
    return weight.astype(jnp.float32) - learn_rate * (mm(left, right, ((1,), (0,))) * scale)


def step_rows(weight, left, right, scale, first, rows, after=(), beside=(), costs=None):
    at = first // BLOCK
    ins = (weight, left, right, *beside)
    widths = [x.shape[1] for x in beside]

    def body(weight_ref, left_ref, right_ref, *rest):
        out_ref = rest[-1]
        out_ref[:, :D] = stepped(weight_ref[...], left_ref[...], right_ref[...], scale).astype(jnp.bfloat16)
        column = D
        for x_ref, width in zip(rest, widths):
            out_ref[:, column : column + width] = x_ref[...]
            column += width

    return pl.pallas_call(
        body,
        grid=(rows // BLOCK,),
        in_specs=[rows_spec(at), rows_spec(at, left.shape[1]), whole_spec(right)]
        + [rows_spec(0, width) for width in widths]
        + [ANY] * len(after),
        out_specs=rows_spec(0, D + sum(widths)),
        out_shape=jax.ShapeDtypeStruct((rows, D + sum(widths)), jnp.bfloat16),
        compiler_params=PARAMS,
        cost_estimate=costs or cost(1, rows, 2),
        name="step_rows",
    )(*ins, *after)


def halved_sum(mine, theirs):
    return ((mine.astype(jnp.float32) + theirs.astype(jnp.float32)) * 0.5).astype(jnp.bfloat16)


def into_rows(body, ins, in_specs, base, first, rows, units, costs, name, after, scratch=()):
    others = after if base is None else (base, *after)

    def with_others(*refs):
        body(*refs[: len(ins)], *refs[len(ins) + len(others) :])
    return pl.pallas_call(
        with_others,
        grid=(rows // BLOCK,),
        in_specs=in_specs + [ANY] * len(others),
        out_specs=rows_spec(first // BLOCK),
        out_shape=jax.ShapeDtypeStruct((units, D), jnp.bfloat16),
        input_output_aliases={} if base is None else {len(ins): 0},
        scratch_shapes=scratch,
        compiler_params=PARAMS,
        cost_estimate=costs,
        name=name,
    )(*ins, *others)


def mean_rows(mine, theirs, rows, base, first, units, after=(), source=0):
    def body(mine_ref, theirs_ref, out_ref):
        @pl.loop(0, BLOCK // 16)
        def _(strip):
            at = pl.ds(pl.multiple_of(strip * 16, 16), 16)
            out_ref[at] = halved_sum(mine_ref[at], theirs_ref[at])

    specs = [rows_spec(source // BLOCK)] * 2
    return into_rows(
        body, (mine, theirs), specs, base, first, rows, units, cost(0, rows, 3), "mean_rows", after
    )


def mean_of_steps(mine, left, right, theirs, their_left, their_blocks, scale, rows, units, after):
    part = their_blocks[0].shape[0]

    def body(mine_ref, left_ref, right_ref, theirs_ref, their_left_ref, *rest):
        out_ref, their_right = rest[-2:]

        @pl.when(pl.program_id(0) == 0)
        def _():
            for at in range(len(their_blocks)):
                their_right[pl.ds(at * part, part)] = rest[at][...]

        own = stepped(mine_ref[...], left_ref[...], right_ref[...], scale).astype(jnp.bfloat16)
        other = stepped(theirs_ref[...], their_left_ref[...], their_right[...], scale).astype(jnp.bfloat16)
        out_ref[...] = halved_sum(own, other)

    count = left.shape[1]
    return into_rows(
        body,
        (mine, left, right, theirs, their_left, *their_blocks),
        [rows_spec(), rows_spec(0, count), whole_spec(right)]
        + [rows_spec(), pl.BlockSpec((BLOCK, count), lambda i: (i, D // count))]
        + [whole_spec(block) for block in their_blocks],
        None,
        0,
        rows,
        units,
        cost(2, rows, 3),
        "mean_of_steps",
        after,
        [pltpu.VMEM((count, D), jnp.bfloat16)],
    )


def partial_sums(hidden, d_gate, d_up, gate_w, up_w, down_w, after):
    units, count = hidden.shape
    block = block_of(units, 432)
    steps = units // block

    def body(hidden_ref, d_gate_ref, d_up_ref, gate_ref, up_ref, down_ref, *rest):
        layer_ref, grad_ref = rest[-2:]

        @pl.when(pl.program_id(0) == 0)
        def _():
            layer_ref[...] = jnp.zeros_like(layer_ref)
            grad_ref[...] = jnp.zeros_like(grad_ref)

        layer_ref[...] += mm(hidden_ref[...], down_ref[...], ((0,), (0,))) * hidden_scale
        grad_sum = mm(d_gate_ref[...], gate_ref[...], ((0,), (0,))) + mm(d_up_ref[...], up_ref[...], ((0,), (0,)))
        grad_ref[...] += grad_sum * width_scale

    out = jax.ShapeDtypeStruct((count, D), jnp.float32)
    return pl.pallas_call(
        body,
        grid=(steps,),
        in_specs=[rows_spec(0, count, block)] * 3 + [rows_spec(block=block)] * 3 + [ANY] * len(after),
        out_specs=[whole_spec(out)] * 2,
        out_shape=[out] * 2,
        compiler_params=PARAMS,
        cost_estimate=cost(3, units, 3),
        name="partial_sums",
    )(hidden, d_gate, d_up, gate_w, up_w, down_w, *after)


def whole_step(distance, turned, tokens_local, grads_local, gate_w, up_w, down_w):
    units = gate_w.shape[0]
    devices = lax.axis_size("tp")
    ring = ring_of(devices)

    def send(x, parity=None):
        replicas = lax.axis_size("rep")
        senders = [i for i in range(replicas) if parity is None or i % 2 == parity]
        return lax.ppermute(x, "rep", [(i, (i + distance) % replicas) for i in senders])

    def along(x, by):
        return lax.ppermute(x, "tp", [(ring[i], ring[(i + by) % devices]) for i in range(devices)])

    shared = distance % 2 == 0
    early = 0 if shared else None
    is_early = lax.axis_index("rep") % 2 == 0
    theirs_raw = send(up_w, early)

    half = devices // 2

    def gather(turn, locals_):
        held = [[x] * devices for x in locals_]
        for hop in range(1, half + 1):
            for at, blocks_held in enumerate(held):
                last_way = turn if at % 2 == 0 else -turn
                for way in (turn, -turn):
                    if hop < half or way == last_way:
                        blocks_held[-way * hop] = along(blocks_held[-way * (hop - 1)], way)
        return [blocks_held[1:] for blocks_held in held]

    def gathered(*locals_):
        if devices > 8:
            return [list(lax.all_gather(x, "tp")) for x in locals_]
        others = lax.cond(turned, partial(gather, 1), partial(gather, -1), locals_)
        return [[x, *rest] for x, rest in zip(locals_, others)]

    def gathered_beside(x, mine, theirs):
        if devices > 8:
            return list(lax.all_gather(x, "tp")), mean_rows(mine, theirs, units, None, 0, units)

        def branch(turn, x, mine, theirs):
            held, mean, done = [x] * devices, None, 0
            for hop in range(1, half + 1):
                for way in (turn, -turn):
                    if hop < half or way == turn:
                        held[-way * hop] = along(held[-way * (hop - 1)], way)
                if hop < half:
                    upto = units // BLOCK * hop // (half - 1) * BLOCK
                    mean = mean_rows(mine, theirs, upto - done, mean, done, units, (), done)
                    held[-turn * hop], mean = lax.optimization_barrier((held[-turn * hop], mean))
                    done = upto
            return held[1:], mean

        others, mean = lax.cond(turned, partial(branch, 1), partial(branch, -1), x, mine, theirs)
        return [x, *others], mean

    def summed(terms):
        if devices > 8:
            totals = [lax.psum_scatter(term, "tp", scatter_dimension=0, tiled=True) for term in terms]
            return [total.astype(jnp.bfloat16) for total in totals]
        return lax.cond(turned, partial(sums, 1), partial(sums, -1), terms)

    def sums(turn, terms):
        part = terms[0].shape[0] // devices
        block_at = lambda term, offset: term[(offset % devices) * part : (offset % devices + 1) * part]
        ways = [(at, way, half - (0 if (way == turn) == (at == 0) else 1)) for at in (0, 1) for way in (turn, -turn)]
        moving = {}
        for hop in range(1, half + 1):
            for at, way, hops in ways:
                if hop <= hops:
                    block = block_at(terms[at], way * (hops + 1 - hop))
                    if hop > 1:
                        block = block + moving[at, way].astype(jnp.float32)
                    moving[at, way] = along(block.astype(jnp.bfloat16), way)
        totals = []
        for at, term in enumerate(terms):
            total = block_at(term, 0)
            for way in (turn, -turn):
                total = total + moving[at, way].astype(jnp.float32)
            totals.append(total.astype(jnp.bfloat16))
        return totals

    token_blocks, grad_blocks = gathered(tokens_local, grads_local)
    tokens, grads, hidden, d_gate, d_up = forward(token_blocks, grad_blocks, gate_w, up_w, down_w)
    cut = units - BLOCK
    down_step = partial(step_rows, down_w, hidden, grads, hidden_scale, 0, units)
    head_step = partial(step_rows, gate_w, d_gate, tokens, width_scale, 0, cut)
    long_step = cost(20, units, 40)
    shard = tokens_local.reshape(-1, 128)
    padding = ((0, units - shard.shape[0]), (0, 0))
    first = down_step(beside=(d_up, jnp.pad(shard, padding)))
    their_first = send(first, early)
    if shared:
        second = up_new = step_rows(up_w, d_up, tokens, width_scale, 0, units, (theirs_raw,), costs=long_step)
        their_up = send(up_new, 1)
    else:
        second = gate_head = head_step((theirs_raw,), costs=long_step)
        their_gate_head = send(gate_head)
    terms = partial_sums(hidden, d_gate, d_up, gate_w, up_w, down_w, (second,))
    layer_out, grad_in = summed(terms)
    if shared:
        down_new = down_step((layer_out,))
        their_down = send(down_new, 1)
        gate_head = head_step((their_first, down_new))
        their_gate_head = send(gate_head)
    landed = their_up if shared else their_first
    gate_tail = step_rows(gate_w, d_gate, tokens, width_scale, cut, BLOCK, (landed, gate_head, layer_out))
    their_gate_tail = send(gate_tail)

    their_tokens = their_first[: shard.shape[0], -128:].reshape(tokens_local.shape)
    their_tokens, gate_tail = lax.optimization_barrier((their_tokens, gate_tail))

    def up_from_raw(their_blocks):
        return mean_of_steps(
            up_w, d_up, tokens, theirs_raw, their_first, their_blocks, width_scale, units, units, (gate_tail,)
        )

    if shared:
        (their_blocks,) = gathered(their_tokens)
        new_up = lax.cond(
            is_early,
            up_from_raw,
            lambda _: mean_rows(up_new, their_up, units, None, 0, units),
            their_blocks,
        )
        new_down = lax.cond(
            is_early,
            lambda after: mean_rows(first, their_first, units, None, 0, units, (after,)),
            lambda after: mean_rows(down_new, their_down, units, None, 0, units, (after,)),
            new_up,
        )
    else:
        their_blocks, new_down = gathered_beside(their_tokens, first, their_first)
        new_up = up_from_raw(their_blocks)
    new_gate = mean_rows(gate_head, their_gate_head, cut, None, 0, units, (new_up, new_down))
    new_gate = mean_rows(gate_tail, their_gate_tail, BLOCK, new_gate, cut, units)
    return layer_out, grad_in, new_gate, new_up, new_down


def shards(activations, out_grad, gate_weight, up_weight, down_weight, step_index):
    levels = lax.axis_size("rep").bit_length() - 1
    branches = [partial(whole_step, 1 << level) for level in range(levels)]
    layer_out, grad_in, gate, up, down = lax.switch(
        step_index[0] % levels,
        branches,
        (step_index[0] // levels) % 2 == 0,
        activations[0],
        out_grad[0],
        gate_weight[0].T,
        up_weight[0].T,
        down_weight[0],
    )
    return layer_out[None], grad_in[None], gate.T[None], up.T[None], down[None]


def solution(mesh):
    in_specs = (
        P("rep", "tp", None),
        P("rep", "tp", None),
        P("rep", None, "tp"),
        P("rep", None, "tp"),
        P("rep", "tp", None),
        P(),
    )
    out_specs = (
        P("rep", "tp", None),
        P("rep", "tp", None),
        P("rep", None, "tp"),
        P("rep", None, "tp"),
        P("rep", "tp", None),
    )
    return jax.shard_map(shards, mesh=mesh, in_specs=in_specs, out_specs=out_specs, check_vma=False)
```

```python
from functools import partial
import math

import jax
import jax.numpy as jnp
from jax import lax
from jax.experimental import pallas as pl
from jax.experimental.pallas import tpu as pltpu
from jax.sharding import PartitionSpec as P

D = 2560
FF = 6912
BLOCK = 144


learn_rate = 0.8
width_scale = 1.0 / math.sqrt(D)
hidden_scale = 1.0 / math.sqrt(FF)

ANY = pl.BlockSpec(memory_space=pl.ANY)
PARAMS = pltpu.CompilerParams(vmem_limit_bytes=40 * 1024 * 1024)


def ring_of(devices):
    y_size = 1 << ((devices.bit_length() - 1) // 2)
    z_size = devices // y_size
    walk = [(z, 0) for z in range(z_size)]
    for z in reversed(range(z_size)):
        ys = list(range(1, y_size))
        walk += [(z, y) for y in (ys if (z_size - 1 - z) % 2 == 0 else reversed(ys))]
    return [z * y_size + y for z, y in walk]


def mm(a, b, dims):
    return lax.dot_general(a, b, (dims, ((), ())), preferred_element_type=jnp.float32)


def cost(matmuls, rows, blocks_moved):
    return pl.CostEstimate(
        flops=2 * matmuls * rows * 256 * D, bytes_accessed=blocks_moved * rows * D * 2, transcendentals=0
    )


def rows_spec(first=0, width=D, block=BLOCK):
    return pl.BlockSpec((block, width), lambda i: (i + first, 0))


def block_of(units, most):
    return max(size for size in range(BLOCK, most + 1, BLOCK) if units % size == 0)


def whole_spec(x):
    return pl.BlockSpec(x.shape, lambda i: (0,) * x.ndim)


def forward(token_blocks, grad_blocks, gate_w, up_w, down_w):
    units, devices = gate_w.shape[0], len(token_blocks)
    part = token_blocks[0].shape[0]
    count = devices * part
    block = block_of(units, 288)

    def body(*refs):
        gate_ref, up_ref, down_ref = refs[2 * devices : 2 * devices + 3]
        tokens_ref, grads_ref, hidden_ref, d_gate_ref, d_up_ref, turned, turned_grads = refs[-7:]

        @pl.when(pl.program_id(0) == 0)
        def _():
            for at in range(devices):
                tokens_ref[pl.ds(at * part, part)] = refs[at][...]
                grads_ref[pl.ds(at * part, part)] = refs[devices + at][...]
            turned[...] = tokens_ref[...].T
            turned_grads[...] = grads_ref[...].T

        gate_pre = mm(gate_ref[...], turned[...], ((1,), (0,))) * width_scale
        up_pre = mm(up_ref[...], turned[...], ((1,), (0,))) * width_scale
        d_hidden = mm(down_ref[...], turned_grads[...], ((1,), (0,))) * hidden_scale
        sigmoid_gate = jax.nn.sigmoid(gate_pre)
        activated = gate_pre * sigmoid_gate
        slope = sigmoid_gate * (1.0 + gate_pre * (1.0 - sigmoid_gate))
        hidden_ref[...] = (activated * up_pre).astype(jnp.bfloat16)
        d_gate_ref[...] = (d_hidden * up_pre * slope).astype(jnp.bfloat16)
        d_up_ref[...] = (d_hidden * activated).astype(jnp.bfloat16)

    whole = jax.ShapeDtypeStruct((count, D), jnp.bfloat16)
    out = jax.ShapeDtypeStruct((units, count), jnp.bfloat16)
    pieces = [*token_blocks, *grad_blocks]
    return pl.pallas_call(
        body,
        grid=(units // block,),
        in_specs=[whole_spec(piece) for piece in pieces] + [rows_spec(block=block)] * 3,
        out_specs=[whole_spec(whole)] * 2 + [rows_spec(0, count, block)] * 3,
        out_shape=[whole] * 2 + [out] * 3,
        scratch_shapes=[pltpu.VMEM((D, count), jnp.bfloat16)] * 2,
        compiler_params=PARAMS,
        cost_estimate=cost(3, units, 3),
        name="forward",
    )(*pieces, gate_w, up_w, down_w)


def stepped(weight, left, right, scale):
    return weight.astype(jnp.float32) - learn_rate * (mm(left, right, ((1,), (0,))) * scale)


def step_rows(weight, left, right, scale, first, rows, after=(), costs=None):
    at = first // BLOCK

    def body(weight_ref, left_ref, right_ref, *rest):
        rest[-1][...] = stepped(weight_ref[...], left_ref[...], right_ref[...], scale).astype(jnp.bfloat16)

    return pl.pallas_call(
        body,
        grid=(rows // BLOCK,),
        in_specs=[rows_spec(at), rows_spec(at, left.shape[1]), whole_spec(right)] + [ANY] * len(after),
        out_specs=rows_spec(),
        out_shape=jax.ShapeDtypeStruct((rows, D), jnp.bfloat16),
        compiler_params=PARAMS,
        cost_estimate=costs or cost(1, rows, 2),
        name="step_rows",
    )(weight, left, right, *after)


def step_with(weight, left, right, scale, beside, below):
    units, width = beside.shape
    part = below.shape[0]
    steps = D // width
    here = lambda i: (0, jnp.minimum(i, steps - 1))

    def body(weight_ref, left_ref, right_ref, beside_ref, below_ref, out_ref):
        @pl.when(pl.program_id(0) < steps)
        def _():
            new = stepped(weight_ref[...], left_ref[...], right_ref[...], scale)
            out_ref[pl.ds(0, units)] = new.astype(jnp.bfloat16)
            out_ref[pl.ds(units, part)] = below_ref[...]

        @pl.when(pl.program_id(0) == steps)
        def _():
            out_ref[pl.ds(0, units)] = beside_ref[...]
            out_ref[pl.ds(units, part)] = jnp.zeros((part, width), jnp.bfloat16)

    return pl.pallas_call(
        body,
        grid=(steps + 1,),
        in_specs=[
            pl.BlockSpec((units, width), here),
            whole_spec(left),
            pl.BlockSpec((right.shape[0], width), here),
            whole_spec(beside),
            pl.BlockSpec((part, width), here),
        ],
        out_specs=pl.BlockSpec((units + part, width), lambda i: (0, i)),
        out_shape=jax.ShapeDtypeStruct((units + part, D + width), jnp.bfloat16),
        compiler_params=PARAMS,
        cost_estimate=cost(1, units, 2),
        name="step_with",
    )(weight, left, right, beside, below)


def last_rows(x, rows):
    at = (x.shape[0] - rows) // 16

    def body(x_ref, out_ref):
        out_ref[...] = x_ref[...]

    return pl.pallas_call(
        body,
        grid=(rows // 16,),
        in_specs=[rows_spec(at, block=16)],
        out_specs=rows_spec(block=16),
        out_shape=jax.ShapeDtypeStruct((rows, D), x.dtype),
        compiler_params=PARAMS,
        cost_estimate=cost(0, rows, 2),
        name="last_rows",
    )(x)


def halved_sum(mine, theirs):
    return ((mine.astype(jnp.float32) + theirs.astype(jnp.float32)) * 0.5).astype(jnp.bfloat16)


def into_rows(body, ins, in_specs, base, first, rows, units, costs, name, after, scratch=()):
    others = after if base is None else (base, *after)

    def with_others(*refs):
        body(*refs[: len(ins)], *refs[len(ins) + len(others) :])
    return pl.pallas_call(
        with_others,
        grid=(rows // BLOCK,),
        in_specs=in_specs + [ANY] * len(others),
        out_specs=rows_spec(first // BLOCK),
        out_shape=jax.ShapeDtypeStruct((units, D), jnp.bfloat16),
        input_output_aliases={} if base is None else {len(ins): 0},
        scratch_shapes=scratch,
        compiler_params=PARAMS,
        cost_estimate=costs,
        name=name,
    )(*ins, *others)


def mean_rows(mine, theirs, rows, base, first, units, after=(), source=0):
    def body(mine_ref, theirs_ref, out_ref):
        @pl.loop(0, BLOCK // 16)
        def _(strip):
            at = pl.ds(pl.multiple_of(strip * 16, 16), 16)
            out_ref[at] = halved_sum(mine_ref[at], theirs_ref[at])

    specs = [rows_spec(source // BLOCK)] * 2
    return into_rows(
        body, (mine, theirs), specs, base, first, rows, units, cost(0, rows, 3), "mean_rows", after
    )


def mean_of_steps(mine, left, right, theirs, their_left, their_blocks, scale, rows, units, after):
    part = their_blocks[0].shape[0]

    def body(mine_ref, left_ref, right_ref, theirs_ref, their_left_ref, *rest):
        out_ref, their_right = rest[-2:]

        @pl.when(pl.program_id(0) == 0)
        def _():
            for at in range(len(their_blocks)):
                their_right[pl.ds(at * part, part)] = rest[at][...]

        own = stepped(mine_ref[...], left_ref[...], right_ref[...], scale).astype(jnp.bfloat16)
        other = stepped(theirs_ref[...], their_left_ref[...], their_right[...], scale).astype(jnp.bfloat16)
        out_ref[...] = halved_sum(own, other)

    count = left.shape[1]
    return into_rows(
        body,
        (mine, left, right, theirs, their_left, *their_blocks),
        [rows_spec(), rows_spec(0, count), whole_spec(right)]
        + [rows_spec(), pl.BlockSpec((BLOCK, count), lambda i: (i, D // count))]
        + [whole_spec(block) for block in their_blocks],
        None,
        0,
        rows,
        units,
        cost(2, rows, 3),
        "mean_of_steps",
        after,
        [pltpu.VMEM((count, D), jnp.bfloat16)],
    )


def partial_sums(hidden, d_gate, d_up, gate_w, up_w, down_w, after):
    units, count = hidden.shape
    block = block_of(units, 432)
    steps = units // block

    def body(hidden_ref, d_gate_ref, d_up_ref, gate_ref, up_ref, down_ref, *rest):
        layer_ref, grad_ref = rest[-2:]

        @pl.when(pl.program_id(0) == 0)
        def _():
            layer_ref[...] = jnp.zeros_like(layer_ref)
            grad_ref[...] = jnp.zeros_like(grad_ref)

        layer_ref[...] += mm(hidden_ref[...], down_ref[...], ((0,), (0,))) * hidden_scale
        grad_sum = mm(d_gate_ref[...], gate_ref[...], ((0,), (0,))) + mm(d_up_ref[...], up_ref[...], ((0,), (0,)))
        grad_ref[...] += grad_sum * width_scale

    out = jax.ShapeDtypeStruct((count, D), jnp.float32)
    return pl.pallas_call(
        body,
        grid=(steps,),
        in_specs=[rows_spec(0, count, block)] * 3 + [rows_spec(block=block)] * 3 + [ANY] * len(after),
        out_specs=[whole_spec(out)] * 2,
        out_shape=[out] * 2,
        compiler_params=PARAMS,
        cost_estimate=cost(3, units, 3),
        name="partial_sums",
    )(hidden, d_gate, d_up, gate_w, up_w, down_w, *after)


def whole_step(distance, turned, tokens_local, grads_local, gate_w, up_w, down_w):
    units = gate_w.shape[0]
    devices = lax.axis_size("tp")
    ring = ring_of(devices)

    def send(x, parity=None):
        replicas = lax.axis_size("rep")
        senders = [i for i in range(replicas) if parity is None or i % 2 == parity]
        return lax.ppermute(x, "rep", [(i, (i + distance) % replicas) for i in senders])

    def along(x, by):
        return lax.ppermute(x, "tp", [(ring[i], ring[(i + by) % devices]) for i in range(devices)])

    shared = distance % 2 == 0
    early = 0 if shared else None
    is_early = lax.axis_index("rep") % 2 == 0
    theirs_raw = send(up_w, early)

    half = devices // 2

    def gather(turn, locals_):
        held = [[x] * devices for x in locals_]
        for hop in range(1, half + 1):
            for at, blocks_held in enumerate(held):
                last_way = turn if at % 2 == 0 else -turn
                for way in (turn, -turn):
                    if hop < half or way == last_way:
                        blocks_held[-way * hop] = along(blocks_held[-way * (hop - 1)], way)
        return [blocks_held[1:] for blocks_held in held]

    def gathered(*locals_):
        if devices > 8:
            return [list(lax.all_gather(x, "tp")) for x in locals_]
        others = lax.cond(turned, partial(gather, 1), partial(gather, -1), locals_)
        return [[x, *rest] for x, rest in zip(locals_, others)]

    def gathered_beside(x, mine, theirs):
        if devices > 8:
            return list(lax.all_gather(x, "tp")), mean_rows(mine, theirs, units, None, 0, units)

        def branch(turn, x, mine, theirs):
            held, mean, done = [x] * devices, None, 0
            for hop in range(1, half + 1):
                for way in (turn, -turn):
                    if hop < half or way == turn:
                        held[-way * hop] = along(held[-way * (hop - 1)], way)
                if hop < half:
                    upto = units // BLOCK * hop // (half - 1) * BLOCK
                    mean = mean_rows(mine, theirs, upto - done, mean, done, units, (), done)
                    held[-turn * hop], mean = lax.optimization_barrier((held[-turn * hop], mean))
                    done = upto
            return held[1:], mean

        others, mean = lax.cond(turned, partial(branch, 1), partial(branch, -1), x, mine, theirs)
        return [x, *others], mean

    def summed(terms):
        if devices > 8:
            totals = [lax.psum_scatter(term, "tp", scatter_dimension=0, tiled=True) for term in terms]
            return [total.astype(jnp.bfloat16) for total in totals]
        return lax.cond(turned, partial(sums, 1), partial(sums, -1), terms)

    def sums(turn, terms):
        part = terms[0].shape[0] // devices
        block_at = lambda term, offset: term[(offset % devices) * part : (offset % devices + 1) * part]
        ways = [(at, way, half - (0 if (way == turn) == (at == 0) else 1)) for at in (0, 1) for way in (turn, -turn)]
        moving = {}
        for hop in range(1, half + 1):
            for at, way, hops in ways:
                if hop <= hops:
                    block = block_at(terms[at], way * (hops + 1 - hop))
                    if hop > 1:
                        block = block + moving[at, way].astype(jnp.float32)
                    moving[at, way] = along(block.astype(jnp.bfloat16), way)
        totals = []
        for at, term in enumerate(terms):
            total = block_at(term, 0)
            for way in (turn, -turn):
                total = total + moving[at, way].astype(jnp.float32)
            totals.append(total.astype(jnp.bfloat16))
        return totals

    token_blocks, grad_blocks = gathered(tokens_local, grads_local)
    tokens, grads, hidden, d_gate, d_up = forward(token_blocks, grad_blocks, gate_w, up_w, down_w)
    cut = units - BLOCK
    down_step = partial(step_rows, down_w, hidden, grads, hidden_scale, 0, units)
    head_step = partial(step_rows, gate_w, d_gate, tokens, width_scale, 0, cut)
    long_step = cost(20, units, 40)
    first = step_with(down_w, hidden, grads, hidden_scale, d_up, tokens_local)
    their_first = send(first, early)
    if shared:
        second = up_new = step_rows(up_w, d_up, tokens, width_scale, 0, units, (theirs_raw,), costs=long_step)
        their_up = send(up_new, 1)
    else:
        second = gate_head = head_step((theirs_raw,), costs=long_step)
        their_gate_head = send(gate_head)
    terms = partial_sums(hidden, d_gate, d_up, gate_w, up_w, down_w, (second,))
    layer_out, grad_in = summed(terms)
    if shared:
        down_new = down_step((layer_out,))
        their_down = send(down_new, 1)
        gate_head = head_step((their_first, down_new))
        their_gate_head = send(gate_head)
    landed = their_up if shared else their_first
    gate_tail = step_rows(gate_w, d_gate, tokens, width_scale, cut, BLOCK, (landed, gate_head, layer_out))
    their_gate_tail = send(gate_tail)

    their_tokens = last_rows(their_first, tokens_local.shape[0])
    their_tokens, gate_tail = lax.optimization_barrier((their_tokens, gate_tail))

    def up_from_raw(their_blocks):
        return mean_of_steps(
            up_w, d_up, tokens, theirs_raw, their_first, their_blocks, width_scale, units, units, (gate_tail,)
        )

    if shared:
        (their_blocks,) = gathered(their_tokens)
        new_up = lax.cond(
            is_early,
            up_from_raw,
            lambda _: mean_rows(up_new, their_up, units, None, 0, units),
            their_blocks,
        )
        new_down = lax.cond(
            is_early,
            lambda after: mean_rows(first, their_first, units, None, 0, units, (after,)),
            lambda after: mean_rows(down_new, their_down, units, None, 0, units, (after,)),
            new_up,
        )
    else:
        their_blocks, new_down = gathered_beside(their_tokens, first, their_first)
        new_up = up_from_raw(their_blocks)
    new_gate = mean_rows(gate_head, their_gate_head, cut, None, 0, units, (new_up, new_down))
    new_gate = mean_rows(gate_tail, their_gate_tail, BLOCK, new_gate, cut, units)
    return layer_out, grad_in, new_gate, new_up, new_down


def shards(activations, out_grad, gate_weight, up_weight, down_weight, step_index):
    levels = lax.axis_size("rep").bit_length() - 1
    branches = [partial(whole_step, 1 << level) for level in range(levels)]
    layer_out, grad_in, gate, up, down = lax.switch(
        step_index[0] % levels,
        branches,
        (step_index[0] // levels) % 2 == 0,
        activations[0],
        out_grad[0],
        gate_weight[0].T,
        up_weight[0].T,
        down_weight[0],
    )
    return layer_out[None], grad_in[None], gate.T[None], up.T[None], down[None]


def solution(mesh):
    in_specs = (
        P("rep", "tp", None),
        P("rep", "tp", None),
        P("rep", None, "tp"),
        P("rep", None, "tp"),
        P("rep", "tp", None),
        P(),
    )
    out_specs = (
        P("rep", "tp", None),
        P("rep", "tp", None),
        P("rep", None, "tp"),
        P("rep", None, "tp"),
        P("rep", "tp", None),
    )
    return jax.shard_map(shards, mesh=mesh, in_specs=in_specs, out_specs=out_specs, check_vma=False)
```

```python
from functools import partial
import math

import jax
import jax.numpy as jnp
from jax import lax
from jax.experimental import pallas as pl
from jax.experimental.pallas import tpu as pltpu
from jax.sharding import PartitionSpec as P

D = 2560
FF = 6912
BLOCK = 144


learn_rate = 0.8
width_scale = 1.0 / math.sqrt(D)
hidden_scale = 1.0 / math.sqrt(FF)

ANY = pl.BlockSpec(memory_space=pl.ANY)
PARAMS = pltpu.CompilerParams(vmem_limit_bytes=40 * 1024 * 1024)


def ring_of(devices):
    y_size = 1 << ((devices.bit_length() - 1) // 2)
    z_size = devices // y_size
    walk = [(z, 0) for z in range(z_size)]
    for z in reversed(range(z_size)):
        ys = list(range(1, y_size))
        walk += [(z, y) for y in (ys if (z_size - 1 - z) % 2 == 0 else reversed(ys))]
    return [z * y_size + y for z, y in walk]


def mm(a, b, dims):
    return lax.dot_general(a, b, (dims, ((), ())), preferred_element_type=jnp.float32)


def cost(matmuls, rows, blocks_moved):
    return pl.CostEstimate(
        flops=2 * matmuls * rows * 256 * D, bytes_accessed=blocks_moved * rows * D * 2, transcendentals=0
    )


def rows_spec(first=0, width=D, block=BLOCK):
    return pl.BlockSpec((block, width), lambda i: (i + first, 0))


def block_of(units, most):
    return max(size for size in range(BLOCK, most + 1, BLOCK) if units % size == 0)


def whole_spec(x):
    return pl.BlockSpec(x.shape, lambda i: (0,) * x.ndim)


def forward(token_blocks, grad_blocks, gate_w, up_w, down_w):
    units, devices = gate_w.shape[0], len(token_blocks)
    part = token_blocks[0].shape[0]
    count = devices * part
    block = block_of(units, 288)

    def body(*refs):
        gate_ref, up_ref, down_ref = refs[2 * devices : 2 * devices + 3]
        tokens_ref, grads_ref, hidden_ref, d_gate_ref, d_up_ref, turned, turned_grads = refs[-7:]

        @pl.when(pl.program_id(0) == 0)
        def _():
            for at in range(devices):
                tokens_ref[pl.ds(at * part, part)] = refs[at][...]
                grads_ref[pl.ds(at * part, part)] = refs[devices + at][...]
            turned[...] = tokens_ref[...].T
            turned_grads[...] = grads_ref[...].T

        gate_pre = mm(gate_ref[...], turned[...], ((1,), (0,))) * width_scale
        up_pre = mm(up_ref[...], turned[...], ((1,), (0,))) * width_scale
        d_hidden = mm(down_ref[...], turned_grads[...], ((1,), (0,))) * hidden_scale
        sigmoid_gate = jax.nn.sigmoid(gate_pre)
        activated = gate_pre * sigmoid_gate
        slope = sigmoid_gate * (1.0 + gate_pre * (1.0 - sigmoid_gate))
        hidden_ref[...] = (activated * up_pre).astype(jnp.bfloat16)
        d_gate_ref[...] = (d_hidden * up_pre * slope).astype(jnp.bfloat16)
        d_up_ref[...] = (d_hidden * activated).astype(jnp.bfloat16)

    whole = jax.ShapeDtypeStruct((count, D), jnp.bfloat16)
    out = jax.ShapeDtypeStruct((units, count), jnp.bfloat16)
    pieces = [*token_blocks, *grad_blocks]
    return pl.pallas_call(
        body,
        grid=(units // block,),
        in_specs=[whole_spec(piece) for piece in pieces] + [rows_spec(block=block)] * 3,
        out_specs=[whole_spec(whole)] * 2 + [rows_spec(0, count, block)] * 3,
        out_shape=[whole] * 2 + [out] * 3,
        scratch_shapes=[pltpu.VMEM((D, count), jnp.bfloat16)] * 2,
        compiler_params=PARAMS,
        cost_estimate=cost(3, units, 3),
        name="forward",
    )(*pieces, gate_w, up_w, down_w)


def stepped(weight, left, right, scale):
    return weight.astype(jnp.float32) - learn_rate * (mm(left, right, ((1,), (0,))) * scale)


def step_rows(weight, left, right, scale, first, rows, after=(), beside=None, base=None, costs=None):
    at = first // BLOCK
    count = left.shape[1]
    ins = (weight, left, right) if beside is None else (weight, left, right, beside)
    others = after if base is None else (base, *after)
    shape = (rows, D) if base is None else base.shape

    def body(weight_ref, left_ref, right_ref, *rest):
        out_ref = rest[-1]
        out_ref[:, :D] = stepped(weight_ref[...], left_ref[...], right_ref[...], scale).astype(jnp.bfloat16)
        if beside is not None:
            out_ref[:, D:] = rest[0][...]

    return pl.pallas_call(
        body,
        grid=(rows // BLOCK,),
        in_specs=[rows_spec(at), rows_spec(at, count), whole_spec(right)]
        + ([] if beside is None else [rows_spec(0, count)])
        + [ANY] * len(others),
        out_specs=rows_spec(0, shape[1]),
        out_shape=jax.ShapeDtypeStruct(shape, jnp.bfloat16),
        input_output_aliases={} if base is None else {len(ins): 0},
        compiler_params=PARAMS,
        cost_estimate=costs or cost(1, rows, 2),
        name="step_rows",
    )(*ins, *others)


def rows_below(x, above, beside):
    part = x.shape[0]

    def body(x_ref, out_ref):
        out_ref[...] = x_ref[...]

    return pl.pallas_call(
        body,
        grid=(1,),
        in_specs=[whole_spec(x)],
        out_specs=pl.BlockSpec((part, D), lambda i: (above // part, 0)),
        out_shape=jax.ShapeDtypeStruct((above + part, D + beside), x.dtype),
        compiler_params=PARAMS,
        cost_estimate=cost(0, part, 2),
        name="rows_below",
    )(x)


def rows_of(x, first, rows, block):
    at = first // block

    def body(x_ref, out_ref):
        out_ref[...] = x_ref[...]

    return pl.pallas_call(
        body,
        grid=(rows // block,),
        in_specs=[rows_spec(at, block=block)],
        out_specs=rows_spec(block=block),
        out_shape=jax.ShapeDtypeStruct((rows, D), x.dtype),
        compiler_params=PARAMS,
        cost_estimate=cost(0, rows, 2),
        name="rows_of",
    )(x)


def halved_sum(mine, theirs):
    return ((mine.astype(jnp.float32) + theirs.astype(jnp.float32)) * 0.5).astype(jnp.bfloat16)


def into_rows(body, ins, in_specs, base, first, rows, units, costs, name, after, scratch=()):
    others = after if base is None else (base, *after)

    def with_others(*refs):
        body(*refs[: len(ins)], *refs[len(ins) + len(others) :])
    return pl.pallas_call(
        with_others,
        grid=(rows // BLOCK,),
        in_specs=in_specs + [ANY] * len(others),
        out_specs=rows_spec(first // BLOCK),
        out_shape=jax.ShapeDtypeStruct((units, D), jnp.bfloat16),
        input_output_aliases={} if base is None else {len(ins): 0},
        scratch_shapes=scratch,
        compiler_params=PARAMS,
        cost_estimate=costs,
        name=name,
    )(*ins, *others)


def mean_rows(mine, theirs, rows, base, first, units, after=(), source=0):
    def body(mine_ref, theirs_ref, out_ref):
        @pl.loop(0, BLOCK // 48)
        def _(strip):
            at = pl.ds(pl.multiple_of(strip * 48, 48), 48)
            out_ref[at] = halved_sum(mine_ref[at], theirs_ref[at])

    specs = [rows_spec(source // BLOCK)] * 2
    return into_rows(
        body, (mine, theirs), specs, base, first, rows, units, cost(0, rows, 3), "mean_rows", after
    )


def mean_of_steps(mine, left, right, theirs, their_left, their_blocks, scale, rows, units, after):
    part = their_blocks[0].shape[0]

    def body(mine_ref, left_ref, right_ref, theirs_ref, their_left_ref, *rest):
        out_ref, their_right = rest[-2:]

        @pl.when(pl.program_id(0) == 0)
        def _():
            for at in range(len(their_blocks)):
                their_right[pl.ds(at * part, part)] = rest[at][...]

        own = stepped(mine_ref[...], left_ref[...], right_ref[...], scale).astype(jnp.bfloat16)
        other = stepped(theirs_ref[...], their_left_ref[...], their_right[...], scale).astype(jnp.bfloat16)
        out_ref[...] = halved_sum(own, other)

    count = left.shape[1]
    return into_rows(
        body,
        (mine, left, right, theirs, their_left, *their_blocks),
        [rows_spec(), rows_spec(0, count), whole_spec(right)]
        + [rows_spec(), pl.BlockSpec((BLOCK, count), lambda i: (i, D // count))]
        + [whole_spec(block) for block in their_blocks],
        None,
        0,
        rows,
        units,
        cost(2, rows, 3),
        "mean_of_steps",
        after,
        [pltpu.VMEM((count, D), jnp.bfloat16)],
    )


def partial_sums(hidden, d_gate, d_up, gate_w, up_w, down_w, after):
    units, count = hidden.shape
    block = block_of(units, 432)
    steps = units // block

    def body(hidden_ref, d_gate_ref, d_up_ref, gate_ref, up_ref, down_ref, *rest):
        layer_ref, grad_ref = rest[-2:]

        @pl.when(pl.program_id(0) == 0)
        def _():
            layer_ref[...] = jnp.zeros_like(layer_ref)
            grad_ref[...] = jnp.zeros_like(grad_ref)

        layer_ref[...] += mm(hidden_ref[...], down_ref[...], ((0,), (0,))) * hidden_scale
        grad_sum = mm(d_gate_ref[...], gate_ref[...], ((0,), (0,))) + mm(d_up_ref[...], up_ref[...], ((0,), (0,)))
        grad_ref[...] += grad_sum * width_scale

    out = jax.ShapeDtypeStruct((count, D), jnp.float32)
    return pl.pallas_call(
        body,
        grid=(steps,),
        in_specs=[rows_spec(0, count, block)] * 3 + [rows_spec(block=block)] * 3 + [ANY] * len(after),
        out_specs=[whole_spec(out)] * 2,
        out_shape=[out] * 2,
        compiler_params=PARAMS,
        cost_estimate=cost(3, units, 3),
        name="partial_sums",
    )(hidden, d_gate, d_up, gate_w, up_w, down_w, *after)


def whole_step(distance, turned, tokens_local, grads_local, gate_w, up_w, down_w):
    units = gate_w.shape[0]
    devices = lax.axis_size("tp")
    ring = ring_of(devices)

    def send(x, parity=None):
        replicas = lax.axis_size("rep")
        senders = [i for i in range(replicas) if parity is None or i % 2 == parity]
        return lax.ppermute(x, "rep", [(i, (i + distance) % replicas) for i in senders])

    def along(x, by):
        return lax.ppermute(x, "tp", [(ring[i], ring[(i + by) % devices]) for i in range(devices)])

    shared = distance % 2 == 0
    early = 0 if shared else None
    is_early = lax.axis_index("rep") % 2 == 0
    theirs_raw = send(up_w, early)

    half = devices // 2

    def gather(turn, locals_):
        held = [[x] * devices for x in locals_]
        for hop in range(1, half + 1):
            for at, blocks_held in enumerate(held):
                last_way = turn if at % 2 == 0 else -turn
                for way in (turn, -turn):
                    if hop < half or way == last_way:
                        blocks_held[-way * hop] = along(blocks_held[-way * (hop - 1)], way)
        return [blocks_held[1:] for blocks_held in held]

    def gathered(*locals_):
        if devices > 8:
            return [list(lax.all_gather(x, "tp")) for x in locals_]
        others = lax.cond(turned, partial(gather, 1), partial(gather, -1), locals_)
        return [[x, *rest] for x, rest in zip(locals_, others)]

    def gathered_beside(x, mine, theirs):
        if devices > 8:
            return list(lax.all_gather(x, "tp")), mean_rows(mine, theirs, units, None, 0, units)

        def branch(turn, x, mine, theirs):
            held, mean, done = [x] * devices, None, 0
            for hop in range(1, half + 1):
                for way in (turn, -turn):
                    if hop < half or way == turn:
                        held[-way * hop] = along(held[-way * (hop - 1)], way)
                if hop < half:
                    upto = units // BLOCK * hop // (half - 1) * BLOCK
                    mean = mean_rows(mine, theirs, upto - done, mean, done, units, (), done)
                    held[-turn * hop], mean = lax.optimization_barrier((held[-turn * hop], mean))
                    done = upto
            return held[1:], mean

        others, mean = lax.cond(turned, partial(branch, 1), partial(branch, -1), x, mine, theirs)
        return [x, *others], mean

    def summed(terms):
        if devices > 8:
            totals = [lax.psum_scatter(term, "tp", scatter_dimension=0, tiled=True) for term in terms]
            return [total.astype(jnp.bfloat16) for total in totals]
        return lax.cond(turned, partial(sums, 1), partial(sums, -1), terms)

    def sums(turn, terms):
        part = terms[0].shape[0] // devices
        block_at = lambda term, offset: term[(offset % devices) * part : (offset % devices + 1) * part]
        ways = [(at, way, half - (0 if (way == turn) == (at == 0) else 1)) for at in (0, 1) for way in (turn, -turn)]
        moving = {}
        for hop in range(1, half + 1):
            for at, way, hops in ways:
                if hop <= hops:
                    block = block_at(terms[at], way * (hops + 1 - hop))
                    if hop > 1:
                        block = block + moving[at, way].astype(jnp.float32)
                    moving[at, way] = along(block.astype(jnp.bfloat16), way)
        totals = []
        for at, term in enumerate(terms):
            total = block_at(term, 0)
            for way in (turn, -turn):
                total = total + moving[at, way].astype(jnp.float32)
            totals.append(total.astype(jnp.bfloat16))
        return totals

    token_blocks, grad_blocks = gathered(tokens_local, grads_local)
    tokens, grads, hidden, d_gate, d_up = forward(token_blocks, grad_blocks, gate_w, up_w, down_w)
    cut = units - BLOCK
    down_step = partial(step_rows, down_w, hidden, grads, hidden_scale, 0, units)
    head_step = partial(step_rows, gate_w, d_gate, tokens, width_scale, 0, cut)
    long_step = cost(20, units, 40)
    first = down_step(beside=d_up, base=rows_below(tokens_local, units, d_up.shape[1]))
    their_first = send(first, early)
    if shared:
        second = up_new = step_rows(up_w, d_up, tokens, width_scale, 0, units, (theirs_raw,), costs=long_step)
        their_up = send(up_new, 1)
    else:
        second = gate_head = head_step((theirs_raw,), costs=long_step)
        their_gate_head = send(gate_head)
    terms = partial_sums(hidden, d_gate, d_up, gate_w, up_w, down_w, (second,))
    layer_out, grad_in = summed(terms)
    if shared:
        down_new = down_step((layer_out,))
        their_down = send(down_new, 1)
        gate_head = head_step((their_first, down_new))
        their_gate_head = send(gate_head)
    landed = their_up if shared else their_first
    gate_tail = step_rows(gate_w, d_gate, tokens, width_scale, cut, BLOCK, (landed, gate_head, layer_out))
    their_gate_tail = send(gate_tail)

    their_tokens = rows_of(their_first, units, tokens_local.shape[0], 16)
    their_tokens, gate_tail = lax.optimization_barrier((their_tokens, gate_tail))

    def up_from_raw(their_blocks):
        return mean_of_steps(
            up_w, d_up, tokens, theirs_raw, their_first, their_blocks, width_scale, units, units, (gate_tail,)
        )

    if shared:
        (their_blocks,) = gathered(their_tokens)
        new_up = lax.cond(
            is_early,
            up_from_raw,
            lambda _: mean_rows(up_new, their_up, units, None, 0, units),
            their_blocks,
        )
        new_down = lax.cond(
            is_early,
            lambda after: mean_rows(first, their_first, units, None, 0, units, (after,)),
            lambda after: mean_rows(down_new, their_down, units, None, 0, units, (after,)),
            new_up,
        )
    else:
        their_blocks, new_down = gathered_beside(their_tokens, first, their_first)
        new_up = up_from_raw(their_blocks)
    new_gate = mean_rows(gate_head, their_gate_head, cut, None, 0, units, (new_up, new_down))
    new_gate = mean_rows(gate_tail, their_gate_tail, BLOCK, new_gate, cut, units)
    return layer_out, grad_in, new_gate, new_up, new_down


def shards(activations, out_grad, gate_weight, up_weight, down_weight, step_index):
    levels = lax.axis_size("rep").bit_length() - 1
    branches = [partial(whole_step, 1 << level) for level in range(levels)]
    layer_out, grad_in, gate, up, down = lax.switch(
        step_index[0] % levels,
        branches,
        (step_index[0] // levels) % 2 == 0,
        activations[0],
        out_grad[0],
        gate_weight[0].T,
        up_weight[0].T,
        down_weight[0],
    )
    return layer_out[None], grad_in[None], gate.T[None], up.T[None], down[None]


def solution(mesh):
    in_specs = (
        P("rep", "tp", None),
        P("rep", "tp", None),
        P("rep", None, "tp"),
        P("rep", None, "tp"),
        P("rep", "tp", None),
        P(),
    )
    out_specs = (
        P("rep", "tp", None),
        P("rep", "tp", None),
        P("rep", None, "tp"),
        P("rep", None, "tp"),
        P("rep", "tp", None),
    )
    return jax.shard_map(shards, mesh=mesh, in_specs=in_specs, out_specs=out_specs, check_vma=False)
```

```python
from functools import partial
import math

import jax
import jax.numpy as jnp
from jax import lax
from jax.experimental import pallas as pl
from jax.experimental.pallas import tpu as pltpu
from jax.sharding import PartitionSpec as P

D = 2560
FF = 6912
BLOCK = 144


learn_rate = 0.8
width_scale = 1.0 / math.sqrt(D)
hidden_scale = 1.0 / math.sqrt(FF)

ANY = pl.BlockSpec(memory_space=pl.ANY)
PARAMS = pltpu.CompilerParams(vmem_limit_bytes=40 * 1024 * 1024)


def ring_of(devices):
    y_size = 1 << ((devices.bit_length() - 1) // 2)
    z_size = devices // y_size
    walk = [(z, 0) for z in range(z_size)]
    for z in reversed(range(z_size)):
        ys = list(range(1, y_size))
        walk += [(z, y) for y in (ys if (z_size - 1 - z) % 2 == 0 else reversed(ys))]
    return [z * y_size + y for z, y in walk]


def mm(a, b, dims):
    return lax.dot_general(a, b, (dims, ((), ())), preferred_element_type=jnp.float32)


def cost(matmuls, rows, blocks_moved):
    return pl.CostEstimate(
        flops=2 * matmuls * rows * 256 * D, bytes_accessed=blocks_moved * rows * D * 2, transcendentals=0
    )


def rows_spec(first=0, width=D, block=BLOCK):
    return pl.BlockSpec((block, width), lambda i: (i + first, 0))


def block_of(units, most):
    return max(size for size in range(BLOCK, most + 1, BLOCK) if units % size == 0)


def whole_spec(x):
    return pl.BlockSpec(x.shape, lambda i: (0,) * x.ndim)


def forward(token_blocks, grad_blocks, gate_w, up_w, down_w):
    units, devices = gate_w.shape[0], len(token_blocks)
    part = token_blocks[0].shape[0]
    count = devices * part
    block = block_of(units, 288)

    def body(*refs):
        gate_ref, up_ref, down_ref = refs[2 * devices : 2 * devices + 3]
        tokens_ref, grads_ref, hidden_ref, d_gate_ref, d_up_ref, turned, turned_grads = refs[-7:]

        @pl.when(pl.program_id(0) == 0)
        def _():
            for at in range(devices):
                tokens_ref[pl.ds(at * part, part)] = refs[at][...]
                grads_ref[pl.ds(at * part, part)] = refs[devices + at][...]
            turned[...] = tokens_ref[...].T
            turned_grads[...] = grads_ref[...].T

        gate_pre = mm(gate_ref[...], turned[...], ((1,), (0,))) * width_scale
        up_pre = mm(up_ref[...], turned[...], ((1,), (0,))) * width_scale
        d_hidden = mm(down_ref[...], turned_grads[...], ((1,), (0,))) * hidden_scale
        sigmoid_gate = jax.nn.sigmoid(gate_pre)
        activated = gate_pre * sigmoid_gate
        slope = sigmoid_gate * (1.0 + gate_pre * (1.0 - sigmoid_gate))
        hidden_ref[...] = (activated * up_pre).astype(jnp.bfloat16)
        d_gate_ref[...] = (d_hidden * up_pre * slope).astype(jnp.bfloat16)
        d_up_ref[...] = (d_hidden * activated).astype(jnp.bfloat16)

    whole = jax.ShapeDtypeStruct((count, D), jnp.bfloat16)
    out = jax.ShapeDtypeStruct((units, count), jnp.bfloat16)
    pieces = [*token_blocks, *grad_blocks]
    return pl.pallas_call(
        body,
        grid=(units // block,),
        in_specs=[whole_spec(piece) for piece in pieces] + [rows_spec(block=block)] * 3,
        out_specs=[whole_spec(whole)] * 2 + [rows_spec(0, count, block)] * 3,
        out_shape=[whole] * 2 + [out] * 3,
        scratch_shapes=[pltpu.VMEM((D, count), jnp.bfloat16)] * 2,
        compiler_params=PARAMS,
        cost_estimate=cost(3, units, 3),
        name="forward",
    )(*pieces, gate_w, up_w, down_w)


def stepped(weight, left, right, scale):
    return weight.astype(jnp.float32) - learn_rate * (mm(left, right, ((1,), (0,))) * scale)


def step_rows(weight, left, right, scale, first, rows, after=(), beside=None, base=None, costs=None):
    at = first // BLOCK
    count = left.shape[1]
    ins = (weight, left, right) if beside is None else (weight, left, right, beside)
    others = after if base is None else (base, *after)
    shape = (rows, D) if base is None else base.shape

    def body(weight_ref, left_ref, right_ref, *rest):
        out_ref = rest[-1]
        out_ref[:, :D] = stepped(weight_ref[...], left_ref[...], right_ref[...], scale).astype(jnp.bfloat16)
        if beside is not None:
            out_ref[:, D:] = rest[0][...]

    return pl.pallas_call(
        body,
        grid=(rows // BLOCK,),
        in_specs=[rows_spec(at), rows_spec(at, count), whole_spec(right)]
        + ([] if beside is None else [rows_spec(0, count)])
        + [ANY] * len(others),
        out_specs=rows_spec(0, shape[1]),
        out_shape=jax.ShapeDtypeStruct(shape, jnp.bfloat16),
        input_output_aliases={} if base is None else {len(ins): 0},
        compiler_params=PARAMS,
        cost_estimate=costs or cost(1, rows, 2),
        name="step_rows",
    )(*ins, *others)


def rows_below(x, above, beside):
    part = x.shape[0]

    def body(x_ref, out_ref):
        out_ref[...] = x_ref[...]

    return pl.pallas_call(
        body,
        grid=(1,),
        in_specs=[whole_spec(x)],
        out_specs=pl.BlockSpec((part, D), lambda i: (above // part, 0)),
        out_shape=jax.ShapeDtypeStruct((above + part, D + beside), x.dtype),
        compiler_params=PARAMS,
        cost_estimate=cost(0, part, 2),
        name="rows_below",
    )(x)


def rows_of(x, first, rows, block):
    at = first // block

    def body(x_ref, out_ref):
        out_ref[...] = x_ref[...]

    return pl.pallas_call(
        body,
        grid=(rows // block,),
        in_specs=[rows_spec(at, block=block)],
        out_specs=rows_spec(block=block),
        out_shape=jax.ShapeDtypeStruct((rows, D), x.dtype),
        compiler_params=PARAMS,
        cost_estimate=cost(0, rows, 2),
        name="rows_of",
    )(x)


def halved_sum(mine, theirs):
    return ((mine.astype(jnp.float32) + theirs.astype(jnp.float32)) * 0.5).astype(jnp.bfloat16)


def into_rows(body, ins, in_specs, base, first, rows, units, costs, name, after, scratch=()):
    others = after if base is None else (base, *after)

    def with_others(*refs):
        body(*refs[: len(ins)], *refs[len(ins) + len(others) :])
    return pl.pallas_call(
        with_others,
        grid=(rows // BLOCK,),
        in_specs=in_specs + [ANY] * len(others),
        out_specs=rows_spec(first // BLOCK),
        out_shape=jax.ShapeDtypeStruct((units, D), jnp.bfloat16),
        input_output_aliases={} if base is None else {len(ins): 0},
        scratch_shapes=scratch,
        compiler_params=PARAMS,
        cost_estimate=costs,
        name=name,
    )(*ins, *others)


def mean_rows(mine, theirs, rows, base, first, units, after=(), source=0):
    def body(mine_ref, theirs_ref, out_ref):
        @pl.loop(0, BLOCK // 48)
        def _(strip):
            at = pl.ds(pl.multiple_of(strip * 48, 48), 48)
            out_ref[at] = halved_sum(mine_ref[at], theirs_ref[at])

    specs = [rows_spec(source // BLOCK)] * 2
    return into_rows(
        body, (mine, theirs), specs, base, first, rows, units, cost(0, rows, 3), "mean_rows", after
    )


def mean_last(mine, theirs, base, first):
    rows = mine.shape[0]

    def body(mine_ref, theirs_ref, base_ref, out_ref, mean, sem):
        @pl.loop(0, rows // 48)
        def _(strip):
            at = pl.ds(pl.multiple_of(strip * 48, 48), 48)
            mean[at] = halved_sum(mine_ref[at], theirs_ref[at])

        copy = pltpu.make_async_copy(mean, out_ref.at[pl.ds(first, rows)], sem)
        copy.start()
        copy.wait()

    return pl.pallas_call(
        body,
        in_specs=[pl.BlockSpec(memory_space=pltpu.VMEM)] * 2 + [ANY],
        out_specs=ANY,
        out_shape=jax.ShapeDtypeStruct(base.shape, base.dtype),
        scratch_shapes=[pltpu.VMEM((rows, D), base.dtype), pltpu.SemaphoreType.DMA],
        input_output_aliases={2: 0},
        compiler_params=PARAMS,
        cost_estimate=cost(0, rows, 3),
        name="mean_last",
    )(mine, theirs, base)


def mean_of_steps(mine, left, right, theirs, their_left, their_blocks, scale, rows, units, after):
    part = their_blocks[0].shape[0]

    def body(mine_ref, left_ref, right_ref, theirs_ref, their_left_ref, *rest):
        out_ref, their_right = rest[-2:]

        @pl.when(pl.program_id(0) == 0)
        def _():
            for at in range(len(their_blocks)):
                their_right[pl.ds(at * part, part)] = rest[at][...]

        own = stepped(mine_ref[...], left_ref[...], right_ref[...], scale).astype(jnp.bfloat16)
        other = stepped(theirs_ref[...], their_left_ref[...], their_right[...], scale).astype(jnp.bfloat16)
        out_ref[...] = halved_sum(own, other)

    count = left.shape[1]
    return into_rows(
        body,
        (mine, left, right, theirs, their_left, *their_blocks),
        [rows_spec(), rows_spec(0, count), whole_spec(right)]
        + [rows_spec(), pl.BlockSpec((BLOCK, count), lambda i: (i, D // count))]
        + [whole_spec(block) for block in their_blocks],
        None,
        0,
        rows,
        units,
        cost(2, rows, 3),
        "mean_of_steps",
        after,
        [pltpu.VMEM((count, D), jnp.bfloat16)],
    )


def partial_sums(hidden, d_gate, d_up, gate_w, up_w, down_w, after):
    units, count = hidden.shape
    block = block_of(units, 432)
    steps = units // block

    def body(hidden_ref, d_gate_ref, d_up_ref, gate_ref, up_ref, down_ref, *rest):
        layer_ref, grad_ref = rest[-2:]

        @pl.when(pl.program_id(0) == 0)
        def _():
            layer_ref[...] = jnp.zeros_like(layer_ref)
            grad_ref[...] = jnp.zeros_like(grad_ref)

        layer_ref[...] += mm(hidden_ref[...], down_ref[...], ((0,), (0,))) * hidden_scale
        grad_sum = mm(d_gate_ref[...], gate_ref[...], ((0,), (0,))) + mm(d_up_ref[...], up_ref[...], ((0,), (0,)))
        grad_ref[...] += grad_sum * width_scale

    out = jax.ShapeDtypeStruct((count, D), jnp.float32)
    return pl.pallas_call(
        body,
        grid=(steps,),
        in_specs=[rows_spec(0, count, block)] * 3 + [rows_spec(block=block)] * 3 + [ANY] * len(after),
        out_specs=[whole_spec(out)] * 2,
        out_shape=[out] * 2,
        compiler_params=PARAMS,
        cost_estimate=cost(3, units, 3),
        name="partial_sums",
    )(hidden, d_gate, d_up, gate_w, up_w, down_w, *after)


def whole_step(distance, turned, tokens_local, grads_local, gate_w, up_w, down_w):
    units = gate_w.shape[0]
    devices = lax.axis_size("tp")
    ring = ring_of(devices)

    def send(x, parity=None):
        replicas = lax.axis_size("rep")
        senders = [i for i in range(replicas) if parity is None or i % 2 == parity]
        return lax.ppermute(x, "rep", [(i, (i + distance) % replicas) for i in senders])

    def along(x, by):
        return lax.ppermute(x, "tp", [(ring[i], ring[(i + by) % devices]) for i in range(devices)])

    shared = distance % 2 == 0
    early = 0 if shared else None
    is_early = lax.axis_index("rep") % 2 == 0
    theirs_raw = send(up_w, early)

    half = devices // 2

    def gather(turn, locals_):
        held = [[x] * devices for x in locals_]
        for hop in range(1, half + 1):
            for at, blocks_held in enumerate(held):
                last_way = turn if at % 2 == 0 else -turn
                for way in (turn, -turn):
                    if hop < half or way == last_way:
                        blocks_held[-way * hop] = along(blocks_held[-way * (hop - 1)], way)
        return [blocks_held[1:] for blocks_held in held]

    def gathered(*locals_):
        if devices > 8:
            return [list(lax.all_gather(x, "tp")) for x in locals_]
        others = lax.cond(turned, partial(gather, 1), partial(gather, -1), locals_)
        return [[x, *rest] for x, rest in zip(locals_, others)]

    def gathered_beside(x, mine, theirs):
        if devices > 8:
            return list(lax.all_gather(x, "tp")), mean_rows(mine, theirs, units, None, 0, units)

        def branch(turn, x, mine, theirs):
            held, mean, done = [x] * devices, None, 0
            for hop in range(1, half + 1):
                for way in (turn, -turn):
                    if hop < half or way == turn:
                        held[-way * hop] = along(held[-way * (hop - 1)], way)
                if hop < half:
                    upto = units // BLOCK * hop // (half - 1) * BLOCK
                    mean = mean_rows(mine, theirs, upto - done, mean, done, units, (), done)
                    held[-turn * hop], mean = lax.optimization_barrier((held[-turn * hop], mean))
                    done = upto
            return held[1:], mean

        others, mean = lax.cond(turned, partial(branch, 1), partial(branch, -1), x, mine, theirs)
        return [x, *others], mean

    def summed(terms):
        if devices > 8:
            totals = [lax.psum_scatter(term, "tp", scatter_dimension=0, tiled=True) for term in terms]
            return [total.astype(jnp.bfloat16) for total in totals]
        return lax.cond(turned, partial(sums, 1), partial(sums, -1), terms)

    def sums(turn, terms):
        part = terms[0].shape[0] // devices
        block_at = lambda term, offset: term[(offset % devices) * part : (offset % devices + 1) * part]
        ways = [(at, way, half - (0 if (way == turn) == (at == 0) else 1)) for at in (0, 1) for way in (turn, -turn)]
        moving = {}
        for hop in range(1, half + 1):
            for at, way, hops in ways:
                if hop <= hops:
                    block = block_at(terms[at], way * (hops + 1 - hop))
                    if hop > 1:
                        block = block + moving[at, way].astype(jnp.float32)
                    moving[at, way] = along(block.astype(jnp.bfloat16), way)
        totals = []
        for at, term in enumerate(terms):
            total = block_at(term, 0)
            for way in (turn, -turn):
                total = total + moving[at, way].astype(jnp.float32)
            totals.append(total.astype(jnp.bfloat16))
        return totals

    token_blocks, grad_blocks = gathered(tokens_local, grads_local)
    tokens, grads, hidden, d_gate, d_up = forward(token_blocks, grad_blocks, gate_w, up_w, down_w)
    cut = units - BLOCK
    down_step = partial(step_rows, down_w, hidden, grads, hidden_scale, 0, units)
    head_step = partial(step_rows, gate_w, d_gate, tokens, width_scale, 0, cut)
    long_step = cost(20, units, 40)
    first = down_step(beside=d_up, base=rows_below(tokens_local, units, d_up.shape[1]))
    their_first = send(first, early)
    if shared:
        second = up_new = step_rows(up_w, d_up, tokens, width_scale, 0, units, (theirs_raw,), costs=long_step)
        their_up = send(up_new, 1)
    else:
        second = gate_head = head_step((theirs_raw,), costs=long_step)
        their_gate_head = send(gate_head)
    terms = partial_sums(hidden, d_gate, d_up, gate_w, up_w, down_w, (second,))
    layer_out, grad_in = summed(terms)
    if shared:
        down_new = down_step((layer_out,))
        their_down = send(down_new, 1)
        gate_head = head_step((their_first, down_new))
        their_gate_head = send(gate_head)
    landed = their_up if shared else their_first
    gate_tail = step_rows(gate_w, d_gate, tokens, width_scale, cut, BLOCK, (landed, gate_head, layer_out))
    their_gate_tail = send(gate_tail)

    their_tokens = rows_of(their_first, units, tokens_local.shape[0], 16)
    their_tokens, gate_tail = lax.optimization_barrier((their_tokens, gate_tail))

    def up_from_raw(their_blocks):
        return mean_of_steps(
            up_w, d_up, tokens, theirs_raw, their_first, their_blocks, width_scale, units, units, (gate_tail,)
        )

    if shared:
        (their_blocks,) = gathered(their_tokens)
        new_up = lax.cond(
            is_early,
            up_from_raw,
            lambda _: mean_rows(up_new, their_up, units, None, 0, units),
            their_blocks,
        )
        new_down = lax.cond(
            is_early,
            lambda after: mean_rows(first, their_first, units, None, 0, units, (after,)),
            lambda after: mean_rows(down_new, their_down, units, None, 0, units, (after,)),
            new_up,
        )
    else:
        their_blocks, new_down = gathered_beside(their_tokens, first, their_first)
        new_up = up_from_raw(their_blocks)
    new_gate = mean_rows(gate_head, their_gate_head, cut, None, 0, units, (new_up, new_down))
    new_gate = mean_last(gate_tail, their_gate_tail, new_gate, cut)
    return layer_out, grad_in, new_gate, new_up, new_down


def shards(activations, out_grad, gate_weight, up_weight, down_weight, step_index):
    levels = lax.axis_size("rep").bit_length() - 1
    branches = [partial(whole_step, 1 << level) for level in range(levels)]
    layer_out, grad_in, gate, up, down = lax.switch(
        step_index[0] % levels,
        branches,
        (step_index[0] // levels) % 2 == 0,
        activations[0],
        out_grad[0],
        gate_weight[0].T,
        up_weight[0].T,
        down_weight[0],
    )
    return layer_out[None], grad_in[None], gate.T[None], up.T[None], down[None]


def solution(mesh):
    in_specs = (
        P("rep", "tp", None),
        P("rep", "tp", None),
        P("rep", None, "tp"),
        P("rep", None, "tp"),
        P("rep", "tp", None),
        P(),
    )
    out_specs = (
        P("rep", "tp", None),
        P("rep", "tp", None),
        P("rep", None, "tp"),
        P("rep", None, "tp"),
        P("rep", "tp", None),
    )
    return jax.shard_map(shards, mesh=mesh, in_specs=in_specs, out_specs=out_specs, check_vma=False)
```

```python
from functools import partial
import math

import jax
import jax.numpy as jnp
from jax import lax
from jax.experimental import pallas as pl
from jax.experimental.pallas import tpu as pltpu
from jax.sharding import PartitionSpec as P

D = 2560
FF = 6912
BLOCK = 144


learn_rate = 0.8
width_scale = 1.0 / math.sqrt(D)
hidden_scale = 1.0 / math.sqrt(FF)

ANY = pl.BlockSpec(memory_space=pl.ANY)
PARAMS = pltpu.CompilerParams(vmem_limit_bytes=40 * 1024 * 1024)


def ring_of(devices):
    y_size = 1 << ((devices.bit_length() - 1) // 2)
    z_size = devices // y_size
    walk = [(z, 0) for z in range(z_size)]
    for z in reversed(range(z_size)):
        ys = list(range(1, y_size))
        walk += [(z, y) for y in (ys if (z_size - 1 - z) % 2 == 0 else reversed(ys))]
    return [z * y_size + y for z, y in walk]


def mm(a, b, dims):
    return lax.dot_general(a, b, (dims, ((), ())), preferred_element_type=jnp.float32)


def cost(matmuls, rows, blocks_moved):
    return pl.CostEstimate(
        flops=2 * matmuls * rows * 256 * D, bytes_accessed=blocks_moved * rows * D * 2, transcendentals=0
    )


def rows_spec(first=0, width=D, block=BLOCK):
    return pl.BlockSpec((block, width), lambda i: (i + first, 0))


def block_of(units, most):
    return max(size for size in range(BLOCK, most + 1, BLOCK) if units % size == 0)


def whole_spec(x):
    return pl.BlockSpec(x.shape, lambda i: (0,) * x.ndim)


def forward(token_blocks, grad_blocks, gate_w, up_w, down_w):
    units, devices = gate_w.shape[0], len(token_blocks)
    part = token_blocks[0].shape[0]
    count = devices * part
    block = block_of(units, 288)

    def body(*refs):
        gate_ref, up_ref, down_ref = refs[2 * devices : 2 * devices + 3]
        tokens_ref, grads_ref, hidden_ref, d_gate_ref, d_up_ref, turned, turned_grads = refs[-7:]

        @pl.when(pl.program_id(0) == 0)
        def _():
            for at in range(devices):
                tokens_ref[pl.ds(at * part, part)] = refs[at][...]
                grads_ref[pl.ds(at * part, part)] = refs[devices + at][...]
            turned[...] = tokens_ref[...].T
            turned_grads[...] = grads_ref[...].T

        gate_pre = mm(gate_ref[...], turned[...], ((1,), (0,))) * width_scale
        up_pre = mm(up_ref[...], turned[...], ((1,), (0,))) * width_scale
        d_hidden = mm(down_ref[...], turned_grads[...], ((1,), (0,))) * hidden_scale
        sigmoid_gate = jax.nn.sigmoid(gate_pre)
        activated = gate_pre * sigmoid_gate
        slope = sigmoid_gate * (1.0 + gate_pre * (1.0 - sigmoid_gate))
        hidden_ref[...] = (activated * up_pre).astype(jnp.bfloat16)
        d_gate_ref[...] = (d_hidden * up_pre * slope).astype(jnp.bfloat16)
        d_up_ref[...] = (d_hidden * activated).astype(jnp.bfloat16)

    whole = jax.ShapeDtypeStruct((count, D), jnp.bfloat16)
    out = jax.ShapeDtypeStruct((units, count), jnp.bfloat16)
    pieces = [*token_blocks, *grad_blocks]
    return pl.pallas_call(
        body,
        grid=(units // block,),
        in_specs=[whole_spec(piece) for piece in pieces] + [rows_spec(block=block)] * 3,
        out_specs=[whole_spec(whole)] * 2 + [rows_spec(0, count, block)] * 3,
        out_shape=[whole] * 2 + [out] * 3,
        scratch_shapes=[pltpu.VMEM((D, count), jnp.bfloat16)] * 2,
        compiler_params=PARAMS,
        cost_estimate=cost(3, units, 3),
        name="forward",
    )(*pieces, gate_w, up_w, down_w)


def stepped(weight, left, right, scale):
    return weight.astype(jnp.float32) - learn_rate * (mm(left, right, ((1,), (0,))) * scale)


def step_rows(weight, left, right, scale, first, rows, after=(), beside=None, base=None, costs=None):
    at = first // BLOCK
    count = left.shape[1]
    ins = (weight, left, right) if beside is None else (weight, left, right, beside)
    others = after if base is None else (base, *after)
    shape = (rows, D) if base is None else base.shape

    def body(weight_ref, left_ref, right_ref, *rest):
        out_ref = rest[-1]
        out_ref[:, :D] = stepped(weight_ref[...], left_ref[...], right_ref[...], scale).astype(jnp.bfloat16)
        if beside is not None:
            out_ref[:, D:] = rest[0][...]

    return pl.pallas_call(
        body,
        grid=(rows // BLOCK,),
        in_specs=[rows_spec(at), rows_spec(at, count), whole_spec(right)]
        + ([] if beside is None else [rows_spec(0, count)])
        + [ANY] * len(others),
        out_specs=rows_spec(0, shape[1]),
        out_shape=jax.ShapeDtypeStruct(shape, jnp.bfloat16),
        input_output_aliases={} if base is None else {len(ins): 0},
        compiler_params=PARAMS,
        cost_estimate=costs or cost(1, rows, 2),
        name="step_rows",
    )(*ins, *others)


def rows_below(x, above, beside):
    part = x.shape[0]

    def body(x_ref, out_ref):
        out_ref[...] = x_ref[...]

    return pl.pallas_call(
        body,
        grid=(1,),
        in_specs=[whole_spec(x)],
        out_specs=pl.BlockSpec((part, D), lambda i: (above // part, 0)),
        out_shape=jax.ShapeDtypeStruct((above + part, D + beside), x.dtype),
        compiler_params=PARAMS,
        cost_estimate=cost(0, part, 2),
        name="rows_below",
    )(x)


def rows_of(x, first, rows, block):
    at = first // block

    def body(x_ref, out_ref):
        out_ref[...] = x_ref[...]

    return pl.pallas_call(
        body,
        grid=(rows // block,),
        in_specs=[rows_spec(at, block=block)],
        out_specs=rows_spec(block=block),
        out_shape=jax.ShapeDtypeStruct((rows, D), x.dtype),
        compiler_params=PARAMS,
        cost_estimate=cost(0, rows, 2),
        name="rows_of",
    )(x)


def halved_sum(mine, theirs):
    return ((mine.astype(jnp.float32) + theirs.astype(jnp.float32)) * 0.5).astype(jnp.bfloat16)


def into_rows(body, ins, in_specs, base, first, rows, units, costs, name, after, scratch=()):
    others = after if base is None else (base, *after)

    def with_others(*refs):
        body(*refs[: len(ins)], *refs[len(ins) + len(others) :])
    return pl.pallas_call(
        with_others,
        grid=(rows // BLOCK,),
        in_specs=in_specs + [ANY] * len(others),
        out_specs=rows_spec(first // BLOCK),
        out_shape=jax.ShapeDtypeStruct((units, D), jnp.bfloat16),
        input_output_aliases={} if base is None else {len(ins): 0},
        scratch_shapes=scratch,
        compiler_params=PARAMS,
        cost_estimate=costs,
        name=name,
    )(*ins, *others)


def mean_rows(mine, theirs, rows, base, first, units, after=(), source=0):
    def body(mine_ref, theirs_ref, out_ref):
        @pl.loop(0, BLOCK // 48)
        def _(strip):
            at = pl.ds(pl.multiple_of(strip * 48, 48), 48)
            out_ref[at] = halved_sum(mine_ref[at], theirs_ref[at])

    specs = [rows_spec(source // BLOCK)] * 2
    return into_rows(
        body, (mine, theirs), specs, base, first, rows, units, cost(0, rows, 3), "mean_rows", after
    )


def mean_of_steps(mine, left, right, theirs, their_left, their_blocks, scale, rows, units, after):
    part = their_blocks[0].shape[0]

    def body(mine_ref, left_ref, right_ref, theirs_ref, their_left_ref, *rest):
        out_ref, their_right = rest[-2:]

        @pl.when(pl.program_id(0) == 0)
        def _():
            for at in range(len(their_blocks)):
                their_right[pl.ds(at * part, part)] = rest[at][...]

        own = stepped(mine_ref[...], left_ref[...], right_ref[...], scale).astype(jnp.bfloat16)
        other = stepped(theirs_ref[...], their_left_ref[...], their_right[...], scale).astype(jnp.bfloat16)
        out_ref[...] = halved_sum(own, other)

    count = left.shape[1]
    return into_rows(
        body,
        (mine, left, right, theirs, their_left, *their_blocks),
        [rows_spec(), rows_spec(0, count), whole_spec(right)]
        + [rows_spec(), pl.BlockSpec((BLOCK, count), lambda i: (i, D // count))]
        + [whole_spec(block) for block in their_blocks],
        None,
        0,
        rows,
        units,
        cost(2, rows, 3),
        "mean_of_steps",
        after,
        [pltpu.VMEM((count, D), jnp.bfloat16)],
    )


def partial_sums(hidden, d_gate, d_up, gate_w, up_w, down_w, after):
    units, count = hidden.shape
    block = block_of(units, 432)
    steps = units // block

    def body(hidden_ref, d_gate_ref, d_up_ref, gate_ref, up_ref, down_ref, *rest):
        layer_ref, grad_ref = rest[-2:]

        @pl.when(pl.program_id(0) == 0)
        def _():
            layer_ref[...] = jnp.zeros_like(layer_ref)
            grad_ref[...] = jnp.zeros_like(grad_ref)

        layer_ref[...] += mm(hidden_ref[...], down_ref[...], ((0,), (0,))) * hidden_scale
        grad_sum = mm(d_gate_ref[...], gate_ref[...], ((0,), (0,))) + mm(d_up_ref[...], up_ref[...], ((0,), (0,)))
        grad_ref[...] += grad_sum * width_scale

    out = jax.ShapeDtypeStruct((count, D), jnp.float32)
    return pl.pallas_call(
        body,
        grid=(steps,),
        in_specs=[rows_spec(0, count, block)] * 3 + [rows_spec(block=block)] * 3 + [ANY] * len(after),
        out_specs=[whole_spec(out)] * 2,
        out_shape=[out] * 2,
        compiler_params=PARAMS,
        cost_estimate=cost(3, units, 3),
        name="partial_sums",
    )(hidden, d_gate, d_up, gate_w, up_w, down_w, *after)


def whole_step(distance, turned, tokens_local, grads_local, gate_w, up_w, down_w):
    units = gate_w.shape[0]
    devices = lax.axis_size("tp")
    ring = ring_of(devices)

    def send(x, parity=None):
        replicas = lax.axis_size("rep")
        senders = [i for i in range(replicas) if parity is None or i % 2 == parity]
        return lax.ppermute(x, "rep", [(i, (i + distance) % replicas) for i in senders])

    def along(x, by):
        return lax.ppermute(x, "tp", [(ring[i], ring[(i + by) % devices]) for i in range(devices)])

    shared = distance % 2 == 0
    early = 0 if shared else None
    is_early = lax.axis_index("rep") % 2 == 0
    theirs_raw = send(up_w, early)

    half = devices // 2

    def gather(turn, locals_):
        held = [[x] * devices for x in locals_]
        for hop in range(1, half + 1):
            for at, blocks_held in enumerate(held):
                last_way = turn if at % 2 == 0 else -turn
                for way in (turn, -turn):
                    if hop < half or way == last_way:
                        blocks_held[-way * hop] = along(blocks_held[-way * (hop - 1)], way)
        return [blocks_held[1:] for blocks_held in held]

    def gathered(*locals_):
        if devices > 8:
            return [list(lax.all_gather(x, "tp")) for x in locals_]
        others = lax.cond(turned, partial(gather, 1), partial(gather, -1), locals_)
        return [[x, *rest] for x, rest in zip(locals_, others)]

    def gathered_beside(x, mine, theirs):
        if devices > 8:
            return list(lax.all_gather(x, "tp")), mean_rows(mine, theirs, units, None, 0, units)

        def branch(turn, x, mine, theirs):
            held, mean, done = [x] * devices, None, 0
            for hop in range(1, half + 1):
                for way in (turn, -turn):
                    if hop < half or way == turn:
                        held[-way * hop] = along(held[-way * (hop - 1)], way)
                if hop < half:
                    upto = units // BLOCK * hop // (half - 1) * BLOCK
                    mean = mean_rows(mine, theirs, upto - done, mean, done, units, (), done)
                    held[-turn * hop], mean = lax.optimization_barrier((held[-turn * hop], mean))
                    done = upto
            return held[1:], mean

        others, mean = lax.cond(turned, partial(branch, 1), partial(branch, -1), x, mine, theirs)
        return [x, *others], mean

    def summed(terms):
        if devices > 8:
            totals = [lax.psum_scatter(term, "tp", scatter_dimension=0, tiled=True) for term in terms]
            return [total.astype(jnp.bfloat16) for total in totals]
        return lax.cond(turned, partial(sums, 1), partial(sums, -1), terms)

    def sums(turn, terms):
        part = terms[0].shape[0] // devices
        block_at = lambda term, offset: term[(offset % devices) * part : (offset % devices + 1) * part]
        moving = {}
        for hop in range(1, half + 1):
            for way, lead in ((turn, 0), (-turn, 1)):
                offset = way * (half + 1 - hop)
                blocks = [block_at(terms[lead], offset)]
                if hop > 1:
                    came = moving[way].astype(jnp.float32)
                    blocks = [blocks[0] + came[:part], block_at(terms[1 - lead], offset)]
                    if hop > 2:
                        blocks[1] = blocks[1] + came[part:]
                moving[way] = along(jnp.concatenate(blocks).astype(jnp.bfloat16), way)
        totals = []
        for at, term in enumerate(terms):
            total = block_at(term, 0)
            for way, lead in ((turn, 0), (-turn, 1)):
                came = moving[way][:part] if lead == at else moving[way][part:]
                total = total + came.astype(jnp.float32)
            totals.append(total.astype(jnp.bfloat16))
        return totals

    token_blocks, grad_blocks = gathered(tokens_local, grads_local)
    tokens, grads, hidden, d_gate, d_up = forward(token_blocks, grad_blocks, gate_w, up_w, down_w)
    cut = units - BLOCK
    down_step = partial(step_rows, down_w, hidden, grads, hidden_scale, 0, units)
    head_step = partial(step_rows, gate_w, d_gate, tokens, width_scale, 0, cut)
    long_step = cost(20, units, 40)
    first = down_step(beside=d_up, base=rows_below(tokens_local, units, d_up.shape[1]))
    their_first = send(first, early)
    if shared:
        second = up_new = step_rows(up_w, d_up, tokens, width_scale, 0, units, (theirs_raw,), costs=long_step)
        their_up = send(up_new, 1)
    else:
        second = gate_head = head_step((theirs_raw,), costs=long_step)
        their_gate_head = send(gate_head)
    terms = partial_sums(hidden, d_gate, d_up, gate_w, up_w, down_w, (second,))
    layer_out, grad_in = summed(terms)
    if shared:
        down_new = down_step((layer_out,))
        their_down = send(down_new, 1)
        gate_head = head_step((their_first, down_new))
        their_gate_head = send(gate_head)
    landed = their_up if shared else their_first
    gate_tail = step_rows(gate_w, d_gate, tokens, width_scale, cut, BLOCK, (landed, gate_head, layer_out))
    their_gate_tail = send(gate_tail)

    their_tokens = rows_of(their_first, units, tokens_local.shape[0], 16)
    their_tokens, gate_tail = lax.optimization_barrier((their_tokens, gate_tail))

    def up_from_raw(their_blocks):
        return mean_of_steps(
            up_w, d_up, tokens, theirs_raw, their_first, their_blocks, width_scale, units, units, (gate_tail,)
        )

    if shared:
        (their_blocks,) = gathered(their_tokens)
        new_up = lax.cond(
            is_early,
            up_from_raw,
            lambda _: mean_rows(up_new, their_up, units, None, 0, units),
            their_blocks,
        )
        new_down = lax.cond(
            is_early,
            lambda after: mean_rows(first, their_first, units, None, 0, units, (after,)),
            lambda after: mean_rows(down_new, their_down, units, None, 0, units, (after,)),
            new_up,
        )
    else:
        their_blocks, new_down = gathered_beside(their_tokens, first, their_first)
        new_up = up_from_raw(their_blocks)
    new_gate = mean_rows(gate_head, their_gate_head, cut, None, 0, units, (new_up, new_down))
    new_gate = mean_rows(gate_tail, their_gate_tail, BLOCK, new_gate, cut, units)
    return layer_out, grad_in, new_gate, new_up, new_down


def shards(activations, out_grad, gate_weight, up_weight, down_weight, step_index):
    levels = lax.axis_size("rep").bit_length() - 1
    branches = [partial(whole_step, 1 << level) for level in range(levels)]
    layer_out, grad_in, gate, up, down = lax.switch(
        step_index[0] % levels,
        branches,
        (step_index[0] // levels) % 2 == 0,
        activations[0],
        out_grad[0],
        gate_weight[0].T,
        up_weight[0].T,
        down_weight[0],
    )
    return layer_out[None], grad_in[None], gate.T[None], up.T[None], down[None]


def solution(mesh):
    in_specs = (
        P("rep", "tp", None),
        P("rep", "tp", None),
        P("rep", None, "tp"),
        P("rep", None, "tp"),
        P("rep", "tp", None),
        P(),
    )
    out_specs = (
        P("rep", "tp", None),
        P("rep", "tp", None),
        P("rep", None, "tp"),
        P("rep", None, "tp"),
        P("rep", "tp", None),
    )
    return jax.shard_map(shards, mesh=mesh, in_specs=in_specs, out_specs=out_specs, check_vma=False)
```

```python
from functools import partial
import math

import jax
import jax.numpy as jnp
from jax import lax
from jax.experimental import pallas as pl
from jax.experimental.pallas import tpu as pltpu
from jax.sharding import PartitionSpec as P

D = 2560
FF = 6912
BLOCK = 144


learn_rate = 0.8
width_scale = 1.0 / math.sqrt(D)
hidden_scale = 1.0 / math.sqrt(FF)

ANY = pl.BlockSpec(memory_space=pl.ANY)
PARAMS = pltpu.CompilerParams(vmem_limit_bytes=40 * 1024 * 1024)


def ring_of(devices):
    y_size = 1 << ((devices.bit_length() - 1) // 2)
    z_size = devices // y_size
    walk = [(z, 0) for z in range(z_size)]
    for z in reversed(range(z_size)):
        ys = list(range(1, y_size))
        walk += [(z, y) for y in (ys if (z_size - 1 - z) % 2 == 0 else reversed(ys))]
    return [z * y_size + y for z, y in walk]


def mm(a, b, dims):
    return lax.dot_general(a, b, (dims, ((), ())), preferred_element_type=jnp.float32)


def cost(matmuls, rows, blocks_moved):
    return pl.CostEstimate(
        flops=2 * matmuls * rows * 256 * D, bytes_accessed=blocks_moved * rows * D * 2, transcendentals=0
    )


def rows_spec(first=0, width=D, block=BLOCK):
    return pl.BlockSpec((block, width), lambda i: (i + first, 0))


def block_of(units, most):
    return max(size for size in range(BLOCK, most + 1, BLOCK) if units % size == 0)


def whole_spec(x):
    return pl.BlockSpec(x.shape, lambda i: (0,) * x.ndim)


def forward(token_blocks, grad_blocks, gate_w, up_w, down_w):
    units, devices = gate_w.shape[0], len(token_blocks)
    part = token_blocks[0].shape[0]
    count = devices * part
    block = block_of(units, 288)

    def body(*refs):
        gate_ref, up_ref, down_ref = refs[2 * devices : 2 * devices + 3]
        tokens_ref, grads_ref, hidden_ref, d_gate_ref, d_up_ref, turned, turned_grads = refs[-7:]

        @pl.when(pl.program_id(0) == 0)
        def _():
            for at in range(devices):
                tokens_ref[pl.ds(at * part, part)] = refs[at][...]
                grads_ref[pl.ds(at * part, part)] = refs[devices + at][...]
            turned[...] = tokens_ref[...].T
            turned_grads[...] = grads_ref[...].T

        gate_pre = mm(gate_ref[...], turned[...], ((1,), (0,))) * width_scale
        up_pre = mm(up_ref[...], turned[...], ((1,), (0,))) * width_scale
        d_hidden = mm(down_ref[...], turned_grads[...], ((1,), (0,))) * hidden_scale
        sigmoid_gate = jax.nn.sigmoid(gate_pre)
        activated = gate_pre * sigmoid_gate
        slope = sigmoid_gate * (1.0 + gate_pre * (1.0 - sigmoid_gate))
        hidden_ref[...] = (activated * up_pre).astype(jnp.bfloat16)
        d_gate_ref[...] = (d_hidden * up_pre * slope).astype(jnp.bfloat16)
        d_up_ref[...] = (d_hidden * activated).astype(jnp.bfloat16)

    whole = jax.ShapeDtypeStruct((count, D), jnp.bfloat16)
    out = jax.ShapeDtypeStruct((units, count), jnp.bfloat16)
    pieces = [*token_blocks, *grad_blocks]
    return pl.pallas_call(
        body,
        grid=(units // block,),
        in_specs=[whole_spec(piece) for piece in pieces] + [rows_spec(block=block)] * 3,
        out_specs=[whole_spec(whole)] * 2 + [rows_spec(0, count, block)] * 3,
        out_shape=[whole] * 2 + [out] * 3,
        scratch_shapes=[pltpu.VMEM((D, count), jnp.bfloat16)] * 2,
        compiler_params=PARAMS,
        cost_estimate=cost(3, units, 3),
        name="forward",
    )(*pieces, gate_w, up_w, down_w)


def stepped(weight, left, right, scale):
    return weight.astype(jnp.float32) - learn_rate * (mm(left, right, ((1,), (0,))) * scale)


def step_rows(weight, left, right, scale, first, rows, after=(), beside=None, base=None, costs=None):
    at = first // BLOCK
    count = left.shape[1]
    ins = (weight, left, right) if beside is None else (weight, left, right, beside)
    others = after if base is None else (base, *after)
    shape = (rows, D) if base is None else base.shape

    def body(weight_ref, left_ref, right_ref, *rest):
        out_ref = rest[-1]
        out_ref[:, :D] = stepped(weight_ref[...], left_ref[...], right_ref[...], scale).astype(jnp.bfloat16)
        if beside is not None:
            out_ref[:, D:] = rest[0][...]

    return pl.pallas_call(
        body,
        grid=(rows // BLOCK,),
        in_specs=[rows_spec(at), rows_spec(at, count), whole_spec(right)]
        + ([] if beside is None else [rows_spec(0, count)])
        + [ANY] * len(others),
        out_specs=rows_spec(0, shape[1]),
        out_shape=jax.ShapeDtypeStruct(shape, jnp.bfloat16),
        input_output_aliases={} if base is None else {len(ins): 0},
        compiler_params=PARAMS,
        cost_estimate=costs or cost(1, rows, 2),
        name="step_rows",
    )(*ins, *others)


def rows_below(x, above, beside):
    part = x.shape[0]

    def body(x_ref, out_ref):
        out_ref[...] = x_ref[...]

    return pl.pallas_call(
        body,
        grid=(1,),
        in_specs=[whole_spec(x)],
        out_specs=pl.BlockSpec((part, D), lambda i: (above // part, 0)),
        out_shape=jax.ShapeDtypeStruct((above + part, D + beside), x.dtype),
        compiler_params=PARAMS,
        cost_estimate=cost(0, part, 2),
        name="rows_below",
    )(x)


def rows_of(x, first, rows, block):
    at = first // block

    def body(x_ref, out_ref):
        out_ref[...] = x_ref[...]

    return pl.pallas_call(
        body,
        grid=(rows // block,),
        in_specs=[rows_spec(at, block=block)],
        out_specs=rows_spec(block=block),
        out_shape=jax.ShapeDtypeStruct((rows, D), x.dtype),
        compiler_params=PARAMS,
        cost_estimate=cost(0, rows, 2),
        name="rows_of",
    )(x)


def halved_sum(mine, theirs):
    return ((mine.astype(jnp.float32) + theirs.astype(jnp.float32)) * 0.5).astype(jnp.bfloat16)


def into_rows(body, ins, in_specs, base, first, rows, units, costs, name, after, scratch=()):
    others = after if base is None else (base, *after)

    def with_others(*refs):
        body(*refs[: len(ins)], *refs[len(ins) + len(others) :])
    return pl.pallas_call(
        with_others,
        grid=(rows // BLOCK,),
        in_specs=in_specs + [ANY] * len(others),
        out_specs=rows_spec(first // BLOCK),
        out_shape=jax.ShapeDtypeStruct((units, D), jnp.bfloat16),
        input_output_aliases={} if base is None else {len(ins): 0},
        scratch_shapes=scratch,
        compiler_params=PARAMS,
        cost_estimate=costs,
        name=name,
    )(*ins, *others)


def mean_rows(mine, theirs, rows, base, first, units, after=(), source=0):
    def body(mine_ref, theirs_ref, out_ref):
        @pl.loop(0, BLOCK // 48)
        def _(strip):
            at = pl.ds(pl.multiple_of(strip * 48, 48), 48)
            out_ref[at] = halved_sum(mine_ref[at], theirs_ref[at])

    specs = [rows_spec(source // BLOCK)] * 2
    return into_rows(
        body, (mine, theirs), specs, base, first, rows, units, cost(0, rows, 3), "mean_rows", after
    )


def mean_of_steps(mine, left, right, theirs, their_left, their_blocks, scale, rows, units, after):
    part = their_blocks[0].shape[0]

    def body(mine_ref, left_ref, right_ref, theirs_ref, their_left_ref, *rest):
        out_ref, their_right = rest[-2:]

        @pl.when(pl.program_id(0) == 0)
        def _():
            for at in range(len(their_blocks)):
                their_right[pl.ds(at * part, part)] = rest[at][...]

        own = stepped(mine_ref[...], left_ref[...], right_ref[...], scale).astype(jnp.bfloat16)
        other = stepped(theirs_ref[...], their_left_ref[...], their_right[...], scale).astype(jnp.bfloat16)
        out_ref[...] = halved_sum(own, other)

    count = left.shape[1]
    return into_rows(
        body,
        (mine, left, right, theirs, their_left, *their_blocks),
        [rows_spec(), rows_spec(0, count), whole_spec(right)]
        + [rows_spec(), pl.BlockSpec((BLOCK, count), lambda i: (i, D // count))]
        + [whole_spec(block) for block in their_blocks],
        None,
        0,
        rows,
        units,
        cost(2, rows, 3),
        "mean_of_steps",
        after,
        [pltpu.VMEM((count, D), jnp.bfloat16)],
    )


def partial_sums(hidden, d_gate, d_up, gate_w, up_w, down_w, after):
    units, count = hidden.shape
    block = block_of(units, 432)
    steps = units // block

    def body(hidden_ref, d_gate_ref, d_up_ref, gate_ref, up_ref, down_ref, *rest):
        layer_ref, grad_ref = rest[-2:]

        @pl.when(pl.program_id(0) == 0)
        def _():
            layer_ref[...] = jnp.zeros_like(layer_ref)
            grad_ref[...] = jnp.zeros_like(grad_ref)

        layer_ref[...] += mm(hidden_ref[...], down_ref[...], ((0,), (0,))) * hidden_scale
        grad_sum = mm(d_gate_ref[...], gate_ref[...], ((0,), (0,))) + mm(d_up_ref[...], up_ref[...], ((0,), (0,)))
        grad_ref[...] += grad_sum * width_scale

    out = jax.ShapeDtypeStruct((count, D), jnp.float32)
    return pl.pallas_call(
        body,
        grid=(steps,),
        in_specs=[rows_spec(0, count, block)] * 3 + [rows_spec(block=block)] * 3 + [ANY] * len(after),
        out_specs=[whole_spec(out)] * 2,
        out_shape=[out] * 2,
        compiler_params=PARAMS,
        cost_estimate=cost(3, units, 3),
        name="partial_sums",
    )(hidden, d_gate, d_up, gate_w, up_w, down_w, *after)


def whole_step(distance, turned, tokens_local, grads_local, gate_w, up_w, down_w):
    units = gate_w.shape[0]
    devices = lax.axis_size("tp")
    ring = ring_of(devices)

    def send(x, parity=None):
        replicas = lax.axis_size("rep")
        senders = [i for i in range(replicas) if parity is None or i % 2 == parity]
        return lax.ppermute(x, "rep", [(i, (i + distance) % replicas) for i in senders])

    def along(x, by):
        return lax.ppermute(x, "tp", [(ring[i], ring[(i + by) % devices]) for i in range(devices)])

    shared = distance % 2 == 0
    early = 0 if shared else None
    is_early = lax.axis_index("rep") % 2 == 0
    theirs_raw = send(up_w, early)

    half = devices // 2

    def gather(turn, locals_):
        held = [[x] * devices for x in locals_]
        for hop in range(1, half + 1):
            for at, blocks_held in enumerate(held):
                last_way = turn if at % 2 == 0 else -turn
                for way in (turn, -turn):
                    if hop < half or way == last_way:
                        blocks_held[-way * hop] = along(blocks_held[-way * (hop - 1)], way)
        return [blocks_held[1:] for blocks_held in held]

    def gathered(*locals_):
        if devices > 8:
            return [list(lax.all_gather(x, "tp")) for x in locals_]
        others = lax.cond(turned, partial(gather, 1), partial(gather, -1), locals_)
        return [[x, *rest] for x, rest in zip(locals_, others)]

    def gathered_beside(x, mine, theirs):
        if devices > 8:
            return list(lax.all_gather(x, "tp")), mean_rows(mine, theirs, units, None, 0, units)

        def branch(turn, x, mine, theirs):
            held, mean, done = [x] * devices, None, 0
            for hop in range(1, half + 1):
                for way in (turn, -turn):
                    if hop < half or way == turn:
                        held[-way * hop] = along(held[-way * (hop - 1)], way)
                if hop < half:
                    upto = units // BLOCK * hop // (half - 1) * BLOCK
                    mean = mean_rows(mine, theirs, upto - done, mean, done, units, (), done)
                    held[-turn * hop], mean = lax.optimization_barrier((held[-turn * hop], mean))
                    done = upto
            return held[1:], mean

        others, mean = lax.cond(turned, partial(branch, 1), partial(branch, -1), x, mine, theirs)
        return [x, *others], mean

    def summed(terms):
        if devices > 8:
            totals = [lax.psum_scatter(term, "tp", scatter_dimension=0, tiled=True) for term in terms]
            return [total.astype(jnp.bfloat16) for total in totals]
        ring_sums = joined_sums if shared else sums
        return lax.cond(turned, partial(ring_sums, 1), partial(ring_sums, -1), terms)

    def sums(turn, terms):
        part = terms[0].shape[0] // devices
        block_at = lambda term, offset: term[(offset % devices) * part : (offset % devices + 1) * part]
        ways = [(at, way, half - (0 if (way == turn) == (at == 0) else 1)) for at in (0, 1) for way in (turn, -turn)]
        moving = {}
        for hop in range(1, half + 1):
            for at, way, hops in ways:
                if hop <= hops:
                    block = block_at(terms[at], way * (hops + 1 - hop))
                    if hop > 1:
                        block = block + moving[at, way].astype(jnp.float32)
                    moving[at, way] = along(block.astype(jnp.bfloat16), way)
        totals = []
        for at, term in enumerate(terms):
            total = block_at(term, 0)
            for way in (turn, -turn):
                total = total + moving[at, way].astype(jnp.float32)
            totals.append(total.astype(jnp.bfloat16))
        return totals

    def joined_sums(turn, terms):
        part = terms[0].shape[0] // devices
        block_at = lambda term, offset: term[(offset % devices) * part : (offset % devices + 1) * part]
        moving = {}
        for hop in range(1, half + 1):
            for way, lead in ((turn, 0), (-turn, 1)):
                offset = way * (half + 1 - hop)
                blocks = [block_at(terms[lead], offset)]
                if hop > 1:
                    came = moving[way].astype(jnp.float32)
                    blocks = [blocks[0] + came[:part], block_at(terms[1 - lead], offset)]
                    if hop > 2:
                        blocks[1] = blocks[1] + came[part:]
                moving[way] = along(jnp.concatenate(blocks).astype(jnp.bfloat16), way)
        totals = []
        for at, term in enumerate(terms):
            total = block_at(term, 0)
            for way, lead in ((turn, 0), (-turn, 1)):
                came = moving[way][:part] if lead == at else moving[way][part:]
                total = total + came.astype(jnp.float32)
            totals.append(total.astype(jnp.bfloat16))
        return totals

    token_blocks, grad_blocks = gathered(tokens_local, grads_local)
    tokens, grads, hidden, d_gate, d_up = forward(token_blocks, grad_blocks, gate_w, up_w, down_w)
    cut = units - BLOCK
    down_step = partial(step_rows, down_w, hidden, grads, hidden_scale, 0, units)
    head_step = partial(step_rows, gate_w, d_gate, tokens, width_scale, 0, cut)
    long_step = cost(20, units, 40)
    first = down_step(beside=d_up, base=rows_below(tokens_local, units, d_up.shape[1]))
    their_first = send(first, early)
    if shared:
        second = up_new = step_rows(up_w, d_up, tokens, width_scale, 0, units, (theirs_raw,), costs=long_step)
        their_up = send(up_new, 1)
    else:
        second = gate_head = head_step((theirs_raw,), costs=long_step)
        their_gate_head = send(gate_head)
    terms = partial_sums(hidden, d_gate, d_up, gate_w, up_w, down_w, (second,))
    layer_out, grad_in = summed(terms)
    if shared:
        down_new = down_step((layer_out,))
        their_down = send(down_new, 1)
        gate_head = head_step((their_first, down_new))
        their_gate_head = send(gate_head)
    landed = their_up if shared else their_first
    gate_tail = step_rows(gate_w, d_gate, tokens, width_scale, cut, BLOCK, (landed, gate_head, layer_out))
    their_gate_tail = send(gate_tail)

    their_tokens = rows_of(their_first, units, tokens_local.shape[0], 16)
    their_tokens, gate_tail = lax.optimization_barrier((their_tokens, gate_tail))

    def up_from_raw(their_blocks):
        return mean_of_steps(
            up_w, d_up, tokens, theirs_raw, their_first, their_blocks, width_scale, units, units, (gate_tail,)
        )

    if shared:
        (their_blocks,) = gathered(their_tokens)
        new_up = lax.cond(
            is_early,
            up_from_raw,
            lambda _: mean_rows(up_new, their_up, units, None, 0, units),
            their_blocks,
        )
        new_down = lax.cond(
            is_early,
            lambda after: mean_rows(first, their_first, units, None, 0, units, (after,)),
            lambda after: mean_rows(down_new, their_down, units, None, 0, units, (after,)),
            new_up,
        )
    else:
        their_blocks, new_down = gathered_beside(their_tokens, first, their_first)
        new_up = up_from_raw(their_blocks)
    new_gate = mean_rows(gate_head, their_gate_head, cut, None, 0, units, (new_up, new_down))
    new_gate = mean_rows(gate_tail, their_gate_tail, BLOCK, new_gate, cut, units)
    return layer_out, grad_in, new_gate, new_up, new_down


def shards(activations, out_grad, gate_weight, up_weight, down_weight, step_index):
    levels = lax.axis_size("rep").bit_length() - 1
    branches = [partial(whole_step, 1 << level) for level in range(levels)]
    layer_out, grad_in, gate, up, down = lax.switch(
        step_index[0] % levels,
        branches,
        (step_index[0] // levels) % 2 == 0,
        activations[0],
        out_grad[0],
        gate_weight[0].T,
        up_weight[0].T,
        down_weight[0],
    )
    return layer_out[None], grad_in[None], gate.T[None], up.T[None], down[None]


def solution(mesh):
    in_specs = (
        P("rep", "tp", None),
        P("rep", "tp", None),
        P("rep", None, "tp"),
        P("rep", None, "tp"),
        P("rep", "tp", None),
        P(),
    )
    out_specs = (
        P("rep", "tp", None),
        P("rep", "tp", None),
        P("rep", None, "tp"),
        P("rep", None, "tp"),
        P("rep", "tp", None),
    )
    return jax.shard_map(shards, mesh=mesh, in_specs=in_specs, out_specs=out_specs, check_vma=False)
```
